32 devices in a mesh: batch: 8 (over z, y), seq: 4 (over x, core).
Axes of the slice: x: 2, y: 2, z: 4, core: 2. Of those that a mesh axis runs over, the one named last changes fastest.
Arguments:
- hidden_in: bfloat16 [16, 1024, 768], P('batch', 'seq'), may hold values from -6 to 6
- cotangent: bfloat16 [16, 1024, 768], P('batch', 'seq'), may hold values from -6 to 6
- lengths: int32 [16], P('batch'), may hold values from 64 to 1024, as said below
- w_query: bfloat16 [768, 768], replicated, may hold values from -0.21875 to 0.21875
- w_key: bfloat16 [768, 768], replicated, may hold values from -0.21875 to 0.21875
- w_value: bfloat16 [768, 768], replicated, may hold values from -0.21875 to 0.21875
- w_output: bfloat16 [768, 768], replicated, may hold values from -0.875 to 0.875
- w_gate: bfloat16 [768, 2048], replicated, may hold values from -0.21875 to 0.21875
- w_up: bfloat16 [768, 2048], replicated, may hold values from -0.21875 to 0.21875
- w_down: bfloat16 [2048, 768], replicated, may hold values from -0.125 to 0.125
- gain_attn: float32 [768], replicated, may hold values from 0.5 to 1.5
- gain_mlp: float32 [768], replicated, may hold values from 0.5 to 1.5
Outputs:
- layer_out: bfloat16 [16, 1024, 768], P('batch', 'seq')
- grad_in: bfloat16 [16, 1024, 768], P('batch', 'seq')
- grad_query: float32 [768, 768], P(('batch', 'seq'))
- grad_key: float32 [768, 768], P(('batch', 'seq'))
- grad_value: float32 [768, 768], P(('batch', 'seq'))
- grad_output: float32 [768, 768], P(('batch', 'seq'))
- grad_gate: float32 [768, 2048], P(('batch', 'seq'))
- grad_up: float32 [768, 2048], P(('batch', 'seq'))
- grad_down: float32 [2048, 768], P(('batch', 'seq'))
- grad_gain_attn: float32 [768], P(('batch', 'seq'))
- grad_gain_mlp: float32 [768], P(('batch', 'seq'))
The draws below stay inside these ranges and needn't reach their ends.
Inputs may be any that keep to these rules, and one draw needn't show every extreme that they name: Each sequence uses its first lengths slots; in every group of 2 sequences of one batch index one sequence, drawn from the seed, has exactly 1024.
All inputs are finite; a program needn't handle non-finite values.
Results may differ from the reference program's by a relative error of at most 0.018.
Values may be sent and summed in bfloat16 or wider, within the bound.
No kernel may reach another device: no remote copies, remote signals or barrier semaphores. Data moves between devices by JAX's collectives and lax.ppermute only.
A program may use at most 192 MiB of HBM per device.

```python
import jax
import jax.numpy as jnp
from jax import lax

D = 768
HEADS = 12
HEAD_DIM = 64
FF = 2048
SEQ_LEN = 1024
SEQS = 2
SEQUENCES = 16


def draw_lengths(key, part):
    key = jax.random.fold_in(key, 11)
    key_base, key_pick = jax.random.split(key)
    raw = jax.random.randint(key_base, (SEQUENCES,), 0, 1025)
    cube = jnp.minimum(raw * raw // 1024 * raw // 1024, 1024)
    base = SEQ_LEN - (SEQ_LEN - SEQ_LEN // 16) * cube // 1024
    groups = SEQUENCES // SEQS
    pick = jax.random.randint(key_pick, (groups,), 0, SEQS)
    within = jnp.arange(SEQUENCES) % SEQS
    chosen = within == jnp.repeat(pick, SEQS)
    return jnp.where(chosen, SEQ_LEN, base).astype(jnp.int32)


def steps_of(rng, dims, cuts, smallest, largest):
    loudness = 1.0
    for dim, blocks in cuts:
        steps = jax.random.uniform(jax.random.fold_in(jax.random.fold_in(rng, 6), dim), (blocks,), jnp.float32, smallest / len(cuts), largest / len(cuts))
        loudness = loudness * jnp.repeat(jnp.exp(steps), dims[dim] // blocks).reshape((-1,) + (1,) * (len(dims) - 1 - dim))
    return loudness


def scatter_about(key, shape, spread, most, shards=(), held_as=jnp.bfloat16):
    loudness = steps_of(key, shape, shards, -0.22, 0.18) if shards else 1.0
    entries = jax.random.normal(key, shape, jnp.float32) * spread * loudness
    return jnp.minimum(jnp.maximum(entries, -most), most).astype(held_as)


def setup_inputs(seed: int = 0) -> dict:
    arg_keys = jax.random.split(jax.random.key(seed), 13)
    return {
        "hidden_in": scatter_about(arg_keys[0], (SEQUENCES, SEQ_LEN, D), 1.0, 6.0, ((0, 8), (1, 4))),
        "cotangent": scatter_about(arg_keys[1], (SEQUENCES, SEQ_LEN, D), 1.0, 6.0, ((0, 8), (1, 4))),
        "lengths": draw_lengths(jax.random.fold_in(arg_keys[12], 71), 0),
        "w_query": scatter_about(arg_keys[3], (D, D), D ** -0.5, 0.21875),
        "w_key": scatter_about(arg_keys[4], (D, D), D ** -0.5, 0.21875),
        "w_value": scatter_about(arg_keys[5], (D, D), D ** -0.5, 0.21875),
        "w_output": scatter_about(arg_keys[6], (D, D), (D // 16) ** -0.5, 0.875),
        "w_gate": scatter_about(arg_keys[7], (D, FF), D ** -0.5, 0.21875),
        "w_up": scatter_about(arg_keys[8], (D, FF), D ** -0.5, 0.21875),
        "w_down": scatter_about(arg_keys[9], (FF, D), FF ** -0.5, 0.125),
        "gain_attn": jnp.clip(1.0 + 0.1 * jax.random.normal(arg_keys[10], (D,), jnp.float32), 0.5, 1.5),
        "gain_mlp": jnp.clip(1.0 + 0.1 * jax.random.normal(arg_keys[11], (D,), jnp.float32), 0.5, 1.5),
    }


EPS = 1e-06
NEG = -1e+30
HIGH = lax.Precision.HIGHEST

@jax.custom_vjp
def low(v):
    return lax.optimization_barrier(v.astype(jnp.bfloat16)).astype(jnp.float32)

@jax.custom_vjp
def low_back(v):
    return v

def low_keep(v):
    return (low(v), None)

def low_pass(kept, grad):
    return (grad,)

def back_keep(v):
    return (v, None)

def back_low(kept, grad):
    return (low(grad),)
low.defvjp(low_keep, low_pass)
low_back.defvjp(back_keep, back_low)

def rope_tables(count):
    half = HEAD_DIM // 2
    inverse = 10000.0 ** (-(jnp.arange(half, dtype=jnp.float32) * 2.0) / HEAD_DIM)
    angles = jnp.arange(count, dtype=jnp.float32)[:, None] * inverse[None, :]
    cosine = jnp.concatenate([jnp.cos(angles), jnp.cos(angles)], axis=-1)
    sine = jnp.concatenate([jnp.sin(angles), jnp.sin(angles)], axis=-1)
    return (cosine[:, None, :], sine[:, None, :])

def rotate(z, cosine, sine):
    half = HEAD_DIM // 2
    turned = jnp.concatenate([-z[..., half:], z[..., :half]], axis=-1)
    return z * cosine + turned * sine

def attend(pack):
    query, key, value, length = pack
    scale = float(HEAD_DIM) ** (-0.5)
    scores = low_back(jnp.einsum('qhd,khd->hqk', query, key, precision=HIGH) * scale)
    slots = jnp.arange(SEQ_LEN)
    visible = (slots[None, :] <= slots[:, None]) & (slots[None, :] < length)
    scores = jnp.where(visible[None], scores, NEG)
    probs = jax.nn.softmax(scores, axis=-1)
    out = jnp.einsum('hqk,khd->qhd', low(probs), value, precision=HIGH)
    return out.reshape(SEQ_LEN, D)

def rms_norm(v, gain):
    return v * lax.rsqrt(lax.optimization_barrier(jnp.mean(v * v, axis=-1, keepdims=True)) + EPS) * gain

def reference(hidden_in, cotangent, lengths, w_query, w_key, w_value, w_output, w_gate, w_up, w_down, gain_attn, gain_mlp):
    valid = (jnp.arange(SEQ_LEN)[None, :] < lengths[:, None]).astype(jnp.float32).reshape(-1, 1)
    cosine, sine = rope_tables(SEQ_LEN)

    def mm(a, w):
        return jnp.dot(a, w, precision=HIGH)

    def forward(x, wq, wk, wv, wo, wg, wu, wd, g1, g2):
        flat = x.reshape(-1, D)
        shape4 = (SEQUENCES, SEQ_LEN, HEADS, HEAD_DIM)
        query = low(rotate(low_back(mm(flat, wq)).reshape(shape4), cosine, sine))
        key = low(rotate(low_back(mm(flat, wk)).reshape(shape4), cosine, sine))
        value = low(low_back(mm(flat, wv))).reshape(shape4)
        attended = lax.map(jax.checkpoint(attend), (query, key, value, lengths))
        attended = low_back(low(attended.reshape(-1, D)))
        mixed1 = flat + low_back(mm(attended, wo))
        x1 = rms_norm(mixed1, g1)
        x1_low = low(x1)
        gate = low_back(mm(x1_low, wg))
        up = low_back(mm(x1_low, wu))
        hid = low(jax.nn.silu(gate) * up)
        mixed2 = x1 + low_back(mm(hid, wd))
        return valid * rms_norm(mixed2, g2)
    f32 = jnp.float32
    primals = (hidden_in.astype(f32), w_query.astype(f32), w_key.astype(f32), w_value.astype(f32), w_output.astype(f32), w_gate.astype(f32), w_up.astype(f32), w_down.astype(f32), gain_attn, gain_mlp)
    result, pull = jax.vjp(forward, *primals)
    grads = pull(cotangent.astype(f32).reshape(-1, D))
    layer_out = result.reshape(SEQUENCES, SEQ_LEN, D).astype(jnp.bfloat16)
    grad_in = grads[0].reshape(SEQUENCES, SEQ_LEN, D).astype(jnp.bfloat16)
    return (layer_out, grad_in, grads[1], grads[2], grads[3], grads[4], grads[5], grads[6], grads[7], grads[8], grads[9])
```

```python
import functools

import jax
import jax.numpy as jnp
from jax import lax
from jax.experimental import pallas as pl
from jax.experimental.pallas import tpu as pltpu
from jax.sharding import PartitionSpec as P

HEADS = 12
HEAD_DIM = 64
PAIR = 2 * HEAD_DIM

EPS = 1e-06
NEG = -1e30

F32 = jnp.float32
BF16 = jnp.bfloat16


def dot_nn(left, right):
    return lax.dot_general(left, right, (((1,), (0,)), ((), ())), preferred_element_type=F32)


def dot_nt(left, right):
    return lax.dot_general(left, right, (((1,), (1,)), ((), ())), preferred_element_type=F32)


def dot_tn(left, right):
    return lax.dot_general(left, right, (((0,), (0,)), ((), ())), preferred_element_type=F32)


def rope_tables(count):
    half = HEAD_DIM // 2
    inverse = 10000.0 ** (-(jnp.arange(half, dtype=F32) * 2.0) / HEAD_DIM)
    angles = jnp.arange(count, dtype=F32)[:, None] * inverse[None, :]
    cosine, sine = jnp.cos(angles), jnp.sin(angles)
    zero = jnp.zeros_like(sine)
    return (
        jnp.concatenate([cosine] * 4, axis=-1),
        jnp.concatenate([zero, sine] * 2, axis=-1),
        jnp.concatenate([-sine, zero] * 2, axis=-1),
    )


def attention_forward_kernel(
    scal, kept, recv, kept_o, recv_o, wq, wk, wv, cos, sin_a, sin_b,
    q_ref, k_ref, v_ref, att_ref, att_oth_ref, lse_ref,
    w_buf, sems,
):
    core, chip, length = scal[0], scal[1], scal[2]
    block = kept.shape[0]
    cols = q_ref.shape[1]
    pairs = cols // PAIR
    start = pl.multiple_of(core * cols, PAIR)
    copies = []
    for i, w in enumerate((wq, wk, wv)):
        copy = pltpu.make_async_copy(w.at[:, pl.ds(start, cols)], w_buf.at[i], sems.at[i])
        copy.start()
        copies.append(copy)
    other = 1 - core
    far = 1 - chip
    places = (
        (kept, 2 * chip + core),
        (recv, 2 * far + core),
        (kept_o, 2 * chip + other),
        (recv_o, 2 * far + other),
    )
    for i in range(3):
        copies[i].wait()
        out = (q_ref, k_ref, v_ref)[i]
        for x_ref, place in places:
            rows = pl.ds(pl.multiple_of(place * block, block), block)
            z = dot_nn(x_ref[...], w_buf[i])
            if i < 2:
                c, a, b = cos[rows, :], sin_a[rows, :], sin_b[rows, :]
                parts = []
                for p in range(pairs):
                    t = z[:, p * PAIR:(p + 1) * PAIR]
                    parts.append(t * c + pltpu.roll(t, 32, 1) * a + pltpu.roll(t, 96, 1) * b)
                z = jnp.concatenate(parts, axis=1)
            out[rows, :] = z.astype(BF16)

    scale = float(HEAD_DIM) ** (-0.5)
    lane = lax.broadcasted_iota(jnp.int32, (1, PAIR), 1)
    low = lane < HEAD_DIM
    row_i = lax.broadcasted_iota(jnp.int32, (block, block), 0)
    col_i = lax.broadcasted_iota(jnp.int32, (block, block), 1)

    def pair_step(p, _):
        lanes = pl.ds(pl.multiple_of(p * PAIR, PAIR), PAIR)
        for i in range(4):
            span = (i + 1) * block
            rows = slice(i * block, span)

            @pl.when(i * block < length)
            def _():
                qi = q_ref[rows, lanes]
                kk = k_ref[0:span, lanes]
                vv = v_ref[0:span, lanes]
                visible = (col_i <= row_i) & (col_i + i * block < length)
                outs, tops = [], []
                for h in range(2):
                    mine = low if h == 0 else jnp.logical_not(low)
                    s = dot_nt(jnp.where(mine, qi, jnp.zeros_like(qi)), kk)
                    s_diag = jnp.where(visible, s[:, i * block:], NEG)
                    top = jnp.max(s_diag, axis=1, keepdims=True)
                    if i:
                        top = jnp.maximum(top, jnp.max(s[:, :i * block], axis=1, keepdims=True))
                    e = jnp.exp((s_diag - top) * scale).astype(BF16)
                    if i:
                        e = jnp.concatenate(
                            [jnp.exp((s[:, :i * block] - top) * scale).astype(BF16), e], axis=1
                        )
                    outs.append(dot_nn(e, jnp.where(mine, vv, jnp.ones_like(vv))))
                    tops.append(top)
                sums = pltpu.roll(jnp.where(low, outs[1], outs[0]), HEAD_DIM, 1)
                att = (jnp.where(low, outs[0], outs[1]) / sums).astype(BF16)
                att_ref[rows, lanes] = att
                lse = jnp.where(low, tops[0], tops[1]) * scale + jnp.log(sums)
                lse_t = lse.T
                base = pl.multiple_of(p * 16, 16)
                lse_ref[pl.ds(base, 8), rows] = lse_t[0:8, :]
                lse_ref[pl.ds(base + 8, 8), rows] = lse_t[HEAD_DIM:HEAD_DIM + 8, :]

            @pl.when(i * block >= length)
            def _():
                att_ref[rows, lanes] = jnp.zeros((block, PAIR), BF16)
                base = pl.multiple_of(p * 16, 16)
                lse_ref[pl.ds(base, 16), rows] = jnp.zeros((16, block), F32)
        return 0

    lax.fori_loop(0, pairs, pair_step, 0)
    for i in range(2):
        place = pl.multiple_of((2 * (chip if i == 0 else far) + other) * block, block)
        att_oth_ref[i] = att_ref[pl.ds(place, block), :]


def attention_forward(scal, kept, recv, kept_o, recv_o, wq, wk, wv, tables):
    block, width = kept.shape
    full = 4 * block
    cols = width // 2
    vmem = pl.BlockSpec(memory_space=pltpu.VMEM)
    hbm = pl.BlockSpec(memory_space=pl.ANY)
    return pl.pallas_call(
        attention_forward_kernel,
        out_shape=(
            jax.ShapeDtypeStruct((full, cols), BF16),
            jax.ShapeDtypeStruct((full, cols), BF16),
            jax.ShapeDtypeStruct((full, cols), BF16),
            jax.ShapeDtypeStruct((full, cols), BF16),
            jax.ShapeDtypeStruct((2, block, cols), BF16),
            jax.ShapeDtypeStruct((cols // PAIR * 16, full), F32),
        ),
        in_specs=[pl.BlockSpec(memory_space=pltpu.SMEM)] + [vmem] * 4 + [hbm] * 3 + [vmem] * 3,
        out_specs=(vmem,) * 6,
        scratch_shapes=[pltpu.VMEM((3, width, cols), BF16), pltpu.SemaphoreType.DMA((3,))],
        compiler_params=pltpu.CompilerParams(vmem_limit_bytes=56 * 1024 * 1024),
        cost_estimate=pl.CostEstimate(
            flops=2 * full * width * cols * 3 + 4 * full * full * cols, bytes_accessed=12_000_000,
            transcendentals=full * full * 6,
        ),
        name="attention_forward",
    )(scal, kept, recv, kept_o, recv_o, wq, wk, wv, *tables)


def attention_backward_kernel(
    scal, q_ref, k_ref, v_ref, att_ref, do_own, do_oth, lse_ref, cos, sin_a, sin_b,
    dq_ref, dk_ref, dv_ref,
    do_ref, delta_ref, pt_ref, dst_ref, dom_ref,
):
    core, chip, length = scal[0], scal[1], scal[2]
    full, cols = q_ref.shape
    block = full // 4
    pairs = cols // PAIR
    scale = float(HEAD_DIM) ** (-0.5)
    other = 1 - core
    far = 1 - chip
    for source, i, place in (
        (do_own, 0, 2 * chip + core),
        (do_own, 1, 2 * far + core),
        (do_oth, 0, 2 * chip + other),
        (do_oth, 1, 2 * far + other),
    ):
        do_ref[pl.ds(pl.multiple_of(place * block, block), block), :] = source[i]

    low = lax.broadcasted_iota(jnp.int32, (1, PAIR), 1) < HEAD_DIM
    key_i = lax.broadcasted_iota(jnp.int32, (block, block), 0)
    query_i = lax.broadcasted_iota(jnp.int32, (block, block), 1)

    def back(g, rows):
        g = g * scale
        return (
            g * cos[rows, :]
            - pltpu.roll(g, 96, 1) * sin_b[rows, :]
            - pltpu.roll(g, 32, 1) * sin_a[rows, :]
        ).astype(BF16)

    def split(z):
        zero = jnp.zeros_like(z)
        return jnp.where(low, z, zero), jnp.where(low, zero, z)

    def pair_step(p, _):
        lanes = pl.ds(pl.multiple_of(p * PAIR, PAIR), PAIR)
        base = pl.multiple_of(p * 16, 16)
        for i in range(4):
            rows = slice(i * block, (i + 1) * block)
            prod = (do_ref[rows, lanes].astype(F32) * att_ref[rows, lanes].astype(F32)).T
            delta_ref[0:1, rows] = jnp.sum(prod[:HEAD_DIM], axis=0, keepdims=True)
            delta_ref[8:9, rows] = jnp.sum(prod[HEAD_DIM:], axis=0, keepdims=True)
            dom = split(do_ref[rows, lanes])
            for h in range(2):
                dom_ref[h, rows, :] = dom[h]
        for j in range(4):
            keys = slice(j * block, (j + 1) * block)
            kj = split(k_ref[keys, lanes])
            vj = split(v_ref[keys, lanes])
            for i in range(j, 4):
                rows = slice(i * block, (i + 1) * block)

                @pl.when(i * block < length)
                def _():
                    qi = q_ref[rows, lanes]
                    doi = do_ref[rows, lanes]
                    for h in range(2):
                        st = dot_nt(kj[h], qi) * scale
                        dpt = dot_nt(vj[h], doi)
                        pt = jnp.exp(st - lse_ref[pl.ds(base + 8 * h, 1), rows])
                        if i == j:
                            visible = (key_i <= query_i) & (key_i + j * block < length)
                            pt = jnp.where(visible, pt, 0.0)
                        dst = pt * (dpt - delta_ref[8 * h:8 * h + 1, rows])
                        pt_ref[h, keys, rows] = pt.astype(BF16)
                        dst_ref[h, keys, rows] = dst.astype(BF16)

                @pl.when(i * block >= length)
                def _():
                    for h in range(2):
                        pt_ref[h, keys, rows] = jnp.zeros((block, block), BF16)
                        dst_ref[h, keys, rows] = jnp.zeros((block, block), BF16)
            span = slice(j * block, full)
            qm = split(q_ref[span, lanes])
            dk = dot_nn(dst_ref[0, keys, span], qm[0]) + dot_nn(dst_ref[1, keys, span], qm[1])
            dv = dot_nn(pt_ref[0, keys, span], dom_ref[0, span, :]) + dot_nn(
                pt_ref[1, keys, span], dom_ref[1, span, :]
            )
            dk_ref[keys, lanes] = back(dk, keys)
            dv_ref[keys, lanes] = dv.astype(BF16)
        for i in range(4):
            rows = slice(i * block, (i + 1) * block)
            span = slice(0, (i + 1) * block)
            km = split(k_ref[span, lanes])
            dq = dot_tn(dst_ref[0, span, rows], km[0]) + dot_tn(dst_ref[1, span, rows], km[1])
            dq_ref[rows, lanes] = back(dq, rows)
        return 0

    lax.fori_loop(0, pairs, pair_step, 0)


def attention_backward(scal, q, k, v, att, do_own, do_oth, lse, tables):
    full, cols = q.shape
    vmem = pl.BlockSpec(memory_space=pltpu.VMEM)
    shape = jax.ShapeDtypeStruct((full, cols), BF16)
    return pl.pallas_call(
        attention_backward_kernel,
        out_shape=(shape,) * 3,
        in_specs=[pl.BlockSpec(memory_space=pltpu.SMEM)] + [vmem] * 10,
        out_specs=(vmem,) * 3,
        scratch_shapes=[
            pltpu.VMEM((full, cols), BF16),
            pltpu.VMEM((16, full), F32),
            pltpu.VMEM((2, full, full), BF16),
            pltpu.VMEM((2, full, full), BF16),
            pltpu.VMEM((2, full, PAIR), BF16),
        ],
        compiler_params=pltpu.CompilerParams(vmem_limit_bytes=56 * 1024 * 1024),
        cost_estimate=pl.CostEstimate(
            flops=10 * full * full * cols, bytes_accessed=10_000_000, transcendentals=full * full * 6,
        ),
        name="attention_backward",
    )(scal, q, k, v, att, do_own, do_oth, lse, *tables)


class Halving:
    def __init__(self, array, parts, bits):
        rows, cols = array.shape
        self.names = list(bits)
        total = 1
        for n in parts:
            total *= n
        self.leaves = [array.reshape(tuple(parts) + (rows // total, cols))]

    def take(self, name, index):
        at = self.names.index(name)
        return [lax.dynamic_index_in_dim(leaf, index, at, keepdims=False) for leaf in self.leaves]

    def outgoing(self, name, me):
        out = sum(leaf.astype(F32) for leaf in self.take(name, 1 - me))
        return out.astype(BF16)

    def incoming(self, name, me, got):
        self.leaves = self.take(name, me) + [got]
        self.names.remove(name)

    def result(self):
        return sum(leaf.astype(F32) for leaf in self.leaves)


def swap_seq(value, bit):
    return lax.ppermute(value, "seq", [(i, i ^ bit) for i in range(4)])


def on_device(
    batch_size,
    hidden_in,
    cotangent,
    lengths,
    w_query,
    w_key,
    w_value,
    w_output,
    w_gate,
    w_up,
    w_down,
    gain_attn,
    gain_mlp,
):
    seqs, block, width = hidden_in.shape
    tokens = seqs * block
    cols = width // 2
    rank = lax.axis_index("seq")
    batch = lax.axis_index("batch")
    chip, core = rank // 2, rank % 2
    far, other = 1 - chip, 1 - core

    def swap(z):
        kept = lax.dynamic_index_in_dim(z, chip, 0, keepdims=False)
        away = lax.dynamic_index_in_dim(z, far, 0, keepdims=False)
        return kept, swap_seq(away, 2)

    def swap_home(kept, away):
        back = swap_seq(away, 2)
        first = chip == 0
        return jnp.stack([jnp.where(first, kept, back), jnp.where(first, back, kept)])

    kept, recv = swap(hidden_in)
    kept_o = swap_seq(kept, 1)
    recv_o = swap_seq(recv, 1)
    ct_kept, ct_recv = swap(cotangent)
    length = lax.dynamic_index_in_dim(lengths, chip, 0, keepdims=False)
    scal = jnp.stack([core, chip, length]).astype(jnp.int32)
    tables = rope_tables(4 * block)

    q, k, v, att, att_oth, lse = attention_forward(
        scal, kept, recv, kept_o, recv_o, w_query, w_key, w_value, tables
    )
    got = swap_seq(att_oth, 1).reshape(tokens, cols)
    att4 = att.reshape(4, block, cols)
    mine = jnp.concatenate(
        [
            lax.dynamic_index_in_dim(att4, 2 * chip + core, 0, keepdims=False),
            lax.dynamic_index_in_dim(att4, 2 * far + core, 0, keepdims=False),
        ]
    )
    attended = jnp.where(
        core == 0, jnp.concatenate([mine, got], axis=1), jnp.concatenate([got, mine], axis=1)
    )
    flat = jnp.concatenate([kept, recv])
    slots = jnp.arange(block, dtype=jnp.int32)
    positions = jnp.concatenate(
        [(2 * chip + core) * block + slots, (2 * far + core) * block + slots]
    )
    valid = (positions < length).astype(F32)[:, None]

    mixed1 = flat.astype(F32) + dot_nn(attended, w_output)
    root1 = lax.rsqrt(jnp.mean(mixed1 * mixed1, axis=-1, keepdims=True) + EPS)
    norm1 = mixed1 * root1
    x1 = norm1 * gain_attn
    x1_low = x1.astype(BF16)
    gate = dot_nn(x1_low, w_gate)
    up = dot_nn(x1_low, w_up)
    sigma = jax.nn.sigmoid(gate)
    active = gate * sigma
    hid = (active * up).astype(BF16)
    mixed2 = x1 + dot_nn(hid, w_down)
    root2 = lax.rsqrt(jnp.mean(mixed2 * mixed2, axis=-1, keepdims=True) + EPS)
    norm2 = mixed2 * root2
    y = (valid * (norm2 * gain_mlp)).astype(BF16)
    layer_out = swap_home(y[:block], y[block:])
    d_out = valid * jnp.concatenate([ct_kept, ct_recv]).astype(F32)
    grad_g2 = jnp.sum(d_out * norm2, axis=0)
    d_n2 = d_out * gain_mlp
    d_mixed2 = root2 * (d_n2 - norm2 * jnp.mean(d_n2 * norm2, axis=-1, keepdims=True))
    d_mlp = d_mixed2.astype(BF16)
    grad_wd = dot_tn(hid, d_mlp).astype(BF16)
    d_hid = dot_nt(d_mlp, w_down)
    d_gate = (d_hid * up * sigma * (1.0 + gate * (1.0 - sigma))).astype(BF16)
    d_up = (d_hid * active).astype(BF16)
    grad_wg = dot_tn(x1_low, d_gate).astype(BF16)
    grad_wu = dot_tn(x1_low, d_up).astype(BF16)
    d_x1 = d_mixed2 + dot_nt(d_gate, w_gate) + dot_nt(d_up, w_up)
    grad_g1 = jnp.sum(d_x1 * norm1, axis=0)
    d_n1 = d_x1 * gain_attn
    d_mixed1 = root1 * (d_n1 - norm1 * jnp.mean(d_n1 * norm1, axis=-1, keepdims=True))
    d_attn = d_mixed1.astype(BF16)
    grad_wo = dot_tn(attended, d_attn).astype(BF16)
    d_attended = dot_nt(d_attn, w_output).astype(BF16)
    halves = d_attended.reshape(2, block, 2, cols)
    do_own = lax.dynamic_index_in_dim(halves, core, 2, keepdims=False)
    do_oth = swap_seq(lax.dynamic_index_in_dim(halves, other, 2, keepdims=False), 1)

    dzq, dzk, dzv = attention_backward(scal, q, k, v, att, do_own, do_oth, lse, tables)

    def by_slot(a, b):
        first = jnp.where(core == 0, a, b), jnp.where(core == 0, b, a)
        return first

    even_kept, odd_kept = by_slot(kept, kept_o)
    even_recv, odd_recv = by_slot(recv, recv_o)
    chip0 = chip == 0
    x_all = jnp.concatenate(
        [
            jnp.where(chip0, even_kept, even_recv),
            jnp.where(chip0, odd_kept, odd_recv),
            jnp.where(chip0, even_recv, even_kept),
            jnp.where(chip0, odd_recv, odd_kept),
        ]
    )
    grads_qkv = [dot_tn(x_all, dz).astype(BF16) for dz in (dzq, dzk, dzv)]

    def columns(w):
        return lax.dynamic_slice_in_dim(w, core * cols, cols, axis=1)

    part = (
        dot_nt(dzq, columns(w_query)) + dot_nt(dzk, columns(w_key)) + dot_nt(dzv, columns(w_value))
    ).reshape(2, 2, block, width)

    def pick(c):
        one = lax.dynamic_index_in_dim(part, c, 1, keepdims=False)
        return jnp.concatenate(
            [
                lax.dynamic_index_in_dim(one, chip, 0, keepdims=False),
                lax.dynamic_index_in_dim(one, far, 0, keepdims=False),
            ]
        )

    got_in = swap_seq(pick(other).astype(BF16), 1)
    g_in = (d_mixed1 + pick(core) + got_in.astype(F32)).astype(BF16)
    grad_in = swap_home(g_in[:block], g_in[block:])

    bits = batch_size.bit_length() - 1
    batch_names = ["b%d" % i for i in reversed(range(bits))]

    def index_of(name):
        if name == "c":
            return core
        if name == "x":
            return chip
        return (batch >> int(name[1:])) & 1

    def exchange(value, name):
        if name == "c":
            return swap_seq(value, 1)
        if name == "x":
            return swap_seq(value, 2)
        bit = 1 << int(name[1:])
        return lax.ppermute(value, "batch", [(i, i ^ bit) for i in range(batch_size)])

    def reduce_scatter(array, order, cores):
        names = batch_names + ["x"] + (["c"] if cores else [])
        state = Halving(array, (2,) * len(names), names)
        for name in order:
            me = index_of(name)
            state.incoming(name, me, exchange(state.outgoing(name, me), name))
        return state.result()

    tail = ["b%d" % i for i in range(1, bits)]
    order_x = ["x", "b0"] + tail
    order_y = ["b0", "x"] + tail
    if bits == 0:
        order_x = order_y = ["x"]

    g_gate = reduce_scatter(grad_wg, ["c"] + order_x, True)
    g_up = reduce_scatter(grad_wu, ["c"] + order_y, True)
    g_down = jnp.concatenate(
        [
            reduce_scatter(grad_wd[:, :cols], ["c"] + order_x, True),
            reduce_scatter(grad_wd[:, cols:], ["c"] + order_y, True),
        ],
        axis=1,
    )
    wo_qkv = jnp.concatenate(grads_qkv, axis=1)
    g_output = reduce_scatter(grad_wo, ["c"] + order_x, True)
    halves = [
        reduce_scatter(wo_qkv[:, : 3 * cols // 2], order_x, False),
        reduce_scatter(wo_qkv[:, 3 * cols // 2:], order_y, False),
    ]
    qkv_half = jnp.concatenate(halves, axis=1)
    rows = qkv_half.shape[0] // 2
    qkv_half = qkv_half.reshape(2, rows, 3, cols)
    away = swap_seq(lax.dynamic_index_in_dim(qkv_half, other, 0, keepdims=False).astype(BF16), 1)
    stay = lax.dynamic_index_in_dim(qkv_half, core, 0, keepdims=False)
    away = away.astype(F32)
    g_qkv = jnp.where(
        core == 0,
        jnp.concatenate([stay, away], axis=-1),
        jnp.concatenate([away, stay], axis=-1),
    )
    gains = jnp.concatenate([grad_g1[:, None], grad_g2[:, None]], axis=1)
    gains = lax.psum_scatter(gains, ("batch", "seq"), scatter_dimension=0, tiled=True)
    return (
        layer_out,
        grad_in,
        g_qkv[:, 0],
        g_qkv[:, 1],
        g_qkv[:, 2],
        g_output,
        g_gate,
        g_up,
        g_down,
        gains[:, 0],
        gains[:, 1],
    )


def solution(mesh):
    tokens = P("batch", "seq", None)
    rows = P(("batch", "seq"), None)
    return jax.shard_map(
        functools.partial(on_device, mesh.shape["batch"]),
        mesh=mesh,
        in_specs=(tokens, tokens, P("batch")) + (P(),) * 9,
        out_specs=(tokens, tokens) + (rows,) * 7 + (P(("batch", "seq")),) * 2,
        check_vma=False,
    )
```

```python
import functools

import jax
import jax.numpy as jnp
import numpy as np
from jax import lax
from jax.experimental import pallas as pl
from jax.experimental.pallas import tpu as pltpu
from jax.sharding import PartitionSpec as P

HEADS = 12
HEAD_DIM = 64
PAIR = 2 * HEAD_DIM

EPS = 1e-06
NEG = -1e30
LANES = 128
SUPER = 16

F32 = jnp.float32
BF16 = jnp.bfloat16


def dot_nn(left, right):
    return lax.dot_general(left, right, (((1,), (0,)), ((), ())), preferred_element_type=F32)


def dot_nt(left, right):
    return lax.dot_general(left, right, (((1,), (1,)), ((), ())), preferred_element_type=F32)


def dot_tn(left, right):
    return lax.dot_general(left, right, (((0,), (0,)), ((), ())), preferred_element_type=F32)


def rope_tables(count):
    half = HEAD_DIM // 2
    inverse = 10000.0 ** (-(np.arange(half, dtype=np.float32) * np.float32(2.0)) / HEAD_DIM)
    angles = np.arange(count, dtype=np.float32)[:, None] * inverse.astype(np.float32)[None, :]
    cosine, sine = np.cos(angles), np.sin(angles)
    zero = np.zeros_like(sine)
    tables = (
        np.concatenate([cosine] * 4, axis=-1),
        np.concatenate([zero, sine] * 2, axis=-1),
        np.concatenate([-sine, zero] * 2, axis=-1),
    )
    return jnp.asarray(np.stack(tables), F32)


def start(source, target, sem):
    copy = pltpu.make_async_copy(source, target, sem)
    copy.start()
    return copy


def aligned(index, size):
    return pl.ds(pl.multiple_of(index * size, size), size)


def vspec():
    return pl.BlockSpec(memory_space=pltpu.VMEM)


def hspec():
    return pl.BlockSpec(memory_space=pltpu.HBM)


def aspec():
    return pl.BlockSpec(memory_space=pl.ANY)


def sspec():
    return pl.BlockSpec(memory_space=pltpu.SMEM)


def mean_row(z):
    return jnp.sum(z, axis=1, keepdims=True) * (1.0 / z.shape[1])


def reversed_bits(index, bits):
    out = 0
    for i in range(bits):
        out |= ((index >> i) & 1) << (bits - 1 - i)
    return out


def pack(out_ref, value, block0, row0, height):
    low = value.astype(BF16)
    for b in range(value.shape[0] // height):
        for j in range(value.shape[1] // LANES):
            out_ref[reversed_bits(block0 + b, 4), row0 + j * height:row0 + (j + 1) * height, :] = low[
                b * height:(b + 1) * height, j * LANES:(j + 1) * LANES
            ]


def kernel_call(kernel, name, outs, specs, scratch, flops, moved, exps=0, resident=(), vmem=16):
    return pl.pallas_call(
        kernel,
        out_shape=tuple(pltpu.VMEM(*z) for z in resident)
        + tuple(pltpu.HBM(*z) for z in outs),
        in_specs=specs,
        out_specs=(vspec(),) * len(resident) + (hspec(),) * len(outs),
        scratch_shapes=scratch,
        compiler_params=pltpu.CompilerParams(vmem_limit_bytes=vmem * 1024 * 1024),
        cost_estimate=pl.CostEstimate(flops=flops, bytes_accessed=moved, transcendentals=exps),
        name=name,
    )


class Copies:
    def __init__(self, sems):
        self.sems, self.used, self.open = sems, 0, []

    def start(self, source, target):
        copy = start(source, target, self.sems.at[self.used])
        self.used += 1
        return copy

    def send(self, source, target):
        self.open.append(self.start(source, target))

    def drain(self):
        for copy in self.open:
            copy.wait()


def split_three(value):
    first = value.astype(BF16).astype(F32)
    rest = value - first
    second = rest.astype(BF16).astype(F32)
    return first, second, (rest - second).astype(BF16).astype(F32)


def beside(lane, head, mine, pieces):
    own = (lane < HEAD_DIM) if head == 0 else (lane >= HEAD_DIM)
    first = (1 - head) * HEAD_DIM
    out = jnp.zeros_like(mine)
    for i, piece in enumerate(pieces):
        out = jnp.where(lane == first + i, piece, out)
    return jnp.where(own, mine, out)


def attention_forward_kernel(
    scal, kept, recv, kept_o, recv_o, wq, wk, wv, tables,
    q_out, k_out, v_out, att_out, oth_out, x_out,
    x_ref, w_buf, t_ref, q_ref, k_ref, v_ref, att_ref, sems,
):
    core, chip, length = scal[0], scal[1], scal[2]
    block = kept.shape[0]
    full = 4 * block
    pairs = q_ref.shape[0]
    cols = pairs * PAIR
    other, far = 1 - core, 1 - chip
    io = Copies(sems)
    columns = pl.ds(pl.multiple_of(core * cols, PAIR), cols)
    needed = []
    for i, w in enumerate((wq, wk, wv)):
        needed.append(io.start(w.at[:, columns], w_buf.at[:, i * cols:(i + 1) * cols]))
    for source, place in (
        (kept, 2 * chip + core),
        (recv, 2 * far + core),
        (kept_o, 2 * chip + other),
        (recv_o, 2 * far + other),
    ):
        needed.append(io.start(source, x_ref.at[aligned(place, block), :]))
    needed.append(io.start(tables, t_ref))
    for copy in needed:
        copy.wait()
    io.send(x_ref, x_out)
    scale = float(HEAD_DIM) ** (-0.5)
    lane = lax.broadcasted_iota(jnp.int32, (1, PAIR), 1)
    low = lane < HEAD_DIM
    for t in range(2):
        rows = slice(t * 2 * block, (t + 1) * 2 * block)
        z = dot_nn(x_ref[rows, :], w_buf[...])
        c, a, b = t_ref[0, rows, :], t_ref[1, rows, :], t_ref[2, rows, :]
        slot = t * 2 * block + lax.broadcasted_iota(jnp.int32, (2 * block, PAIR), 0)
        bias = jnp.where(slot < length, 0.0, NEG)
        for p in range(3 * pairs):
            part = z[:, p * PAIR:(p + 1) * PAIR]
            if p < 2 * pairs:
                part = part * c + pltpu.roll(part, 32, 1) * a + pltpu.roll(part, 96, 1) * b
            for h in range(2):
                if p < pairs:
                    mine = part.astype(BF16).astype(F32) * scale
                    q_ref[p, h, rows, :] = beside(lane, h, mine, (0.0, 0.0, 0.0, 1.0)).astype(BF16)
                elif p < 2 * pairs:
                    k_ref[p - pairs, h, rows, :] = beside(
                        lane, h, part, (1.0, 1.0, 1.0, bias)
                    ).astype(BF16)
                else:
                    own = low if h == 0 else jnp.logical_not(low)
                    v_ref[p - 2 * pairs, h, rows, :] = jnp.where(own, part, 1.0).astype(BF16)
    io.send(k_ref, k_out)
    io.send(v_ref, v_out)

    causal = lax.broadcasted_iota(jnp.int32, (block, block), 1) <= lax.broadcasted_iota(
        jnp.int32, (block, block), 0
    )
    for p in range(pairs):
        outs, tops = [[], []], [[], []]
        for h in range(2):
            for i in range(4):
                span = (i + 1) * block
                rows = slice(i * block, span)
                s = dot_nt(q_ref[p, h, rows, :], k_ref[p, h, :span, :])
                diag = jnp.where(causal, s[:, i * block:], NEG)
                s = jnp.concatenate([s[:, :i * block], diag], axis=1) if i else diag
                top = jnp.max(s, axis=1, keepdims=True)
                outs[h].append(dot_nn(jnp.exp(s - top).astype(BF16), v_ref[p, h, :span, :]))
                tops[h].append(top)
        for i in range(4):
            rows = slice(i * block, (i + 1) * block)
            sums = pltpu.roll(jnp.where(low, outs[1][i], outs[0][i]), HEAD_DIM, 1)
            att_ref[p, rows, :] = (jnp.where(low, outs[0][i], outs[1][i]) / sums).astype(BF16)
            for h in range(2):
                total = outs[h][i]
                lse = tops[h][i] + jnp.log(total)
                first = (1 - h) * HEAD_DIM
                mine = q_ref[p, h, rows, :].astype(F32)
                for n, piece in enumerate(split_three(-lse)):
                    mine = jnp.where(lane == first + n, piece, mine)
                q_ref[p, h, rows, :] = mine.astype(BF16)
        io.send(q_ref.at[p], q_out.at[p])
        io.send(att_ref.at[p], att_out.at[p])
        for t in range(2):
            place = 2 * (chip if t == 0 else far) + other
            io.send(
                att_ref.at[p, aligned(place, block), :], oth_out.at[p, t * block:(t + 1) * block, :]
            )
    io.drain()


def attention_forward(scal, kept, recv, kept_o, recv_o, wq, wk, wv, tables):
    block, width = kept.shape
    full = 4 * block
    cols = width // 2
    pairs = cols // PAIR
    aug = (pairs, 2, full, PAIR)
    return kernel_call(
        attention_forward_kernel, "attention_forward",
        [(aug, BF16), (aug, BF16), (aug, BF16), ((pairs, full, PAIR), BF16),
         ((pairs, full // 2, PAIR), BF16), ((full, width), BF16)],
        [sspec()] + [aspec()] * 4 + [hspec()] * 4,
        [
            pltpu.VMEM((full, width), BF16),
            pltpu.VMEM((width, 3 * cols), BF16),
            pltpu.VMEM((3, full, PAIR), F32),
            pltpu.VMEM(aug, BF16),
            pltpu.VMEM(aug, BF16),
            pltpu.VMEM(aug, BF16),
            pltpu.VMEM((pairs, full, PAIR), BF16),
            pltpu.SemaphoreType.DMA((11 + 4 * pairs,)),
        ],
        2 * full * width * cols * 3 + 4 * full * full * cols, 16_000_000, full * full * 6, vmem=20,
    )(scal, kept, recv, kept_o, recv_o, wq, wk, wv, tables)


def load_attended(io, target, att, got, places, block):
    pairs = att.shape[0]
    copies = []
    for p in range(pairs):
        for t in range(2):
            copies.append(
                io.start(
                    att.at[p, aligned(places[t], block), :],
                    target.at[t * block:(t + 1) * block, p * PAIR:(p + 1) * PAIR],
                )
            )
        copies.append(io.start(got.at[p], target.at[:, (pairs + p) * PAIR:(pairs + p + 1) * PAIR]))
    return copies


def load_output_weight(io, target, wo, core, cols):
    return [
        io.start(wo.at[aligned(core, cols), :], target.at[0:cols, :]),
        io.start(wo.at[aligned(1 - core, cols), :], target.at[cols:, :]),
    ]


def ffn_forward_kernel(
    scal, gain_a, gain_m, kept, recv, att, got, ct_kept, ct_recv, wo, wg, wu, wd,
    att_ref, x1_low_ref, norm1_ref, root1_ref, gate_ref, up_ref, dm_ref, dmixed2_ref, gain_row_ref,
    lay_kept, lay_away, keep_a, keep_b, send_a, send_b,
    wo_buf, wg_buf, wu_buf, wd_buf, x_ref, ct_ref, lay_ref, hid_ref, keep_ref, send_ref, sems,
):
    core, chip, length = scal[0], scal[1], scal[2]
    block, width = kept.shape
    cols = width // 2
    ff = wg.shape[1]
    step = ff // 4
    other, far = 1 - core, 1 - chip
    places = (2 * chip + core, 2 * far + core)
    io = Copies(sems)
    first = load_attended(io, att_ref, att, got, places, block)
    first += load_output_weight(io, wo_buf, wo, core, cols)
    first.append(io.start(kept, x_ref.at[0:block, :]))
    first.append(io.start(recv, x_ref.at[block:, :]))
    weights = []
    for f in range(4):
        part = slice(f * step, (f + 1) * step)
        weights.append(io.start(wg.at[:, part], wg_buf.at[:, part]))
        weights.append(io.start(wu.at[:, part], wu_buf.at[:, part]))
    down = io.start(wd, wd_buf)
    late = [io.start(ct_kept, ct_ref.at[0:block, :]), io.start(ct_recv, ct_ref.at[block:, :])]
    for copy in first:
        copy.wait()
    mixed = x_ref[...].astype(F32) + dot_nn(att_ref[...], wo_buf[...])
    root = lax.rsqrt(mean_row(mixed * mixed) + EPS)
    norm = mixed * root
    norm1_ref[...] = norm
    root1_ref[...] = jnp.broadcast_to(root, root1_ref.shape)
    x1_low_ref[...] = (norm * gain_a[...]).astype(BF16)
    for f in range(4):
        part = slice(f * step, (f + 1) * step)
        weights[2 * f].wait()
        weights[2 * f + 1].wait()
        gate = dot_nn(x1_low_ref[...], wg_buf[:, part])
        up = dot_nn(x1_low_ref[...], wu_buf[:, part])
        hid_ref[:, part] = (gate * jax.nn.sigmoid(gate) * up).astype(BF16)
        gate_ref[:, part] = gate.astype(BF16)
        up_ref[:, part] = up.astype(BF16)
    down.wait()
    mixed = norm1_ref[...] * gain_a[...] + dot_nn(hid_ref[...], wd_buf[...])
    root = lax.rsqrt(mean_row(mixed * mixed) + EPS)
    norm = mixed * root
    slot = lax.broadcasted_iota(jnp.int32, (2 * block, 1), 0)
    slot = jnp.where(slot < block, places[0] * block + slot, (places[1] - 1) * block + slot)
    valid = (slot < length).astype(F32)
    lay_ref[...] = (valid * (norm * gain_m[...])).astype(BF16)
    io.send(lay_ref.at[0:block, :], lay_kept)
    io.send(lay_ref.at[block:, :], lay_away)
    for copy in late:
        copy.wait()
    d_out = valid * ct_ref[...].astype(F32)
    gain_row = jnp.sum(d_out * norm, axis=0, keepdims=True)
    gain_row_ref[...] = jnp.broadcast_to(gain_row, gain_row_ref.shape)
    d_norm = d_out * gain_m[...]
    d_mixed = root * (d_norm - norm * mean_row(d_norm * norm))
    dmixed2_ref[...] = d_mixed
    dm_ref[...] = d_mixed.astype(BF16)
    right = jnp.concatenate([dm_ref[:, aligned(other, cols)], dm_ref[:, aligned(core, cols)]], axis=1)
    height = ff // SUPER
    cut = keep_a.shape[1]
    for f in range(4):
        grad = dot_tn(hid_ref[:, f * step:(f + 1) * step], right)
        pack(send_ref, grad[:, :cols], f * step // height, 0, height)
        pack(keep_ref, grad[:, cols:], f * step // height, 0, height)
        for b in range(f * step // height, (f + 1) * step // height):
            at = reversed_bits(b, 4)
            io.send(send_ref.at[at, :cut, :], send_a.at[at])
            io.send(send_ref.at[at, cut:, :], send_b.at[at])
            io.send(keep_ref.at[at, :cut, :], keep_a.at[at])
            io.send(keep_ref.at[at, cut:, :], keep_b.at[at])
    io.drain()


def ffn_forward(scal, gain_a, gain_m, kept, recv, att, got, ct_kept, ct_recv, wo, wg, wu, wd):
    block, width = kept.shape
    ff = wg.shape[1]
    tokens, cols = 2 * block, width // 2
    rows = ff // SUPER * (cols // LANES)
    half, packed = ((block, width), BF16), ((SUPER, rows, LANES), BF16)
    part = ((SUPER, rows // 2, LANES), BF16)
    rows16, rows32 = ((tokens, width), BF16), ((tokens, width), F32)
    hidden = ((tokens, ff), BF16)
    return kernel_call(
        ffn_forward_kernel, "ffn_forward",
        [half, half, part, part, part, part],
        [sspec(), vspec(), vspec()] + [aspec()] * 2 + [hspec()] + [aspec()] * 3 + [hspec()] * 4,
        [pltpu.VMEM(*z) for z in [
            ((width, width), BF16), ((width, ff), BF16), ((width, ff), BF16), ((ff, width), BF16),
            rows16, rows16, rows16, hidden, packed, packed,
        ]] + [pltpu.SemaphoreType.DMA((17 + 3 * (cols // PAIR) + 4 * SUPER,))],
        2 * tokens * width * (width + 4 * ff), 18_000_000, tokens * ff, vmem=30,
        resident=[
            rows16, rows16, rows32, ((tokens, LANES), F32), hidden, hidden, rows16, rows32,
            ((8, width), F32),
        ],
    )(scal, gain_a, gain_m, kept, recv, att, got, ct_kept, ct_recv, wo, wg, wu, wd)


def ffn_hidden_kernel(
    scal, dm_ref, gate_ref, up_ref, x1_low_ref, wd,
    dgate_ref, dup_ref,
    keep_a, keep_b, send_a, send_b,
    wd_buf, keep_ref, send_ref, sems,
):
    core = scal[0]
    ff, width = wd.shape
    step = ff // 4
    height = width // SUPER
    rows = step // LANES * height
    io = Copies(sems)
    weights = [
        io.start(wd.at[aligned(side * 2 + sub, step), :], wd_buf.at[n * step:(n + 1) * step, :])
        for n, (side, sub) in enumerate(((1 - core, 0), (1 - core, 1), (core, 0), (core, 1)))
    ]
    for target, outs, side in ((send_ref, (send_a, send_b), 1 - core), (keep_ref, (keep_a, keep_b), core)):
        for sub in range(2):
            part = aligned(side * 2 + sub, step)
            n = sub if target is send_ref else 2 + sub
            weights[n].wait()
            d_hid = dot_nt(dm_ref[...], wd_buf[n * step:(n + 1) * step, :])
            g = gate_ref[:, part].astype(F32)
            sigma = jax.nn.sigmoid(g)
            d_up = (d_hid * (g * sigma)).astype(BF16)
            d_gate = (
                d_hid * up_ref[:, part].astype(F32) * sigma * (1.0 + g * (1.0 - sigma))
            ).astype(BF16)
            dgate_ref[:, part] = d_gate
            dup_ref[:, part] = d_up
            for n, right in ((0, d_gate), (1, d_up)):
                row = (2 * n + sub) * rows
                pack(target, dot_tn(x1_low_ref[...], right), 0, row, height)
                io.send(
                    target.at[:, row:row + rows, :], outs[n].at[:, sub * rows:(sub + 1) * rows, :]
                )
    io.drain()


def ffn_hidden(scal, dm, gate, up, x1_low, wd):
    tokens, ff = gate.shape
    width = dm.shape[1]
    rows = width // SUPER * (ff // 2 // LANES)
    part, packed = ((SUPER, rows, LANES), BF16), ((SUPER, 2 * rows, LANES), BF16)
    hidden = ((tokens, ff), BF16)
    return kernel_call(
        ffn_hidden_kernel, "ffn_hidden", [part, part, part, part],
        [sspec()] + [vspec()] * 4 + [hspec()],
        [pltpu.VMEM((ff, width), BF16), pltpu.VMEM(*packed), pltpu.VMEM(*packed),
         pltpu.SemaphoreType.DMA((12,))],
        2 * tokens * width * 3 * ff, 10_000_000, tokens * ff, vmem=20,
        resident=[hidden, hidden],
    )(scal, dm, gate, up, x1_low, wd)


def ffn_backward_kernel(
    scal, gain_a, gain_row_m, dgate_ref, dup_ref, dmixed2_ref, norm1_ref, root1_ref, att_ref,
    wo, wg, wu,
    dmixed1_out, do_out, do_send_out, send_out, keep_out,
    wo_buf, wg_buf, wu_buf, dmixed1_ref, do_ref, do_send_ref, send_ref, keep_ref, da_ref, sems,
):
    core = scal[0]
    tokens, width = dmixed2_ref.shape
    cols = width // 2
    height = width // SUPER
    chunks = cols // LANES
    other = 1 - core
    ff = wg.shape[1]
    io = Copies(sems)
    weights = []
    for f in range(2):
        part = slice(f * ff // 2, (f + 1) * ff // 2)
        for weight, buffer in ((wg, wg_buf), (wu, wu_buf)):
            weights.append(io.start(weight.at[:, part], buffer.at[:, part]))
    last = load_output_weight(io, wo_buf, wo, core, cols)
    d_x1 = dmixed2_ref[...]
    for f in range(2):
        part = slice(f * ff // 2, (f + 1) * ff // 2)
        for n, (left, right) in enumerate(((dgate_ref, wg_buf), (dup_ref, wu_buf))):
            weights[2 * f + n].wait()
            d_x1 += dot_nt(left[:, part], right[:, part])
    norm = norm1_ref[...]
    gain_row = jnp.sum(d_x1 * norm, axis=0, keepdims=True)
    d_norm = d_x1 * gain_a[...]
    d_mixed = root1_ref[:, 0:1] * (d_norm - norm * mean_row(d_norm * norm))
    dmixed1_ref[...] = d_mixed
    da_ref[...] = d_mixed.astype(BF16)
    io.send(dmixed1_ref, dmixed1_out)
    for copy in last:
        copy.wait()
    d_att = dot_nt(da_ref[...], wo_buf[...]).astype(BF16)
    for p in range(chunks):
        do_ref[p] = d_att[:, p * LANES:(p + 1) * LANES]
        do_send_ref[p] = d_att[:, cols + p * LANES:cols + (p + 1) * LANES]
    io.send(do_ref, do_out)
    io.send(do_send_ref, do_send_out)
    right = jnp.concatenate([da_ref[:, aligned(other, cols)], da_ref[:, aligned(core, cols)]], axis=1)
    grad = dot_tn(att_ref[...], right).astype(BF16)
    for heads, row0 in ((core, 0), (other, cols)):
        for b in range(cols // height):
            position = 2 * reversed_bits(b, 3) + heads
            for j in range(2 * chunks):
                target = send_ref if j < chunks else keep_ref
                target[position, (j % chunks) * height:(j % chunks + 1) * height, :] = grad[
                    row0 + b * height:row0 + (b + 1) * height, j * LANES:(j + 1) * LANES
                ]
    for target, half in ((send_ref, other), (keep_ref, core)):
        row = jnp.where(half == 0, gain_row, gain_row_m[0:1, :])
        column = jnp.broadcast_to(row, (LANES, width)).T
        pack(target, column, 0, chunks * height, height)
    io.send(send_ref, send_out)
    io.send(keep_ref, keep_out)
    io.drain()


def ffn_backward(scal, gain_a, gain_row_m, dgate, dup, dmixed2, norm1, root1, att, wo, wg, wu):
    tokens, width = dmixed2.shape
    ff = wg.shape[1]
    chunks = width // 2 // LANES
    packed = ((SUPER, (chunks + 1) * (width // SUPER), LANES), BF16)
    split = ((chunks, tokens, LANES), BF16)
    outs = [((tokens, width), F32), split, split, packed, packed]
    return kernel_call(
        ffn_backward_kernel, "ffn_backward", outs,
        [sspec()] + [vspec()] * 8 + [hspec()] * 3,
        [pltpu.VMEM(*z) for z in [
            ((width, width), BF16), ((width, ff), BF16), ((width, ff), BF16),
        ] + outs + [((tokens, width), BF16)]] + [pltpu.SemaphoreType.DMA((11,))],
        2 * tokens * width * (2 * width + 2 * ff), 12_000_000, vmem=24,
    )(scal, gain_a, gain_row_m, dgate, dup, dmixed2, norm1, root1, att, wo, wg, wu)


def attention_backward_kernel(
    scal, qa, ka, va, att, do_own, do_oth, x_all, tables, dmixed1, wq, wk, wv,
    own_out, send_out, grad_a, grad_b,
    qa_ref, ka_ref, va_ref, att_ref, do_ref, x_ref, t_ref, dst_ref, doa_ref, dz_ref, grad_ref,
    w_buf, own_ref, send_ref, sems,
):
    core, chip = scal[0], scal[1]
    pairs, _, full, _ = qa_ref.shape
    block = full // 4
    cols = pairs * PAIR
    scale = float(HEAD_DIM) ** (-0.5)
    other, far = 1 - core, 1 - chip
    io = Copies(sems)
    loads = []
    for p in range(pairs):
        copies = []
        for source, t, place in (
            (do_own.at[p], 0, 2 * chip + core),
            (do_own.at[p], 1, 2 * far + core),
            (do_oth.at[p], 0, 2 * chip + other),
            (do_oth.at[p], 1, 2 * far + other),
        ):
            copies.append(
                io.start(source.at[pl.ds(t * block, block), :], do_ref.at[p, aligned(place, block), :])
            )
        for source, target in ((att, att_ref), (ka, ka_ref), (qa, qa_ref), (va, va_ref)):
            copies.append(io.start(source.at[p], target.at[p]))
        if p == 0:
            copies.append(io.start(tables, t_ref))
        loads.append(copies)
        if p == 0:
            late = io.start(x_all, x_ref)
    last = [io.start(dmixed1, own_ref)]
    for p in range(pairs):
        at = pl.ds(pl.multiple_of(core * cols + p * PAIR, PAIR), PAIR)
        for i, w in enumerate((wq, wk, wv)):
            n = 3 * p + i
            last.append(io.start(w.at[:, at], w_buf.at[:, n * PAIR:(n + 1) * PAIR]))

    lane = lax.broadcasted_iota(jnp.int32, (1, PAIR), 1)
    low = lane < HEAD_DIM
    causal = lax.broadcasted_iota(jnp.int32, (block, block), 0) <= lax.broadcasted_iota(
        jnp.int32, (block, block), 1
    )
    height = x_ref.shape[1] // SUPER

    def back(g, rows):
        return (
            g * t_ref[0, rows, :]
            - pltpu.roll(g, 96, 1) * t_ref[2, rows, :]
            - pltpu.roll(g, 32, 1) * t_ref[1, rows, :]
        ).astype(BF16)

    for p in range(pairs):
        for copy in loads[p]:
            copy.wait()
        grad_do = do_ref[p].astype(F32)
        prod = grad_do * att_ref[p].astype(F32)
        for h in range(2):
            mine = low if h == 0 else jnp.logical_not(low)
            delta = jnp.sum(jnp.where(mine, prod, 0.0), axis=1, keepdims=True)
            doa_ref[h] = beside(lane, h, grad_do, split_three(-delta)).astype(BF16)
        for j in range(4):
            keys = slice(j * block, (j + 1) * block)
            span = slice(j * block, full)
            dk, dv = [], []
            for h in range(2):
                st = dot_nt(ka_ref[p, h, keys, :], qa_ref[p, h, span, :])
                dpt = dot_nt(va_ref[p, h, keys, :], doa_ref[h, span, :])
                pt = jnp.exp(st)
                diag = jnp.where(causal, pt[:, :block], 0.0)
                pt = diag if j == 3 else jnp.concatenate([diag, pt[:, block:]], axis=1)
                dst = (pt * dpt).astype(BF16)
                dst_ref[h, keys, span] = dst
                dv.append(dot_nn(pt.astype(BF16), doa_ref[h, span, :]))
                dk.append(dot_nn(dst, qa_ref[p, h, span, :]))
            dz_ref[p, keys, PAIR:2 * PAIR] = back(jnp.where(low, dk[0], dk[1]), keys)
            dz_ref[p, keys, 2 * PAIR:] = jnp.where(low, dv[0], dv[1]).astype(BF16)
        for i in range(4):
            rows = slice(i * block, (i + 1) * block)
            span = slice(0, (i + 1) * block)
            dq = [dot_tn(dst_ref[h, span, rows], ka_ref[p, h, span, :]) for h in range(2)]
            dz_ref[p, rows, :PAIR] = back(jnp.where(low, dq[0], dq[1]) * scale, rows)
        if p == 0:
            late.wait()
        pack(grad_ref, dot_tn(x_ref[...], dz_ref[p]), 0, p * 3 * height, height)
        part = slice(p * 3 * height, (p + 1) * 3 * height)
        if p == 0:
            io.send(grad_ref.at[:, part, :], grad_a)
        else:
            at = slice((p - 1) * 3 * height, p * 3 * height)
            io.send(grad_ref.at[:, part, :], grad_b.at[:, at, :])
    for copy in last:
        copy.wait()
    for side, target, out in ((other, send_ref, send_out), (core, own_ref, own_out)):
        left = jnp.concatenate(
            [
                jnp.concatenate(
                    [dz_ref[p, aligned(2 * x + side, block), :] for p in range(pairs)], axis=1
                )
                for x in (chip, far)
            ]
        )
        grad = dot_nt(left, w_buf[...])
        if target is own_ref:
            grad += own_ref[...]
        target[...] = grad.astype(target.dtype)
        io.send(target, out)
    io.drain()


def attention_backward(scal, qa, ka, va, att, do_own, do_oth, x_all, tables, dmixed1, wq, wk, wv):
    full, width = x_all.shape
    pairs = qa.shape[0]
    height = 3 * (width // SUPER)
    aug, rows = (qa.shape, BF16), ((pairs, full, PAIR), BF16)
    own, send = (dmixed1.shape, F32), (dmixed1.shape, BF16)
    return kernel_call(
        attention_backward_kernel, "attention_backward",
        [own, send, ((SUPER, height, LANES), BF16), ((SUPER, (pairs - 1) * height, LANES), BF16)],
        [sspec()] + [hspec()] * 5 + [aspec()] + [hspec()] * 6,
        [pltpu.VMEM(*z) for z in [
            aug, aug, aug, rows, rows, ((full, width), BF16), (tables.shape, F32),
            ((2, full, full), BF16), ((2, full, PAIR), BF16), ((pairs, full, 3 * PAIR), BF16),
            ((SUPER, pairs * height, LANES), BF16), ((width, pairs * 3 * PAIR), BF16), own, send,
        ]] + [pltpu.SemaphoreType.DMA((12 * pairs + 5,))],
        pairs * (10 * full * full * PAIR + 9 * full * width * PAIR), 20_000_000, full * full * 6, vmem=28,
    )(scal, qa, ka, va, att, do_own, do_oth, x_all, tables, dmixed1, wq, wk, wv)


def assemble_kernel(layout, scal, stay, got, *outs):
    core = scal[0]
    for source, side in ((stay, core), (got, 1 - core)):
        row = 0
        for out, (rows, chunks) in zip(outs, layout):
            for j in range(chunks):
                out[:, aligned(side * chunks + j, LANES)] = source[row:row + rows, :]
                row += rows


def assemble(scal, stay, got, layout):
    return pl.pallas_call(
        functools.partial(assemble_kernel, layout),
        out_shape=tuple(jax.ShapeDtypeStruct((r, 2 * c * LANES), F32) for r, c in layout),
        in_specs=[sspec(), vspec(), vspec()],
        out_specs=(vspec(),) * len(layout),
        compiler_params=pltpu.CompilerParams(vmem_limit_bytes=16 * 1024 * 1024),
        cost_estimate=pl.CostEstimate(flops=0, bytes_accessed=16 * stay.shape[0] * LANES, transcendentals=0),
        name="assemble",
    )(scal, stay, got)


class Part:
    def __init__(self, names, pieces):
        self.names = list(names)
        dims = (2,) * len(self.names)
        self.pieces = [[leaf.reshape(dims + leaf.shape[-2:]) for leaf in piece] for piece in pieces]

    def join(self, other):
        both = Part([], [])
        both.names, both.pieces = self.names, self.pieces + other.pieces
        return both

    def take(self, name, index):
        at = self.names.index(name)
        return [
            [lax.dynamic_index_in_dim(leaf, index, at, keepdims=False) for leaf in piece]
            for piece in self.pieces
        ]

    def outgoing(self, name, me):
        sums = [sum(leaf.astype(F32) for leaf in piece) for piece in self.take(name, 1 - me)]
        return jnp.concatenate([z.astype(BF16) for z in sums], axis=-2)

    def incoming(self, name, me, got):
        pieces = self.take(name, me)
        self.names.remove(name)
        row = 0
        for piece in pieces:
            rows = piece[0].shape[-2]
            piece.append(lax.slice_in_dim(got, row, row + rows, axis=got.ndim - 2))
            row += rows
        self.pieces = pieces

    def result(self):
        return jnp.concatenate([sum(leaf.astype(F32) for leaf in piece) for piece in self.pieces])


def swap_seq(value, bit):
    return lax.ppermute(value, "seq", [(i, i ^ bit) for i in range(4)])


def after(value, *others):
    return lax.optimization_barrier((value,) + others)[0]


def on_device(
    batch_size,
    hidden_in,
    cotangent,
    lengths,
    w_query,
    w_key,
    w_value,
    w_output,
    w_gate,
    w_up,
    w_down,
    gain_attn,
    gain_mlp,
):
    seqs, block, width = hidden_in.shape
    tokens = seqs * block
    cols = width // 2
    pairs = cols // PAIR
    height = width // SUPER
    rank = lax.axis_index("seq")
    batch = lax.axis_index("batch")
    chip, core = rank // 2, rank % 2
    far, other = 1 - chip, 1 - core

    def pick(z, index):
        return lax.dynamic_index_in_dim(z, index, 0, keepdims=False)

    def home(kept, back):
        first = chip == 0
        return jnp.stack([jnp.where(first, kept, back), jnp.where(first, back, kept)])

    kept = pick(hidden_in, chip)
    recv = swap_seq(pick(hidden_in, far), 2)
    kept_o = swap_seq(kept, 1)
    recv_o = swap_seq(recv, 1)
    ct_kept = pick(cotangent, chip)
    ct_recv = swap_seq(after(pick(cotangent, far), recv), 2)
    scal = jnp.stack([core, chip, pick(lengths, chip)]).astype(jnp.int32)
    w_query, w_key, w_value, w_output, w_gate, w_up, w_down, tables = [
        pltpu.with_memory_space_constraint(z, pltpu.HBM)
        for z in (w_query, w_key, w_value, w_output, w_gate, w_up, w_down, rope_tables(4 * block))
    ]
    gain_a, gain_m = gain_attn[None, :], gain_mlp[None, :]

    bits = batch_size.bit_length() - 1
    names = ["b%d" % i for i in reversed(range(bits))] + ["x"]
    top, rest = names[:4][::-1], names[4:]

    def index_of(name):
        return chip if name == "x" else (batch >> int(name[1:])) & 1

    def exchange(value, name):
        if name == "x":
            return swap_seq(value, 2)
        bit = 1 << int(name[1:])
        return lax.ppermute(value, "batch", [(i, i ^ bit) for i in range(batch_size)])

    class Sum:
        def __init__(self, first, second):
            self.parts = [Part(top, first), Part(top, second)]
            self.orders = [[top[0], top[1]], [top[1], top[0]]]
            self.tail = [top[2], top[3]]
            self.both = None

        def out(self):
            if self.orders[0]:
                self.now = [order.pop(0) for order in self.orders]
                self.moving = self.parts
            else:
                if self.both is None:
                    self.both = self.parts[0].join(self.parts[1])
                self.now = [self.tail.pop(0)]
                self.moving = [self.both]
            self.sent = [p.outgoing(n, index_of(n)) for p, n in zip(self.moving, self.now)]
            return self.sent

        def move(self):
            self.got = [exchange(z, n) for z, n in zip(self.sent, self.now)]

        def land(self, *others):
            for part, name, got in zip(self.moving, self.now, self.got):
                part.incoming(name, index_of(name), after(got, *others) if others else got)

    q, k, v, att, att_oth, x_all = attention_forward(
        scal, kept, recv, kept_o, recv_o, w_query, w_key, w_value, tables
    )
    got = swap_seq(att_oth, 1)
    (
        attended, x1_low, norm1, root1, gate, up, dm, dmixed2, gain_row_m,
        lay_kept, lay_away, gd_keep_a, gd_keep_b, gd_send_a, gd_send_b,
    ) = ffn_forward(
        scal, gain_a, gain_m, kept, recv, att, got, ct_kept, ct_recv, w_output, w_gate, w_up, w_down
    )
    gd_got = [swap_seq(gd_send_a, 1), swap_seq(gd_send_b, 1)]
    lay_back = swap_seq(lay_away, 2)
    dgate, dup, gg_keep, gu_keep, gg_send, gu_send = ffn_hidden(scal, dm, gate, up, x1_low, w_down)

    gd_got[0], gd_got[1], lay_back, gg_send, gu_send = lax.optimization_barrier(
        (gd_got[0], gd_got[1], lay_back, gg_send, gu_send)
    )
    down = Sum([[gd_keep_a, gd_got[0]]], [[gd_keep_b, gd_got[1]]])
    sent = down.out()
    scal_c = after(scal, *sent, gg_send)
    down.move()
    gg_got, gu_got = swap_seq(gg_send, 1), swap_seq(gu_send, 1)
    dmixed1, do_own, do_send, wo_send, wo_keep = ffn_backward(
        scal_c, gain_a, gain_row_m, dgate, dup, dmixed2, norm1, root1, attended, w_output, w_gate, w_up
    )

    do_send, wo_send, gg_got, gu_got, *down.got = lax.optimization_barrier(
        (do_send, wo_send, gg_got, gu_got, *down.got)
    )
    do_oth = swap_seq(do_send, 1)
    down.land()
    gate_up = Sum([[gg_keep, gg_got]], [[gu_keep, gu_got]])
    sent = down.out() + gate_up.out()
    scal_d = after(scal, *sent)
    down.move()
    gate_up.move()
    wo_got = swap_seq(wo_send, 1)
    own_in, send_in, grads_a, grads_b = attention_backward(
        scal_d, q, k, v, att, do_own, do_oth, x_all, tables, dmixed1, w_query, w_key, w_value
    )

    send_in, grads_a, grads_b, wo_got, *gots = lax.optimization_barrier(
        (send_in, grads_a, grads_b, wo_got, *down.got, *gate_up.got)
    )
    down.got, gate_up.got = gots[:2], gots[2:]
    got_in = swap_seq(send_in, 1)
    others = Sum([[wo_keep, wo_got], [grads_a]], [[grads_b]])
    others.out()
    others.move()
    gate_up.land()
    gate_up.out()
    gate_up.move()
    down.land()
    down.out()
    down.move()
    g_in = (own_in + got_in.astype(F32)).astype(BF16)
    g_back = swap_seq(g_in[block:], 2)

    down.land()
    down.out()
    down.move()
    gate_up.land()
    gate_up.out()
    gate_up.move()
    others.land()
    others.out()
    others.move()
    down.land()
    gate_up.land()
    gate_up.out()
    gate_up.move()
    others.land()
    others.out()
    others.move()
    gate_up.land()
    others.land()
    others.out()
    others.move()
    others.land()

    high = w_gate.shape[1] // SUPER
    wide = w_gate.shape[1] // 2 // LANES
    layouts = [[(high, pairs)], [(height, wide)] * 2, [(height, pairs), (height, 1)] + [(height, 1)] * (3 * pairs)]
    sums = [down.both.result(), gate_up.both.result(), others.both.result()]
    if rest:
        return finish_general(
            layouts, sums, rest, index_of, exchange, core, pairs,
            home(lay_kept, lay_back), home(g_in[:block], g_back),
        )

    def sides(total, layout):
        row, pieces = 0, []
        for rows, chunks in layout:
            pieces.append(total[row:row + rows * chunks].reshape(chunks, 2, rows // 2, LANES))
            row += rows * chunks
        return [
            jnp.concatenate(
                [lax.dynamic_index_in_dim(z, i, 1, keepdims=False).reshape(-1, LANES) for z in pieces]
            )
            for i in (other, core)
        ]

    away, stay = sides(jnp.concatenate(sums[:2]), layouts[0] + layouts[1])
    g_down, g_gate, g_up = assemble(
        scal, stay, swap_seq(away, 1), [(rows // 2, chunks) for rows, chunks in layouts[0] + layouts[1]]
    )
    away, stay = sides(sums[2], layouts[2])
    last = swap_seq(away, 1)
    half = height // 2
    order = [z.reshape(pairs, 3, half, LANES) for z in (stay[(pairs + 1) * half:], last[(pairs + 1) * half:])]
    by_matrix = [z.transpose(1, 0, 2, 3).reshape(-1, LANES) for z in order]
    stay = jnp.concatenate([stay[: (pairs + 1) * half], by_matrix[0]])
    last = jnp.concatenate([last[: (pairs + 1) * half], by_matrix[1]])
    g_output, gains, g_query, g_key, g_value = assemble(
        scal, stay, last, [(half, pairs), (half, 1)] + [(half, pairs)] * 3
    )
    return (
        home(lay_kept, lay_back), home(g_in[:block], g_back),
        g_query, g_key, g_value, g_output, g_gate, g_up, g_down, gains[:, 0], gains[:, LANES],
    )


def finish_general(layouts, sums, rest, index_of, exchange, core, pairs, layer_out, grad_in):
    def finish(packed, rows, chunks):
        matrix = packed.reshape(chunks, rows, LANES).transpose(1, 0, 2).reshape(rows, chunks * LANES)
        for name in rest:
            matrix = matrix.reshape(2, matrix.shape[0] // 2, matrix.shape[1])
            me = index_of(name)
            away = lax.dynamic_index_in_dim(matrix, 1 - me, 0, keepdims=False)
            stay = lax.dynamic_index_in_dim(matrix, me, 0, keepdims=False)
            matrix = stay + exchange(away.astype(BF16), name).astype(F32)
        matrix = matrix.reshape(2, matrix.shape[0] // 2, matrix.shape[1])
        stay = lax.dynamic_index_in_dim(matrix, core, 0, keepdims=False)
        got = swap_seq(lax.dynamic_index_in_dim(matrix, 1 - core, 0, keepdims=False), 1)
        return jnp.where(
            core == 0,
            jnp.concatenate([stay, got], axis=-1),
            jnp.concatenate([got, stay], axis=-1),
        )

    def matrices(total, layout):
        row, out = 0, []
        for rows, chunks in layout:
            out.append((total[row:row + rows * chunks], rows, chunks))
            row += rows * chunks
        return out

    (down,) = matrices(sums[0], layouts[0])
    gate, up = matrices(sums[1], layouts[1])
    output, gains, *qkv = matrices(sums[2], layouts[2])
    height = output[1]
    by_matrix = [
        (jnp.concatenate([qkv[3 * p + i][0] for p in range(pairs)]), height, pairs) for i in range(3)
    ]
    outs = [finish(*z) for z in by_matrix + [output, gate, up, down, gains]]
    gains = outs.pop()
    return (layer_out, grad_in, *outs, gains[:, 0], gains[:, LANES])


def solution(mesh):
    tokens = P("batch", "seq", None)
    rows = P(("batch", "seq"), None)
    return jax.shard_map(
        functools.partial(on_device, mesh.shape["batch"]),
        mesh=mesh,
        in_specs=(tokens, tokens, P("batch")) + (P(),) * 9,
        out_specs=(tokens, tokens) + (rows,) * 7 + (P(("batch", "seq")),) * 2,
        check_vma=False,
    )
```

```python
import functools

import jax
import jax.numpy as jnp
import numpy as np
from jax import lax
from jax.experimental import pallas as pl
from jax.experimental.pallas import tpu as pltpu
from jax.sharding import PartitionSpec as P

HEADS = 12
HEAD_DIM = 64
PAIR = 2 * HEAD_DIM

EPS = 1e-06
NEG = -1e30
LANES = 128
SUPER = 16

F32 = jnp.float32
BF16 = jnp.bfloat16


def dot_nn(left, right):
    return lax.dot_general(left, right, (((1,), (0,)), ((), ())), preferred_element_type=F32)


def dot_nt(left, right):
    return lax.dot_general(left, right, (((1,), (1,)), ((), ())), preferred_element_type=F32)


def dot_tn(left, right):
    return lax.dot_general(left, right, (((0,), (0,)), ((), ())), preferred_element_type=F32)


def rope_tables(count):
    half = HEAD_DIM // 2
    inverse = 10000.0 ** (-(np.arange(half, dtype=np.float32) * np.float32(2.0)) / HEAD_DIM)
    angles = np.arange(count, dtype=np.float32)[:, None] * inverse.astype(np.float32)[None, :]
    cosine, sine = np.cos(angles), np.sin(angles)
    zero = np.zeros_like(sine)
    tables = (
        np.concatenate([cosine] * 4, axis=-1),
        np.concatenate([zero, sine] * 2, axis=-1),
        np.concatenate([-sine, zero] * 2, axis=-1),
    )
    return jnp.asarray(np.stack(tables), F32)


def start(source, target, sem):
    copy = pltpu.make_async_copy(source, target, sem)
    copy.start()
    return copy


def aligned(index, size):
    return pl.ds(pl.multiple_of(index * size, size), size)


def vspec():
    return pl.BlockSpec(memory_space=pltpu.VMEM)


def hspec():
    return pl.BlockSpec(memory_space=pltpu.HBM)


def aspec():
    return pl.BlockSpec(memory_space=pl.ANY)


def sspec():
    return pl.BlockSpec(memory_space=pltpu.SMEM)


def mean_row(z):
    return jnp.sum(z, axis=1, keepdims=True) * (1.0 / z.shape[1])


def reversed_bits(index, bits):
    out = 0
    for i in range(bits):
        out |= ((index >> i) & 1) << (bits - 1 - i)
    return out


def xy_first(b):
    return reversed_bits(b, 4)


def xz_first(b):
    zh, zl, y, x = (b >> 3) & 1, (b >> 2) & 1, (b >> 1) & 1, b & 1
    return x * 8 + zl * 4 + y * 2 + zh


def yz_first(b):
    zh, zl, y, x = (b >> 3) & 1, (b >> 2) & 1, (b >> 1) & 1, b & 1
    return y * 8 + zl * 4 + x * 2 + zh


def zy_first(b):
    zh, zl, y, x = (b >> 3) & 1, (b >> 2) & 1, (b >> 1) & 1, b & 1
    return zl * 8 + y * 4 + x * 2 + zh


def pack(out_ref, value, place, block0, row0, height):
    low = value.astype(BF16)
    for b in range(value.shape[0] // height):
        for j in range(value.shape[1] // LANES):
            out_ref[place(block0 + b), row0 + j * height:row0 + (j + 1) * height, :] = low[
                b * height:(b + 1) * height, j * LANES:(j + 1) * LANES
            ]


def kernel_call(
    kernel, name, outs, specs, scratch, flops, moved, exps=0, resident=(), vmem=16, free=(), through=()
):
    count = len(resident) + len(outs)
    through = tuple(through)
    if through:
        inner = kernel

        def kernel(*refs):
            at = len(specs) + count
            inner(*refs[:at], *refs[at + len(through):])

    return pl.pallas_call(
        kernel,
        out_shape=tuple(pltpu.VMEM(*z) for z in resident)
        + tuple(
            jax.ShapeDtypeStruct(*z) if i in free else pltpu.HBM(*z) for i, z in enumerate(outs)
        )
        + tuple(pltpu.HBM(*z) for _, z in through),
        in_specs=specs,
        out_specs=(vspec(),) * len(resident)
        + tuple(aspec() if i in free else hspec() for i in range(len(outs)))
        + (hspec(),) * len(through),
        input_output_aliases={n: count + i for i, (n, _) in enumerate(through)},
        scratch_shapes=scratch,
        compiler_params=pltpu.CompilerParams(vmem_limit_bytes=vmem * 1024 * 1024),
        cost_estimate=pl.CostEstimate(flops=flops, bytes_accessed=moved, transcendentals=exps),
        name=name,
    )


class Copies:
    def __init__(self, sems):
        self.sems, self.used, self.open = sems, 0, []

    def start(self, source, target):
        copy = start(source, target, self.sems.at[self.used])
        self.used += 1
        return copy

    def send(self, source, target):
        self.open.append(self.start(source, target))

    def drain(self):
        for copy in self.open:
            copy.wait()


def split_three(value):
    first = value.astype(BF16).astype(F32)
    rest = value - first
    second = rest.astype(BF16).astype(F32)
    return first, second, (rest - second).astype(BF16).astype(F32)


def beside(lane, head, mine, pieces):
    own = (lane < HEAD_DIM) if head == 0 else (lane >= HEAD_DIM)
    first = (1 - head) * HEAD_DIM
    out = jnp.zeros_like(mine)
    for i, piece in enumerate(pieces):
        out = jnp.where(lane == first + i, piece, out)
    return jnp.where(own, mine, out)


def attention_forward_kernel(
    scal, kept, recv, kept_o, recv_o, wq, wk, wv, tables,
    q_out, k_out, v_out, att_out, oth_out, x_out, w_out, t_out,
    x_ref, w_buf, t_ref, q_ref, k_ref, v_ref, att_ref, sems,
):
    core, chip, length = scal[0], scal[1], scal[2]
    block = kept.shape[0]
    full = 4 * block
    pairs = q_ref.shape[0]
    cols = pairs * PAIR
    other, far = 1 - core, 1 - chip
    io = Copies(sems)
    columns = pl.ds(pl.multiple_of(core * cols, PAIR), cols)
    needed = []
    for i, w in enumerate((wq, wk, wv)):
        needed.append(io.start(w.at[:, columns], w_buf.at[:, i * cols:(i + 1) * cols]))
    for source, place in (
        (kept, 2 * chip + core),
        (recv, 2 * far + core),
        (kept_o, 2 * chip + other),
        (recv_o, 2 * far + other),
    ):
        needed.append(io.start(source, x_ref.at[aligned(place, block), :]))
    needed.append(io.start(tables, t_ref))
    for copy in needed:
        copy.wait()
    for source, out in ((x_ref, x_out), (w_buf, w_out), (t_ref, t_out)):
        io.send(source, out)
    scale = float(HEAD_DIM) ** (-0.5)
    lane = lax.broadcasted_iota(jnp.int32, (1, PAIR), 1)
    low = lane < HEAD_DIM
    for t in range(2):
        rows = slice(t * 2 * block, (t + 1) * 2 * block)
        z = dot_nn(x_ref[rows, :], w_buf[...])
        c, a, b = t_ref[0, rows, :], t_ref[1, rows, :], t_ref[2, rows, :]
        slot = t * 2 * block + lax.broadcasted_iota(jnp.int32, (2 * block, PAIR), 0)
        bias = jnp.where(slot < length, 0.0, NEG)
        for p in range(3 * pairs):
            part = z[:, p * PAIR:(p + 1) * PAIR]
            if p < 2 * pairs:
                part = part * c + pltpu.roll(part, 32, 1) * a + pltpu.roll(part, 96, 1) * b
            for h in range(2):
                if p < pairs:
                    mine = part.astype(BF16).astype(F32) * scale
                    q_ref[p, h, rows, :] = beside(lane, h, mine, (0.0, 0.0, 0.0, 1.0)).astype(BF16)
                elif p < 2 * pairs:
                    k_ref[p - pairs, h, rows, :] = beside(
                        lane, h, part, (1.0, 1.0, 1.0, bias)
                    ).astype(BF16)
                else:
                    own = low if h == 0 else jnp.logical_not(low)
                    v_ref[p - 2 * pairs, h, rows, :] = jnp.where(own, part, 1.0).astype(BF16)
    io.send(k_ref, k_out)
    io.send(v_ref, v_out)

    causal = lax.broadcasted_iota(jnp.int32, (block, block), 1) <= lax.broadcasted_iota(
        jnp.int32, (block, block), 0
    )
    for p in range(pairs):
        outs, tops = [[], []], [[], []]
        for h in range(2):
            for i in range(4):
                span = (i + 1) * block
                rows = slice(i * block, span)
                s = dot_nt(q_ref[p, h, rows, :], k_ref[p, h, :span, :])
                diag = jnp.where(causal, s[:, i * block:], NEG)
                s = jnp.concatenate([s[:, :i * block], diag], axis=1) if i else diag
                top = jnp.max(s, axis=1, keepdims=True)
                outs[h].append(dot_nn(jnp.exp(s - top).astype(BF16), v_ref[p, h, :span, :]))
                tops[h].append(top)
        for i in range(4):
            rows = slice(i * block, (i + 1) * block)
            sums = pltpu.roll(jnp.where(low, outs[1][i], outs[0][i]), HEAD_DIM, 1)
            att_ref[p, rows, :] = (jnp.where(low, outs[0][i], outs[1][i]) / sums).astype(BF16)
            for h in range(2):
                total = outs[h][i]
                lse = tops[h][i] + jnp.log(total)
                first = (1 - h) * HEAD_DIM
                mine = q_ref[p, h, rows, :].astype(F32)
                for n, piece in enumerate(split_three(-lse)):
                    mine = jnp.where(lane == first + n, piece, mine)
                q_ref[p, h, rows, :] = mine.astype(BF16)
        io.send(q_ref.at[p], q_out.at[p])
        io.send(att_ref.at[p], att_out.at[p])
        for t in range(2):
            place = 2 * (chip if t == 0 else far) + other
            io.send(
                att_ref.at[p, aligned(place, block), :], oth_out.at[p, t * block:(t + 1) * block, :]
            )
    io.drain()


def attention_forward(scal, kept, recv, kept_o, recv_o, wq, wk, wv, tables):
    block, width = kept.shape
    full = 4 * block
    cols = width // 2
    pairs = cols // PAIR
    aug = (pairs, 2, full, PAIR)
    return kernel_call(
        attention_forward_kernel, "attention_forward",
        [(aug, BF16), (aug, BF16), (aug, BF16), ((pairs, full, PAIR), BF16),
         ((pairs, full // 2, PAIR), BF16), ((full, width), BF16),
         ((width, 3 * cols), BF16), (tables.shape, F32)],
        [sspec()] + [aspec()] * 4 + [hspec()] * 4,
        [
            pltpu.VMEM((full, width), BF16),
            pltpu.VMEM((width, 3 * cols), BF16),
            pltpu.VMEM((3, full, PAIR), F32),
            pltpu.VMEM(aug, BF16),
            pltpu.VMEM(aug, BF16),
            pltpu.VMEM(aug, BF16),
            pltpu.VMEM((pairs, full, PAIR), BF16),
            pltpu.SemaphoreType.DMA((13 + 4 * pairs,)),
        ],
        2 * full * width * cols * 3 + 4 * full * full * cols, 16_000_000, full * full * 6, vmem=52,
    )(scal, kept, recv, kept_o, recv_o, wq, wk, wv, tables)


def load_attended(io, target, att, got, places, block):
    pairs = att.shape[0]
    copies = []
    for p in range(pairs):
        for t in range(2):
            copies.append(
                io.start(
                    att.at[p, aligned(places[t], block), :],
                    target.at[t * block:(t + 1) * block, p * PAIR:(p + 1) * PAIR],
                )
            )
        copies.append(io.start(got.at[p], target.at[:, (pairs + p) * PAIR:(pairs + p + 1) * PAIR]))
    return copies


def load_output_weight(io, target, wo, core, cols):
    return [
        io.start(wo.at[aligned(core, cols), :], target.at[0:cols, :]),
        io.start(wo.at[aligned(1 - core, cols), :], target.at[cols:, :]),
    ]


def ffn_forward_kernel(
    scal, gain_a, gain_m, kept, recv, att, got, ct_kept, ct_recv, wo, wg, wu, wd,
    att_ref, norm1_ref, root1_ref, dmixed2_ref, gain_row_ref, dgate_ref, dup_ref,
    lay_kept, lay_away, down_keep, down_send, gate_keep, gate_send, up_keep, up_send,
    wo_buf, wg_buf, wu_buf, wd_buf, x_ref, ct_ref, lay_ref, x1_low_ref, dm_ref, gate_ref, up_ref,
    hid_ref, dk_ref, ds_ref, gk_ref, gs_ref, uk_ref, us_ref, sems,
):
    core, chip, length = scal[0], scal[1], scal[2]
    block, width = kept.shape
    cols = width // 2
    ff = wg.shape[1]
    step = ff // 4
    other, far = 1 - core, 1 - chip
    places = (2 * chip + core, 2 * far + core)
    io = Copies(sems)
    first = load_attended(io, att_ref, att, got, places, block)
    first += load_output_weight(io, wo_buf, wo, core, cols)
    first.append(io.start(kept, x_ref.at[0:block, :]))
    first.append(io.start(recv, x_ref.at[block:, :]))
    weights = []
    for f in range(4):
        part = slice(f * step, (f + 1) * step)
        weights.append(io.start(wg.at[:, part], wg_buf.at[:, part]))
        weights.append(io.start(wu.at[:, part], wu_buf.at[:, part]))
    down = io.start(wd, wd_buf)
    late = [io.start(ct_kept, ct_ref.at[0:block, :]), io.start(ct_recv, ct_ref.at[block:, :])]
    for copy in first:
        copy.wait()
    mixed = x_ref[...].astype(F32) + dot_nn(att_ref[...], wo_buf[...])
    root = lax.rsqrt(mean_row(mixed * mixed) + EPS)
    norm = mixed * root
    norm1_ref[...] = norm
    root1_ref[...] = jnp.broadcast_to(root, root1_ref.shape)
    x1_low_ref[...] = (norm * gain_a[...]).astype(BF16)
    for f in range(4):
        part = slice(f * step, (f + 1) * step)
        weights[2 * f].wait()
        weights[2 * f + 1].wait()
        gate = dot_nn(x1_low_ref[...], wg_buf[:, part])
        up = dot_nn(x1_low_ref[...], wu_buf[:, part])
        hid_ref[:, part] = (gate * jax.nn.sigmoid(gate) * up).astype(BF16)
        gate_ref[:, part] = gate.astype(BF16)
        up_ref[:, part] = up.astype(BF16)
    down.wait()
    mixed = norm1_ref[...] * gain_a[...] + dot_nn(hid_ref[...], wd_buf[...])
    root = lax.rsqrt(mean_row(mixed * mixed) + EPS)
    norm = mixed * root
    slot = lax.broadcasted_iota(jnp.int32, (2 * block, 1), 0)
    slot = jnp.where(slot < block, places[0] * block + slot, (places[1] - 1) * block + slot)
    valid = (slot < length).astype(F32)
    lay_ref[...] = (valid * (norm * gain_m[...])).astype(BF16)
    io.send(lay_ref.at[0:block, :], lay_kept)
    io.send(lay_ref.at[block:, :], lay_away)
    for copy in late:
        copy.wait()
    d_out = valid * ct_ref[...].astype(F32)
    gain_row = jnp.sum(d_out * norm, axis=0, keepdims=True)
    gain_row_ref[...] = jnp.broadcast_to(gain_row, gain_row_ref.shape)
    d_norm = d_out * gain_m[...]
    d_mixed = root * (d_norm - norm * mean_row(d_norm * norm))
    dmixed2_ref[...] = d_mixed
    dm_ref[...] = d_mixed.astype(BF16)
    right = jnp.concatenate([dm_ref[:, aligned(other, cols)], dm_ref[:, aligned(core, cols)]], axis=1)
    height = ff // SUPER
    for f in range(4):
        grad = dot_tn(hid_ref[:, f * step:(f + 1) * step], right)
        pack(ds_ref, grad[:, :cols], zy_first, f * step // height, 0, height)
        pack(dk_ref, grad[:, cols:], zy_first, f * step // height, 0, height)
    io.send(ds_ref, down_send)
    io.send(dk_ref, down_keep)
    height = width // SUPER
    rows = step // LANES * height
    for gate_part, gate_out, up_part, up_out, side in (
        (gs_ref, gate_send, us_ref, up_send, other), (gk_ref, gate_keep, uk_ref, up_keep, core),
    ):
        for sub in range(2):
            part = aligned(side * 2 + sub, step)
            d_hid = dot_nt(dm_ref[...], wd_buf[part, :])
            g = gate_ref[:, part].astype(F32)
            sigma = jax.nn.sigmoid(g)
            d_up = (d_hid * (g * sigma)).astype(BF16)
            d_gate = (
                d_hid * up_ref[:, part].astype(F32) * sigma * (1.0 + g * (1.0 - sigma))
            ).astype(BF16)
            dgate_ref[:, part] = d_gate
            dup_ref[:, part] = d_up
            pack(gate_part, dot_tn(x1_low_ref[...], d_gate), xz_first, 0, sub * rows, height)
            pack(up_part, dot_tn(x1_low_ref[...], d_up), yz_first, 0, sub * rows, height)
            at = slice(sub * rows, (sub + 1) * rows)
            io.send(gate_part.at[:, at, :], gate_out.at[:, at, :])
            io.send(up_part.at[:, at, :], up_out.at[:, at, :])
    io.drain()


def ffn_forward(scal, gain_a, gain_m, kept, recv, att, got, ct_kept, ct_recv, wo, wg, wu, wd):
    block, width = kept.shape
    ff = wg.shape[1]
    tokens, cols = 2 * block, width // 2
    half = ((block, width), BF16)
    down = ((SUPER, ff // SUPER * (cols // LANES), LANES), BF16)
    wide = ((SUPER, width // SUPER * (ff // 2 // LANES), LANES), BF16)
    rows16, rows32 = ((tokens, width), BF16), ((tokens, width), F32)
    hidden = ((tokens, ff), BF16)
    return kernel_call(
        ffn_forward_kernel, "ffn_forward", [half, half, down, down, wide, wide, wide, wide],
        [sspec(), vspec(), vspec()] + [aspec()] * 2 + [hspec()] + [aspec()] * 3 + [hspec()] * 4,
        [pltpu.VMEM(*z) for z in [
            ((width, width), BF16), ((width, ff), BF16), ((width, ff), BF16), ((ff, width), BF16),
            rows16, rows16, rows16, rows16, rows16, hidden, hidden, hidden,
            down, down, wide, wide, wide, wide,
        ]] + [pltpu.SemaphoreType.DMA((27 + 3 * (cols // PAIR),))],
        2 * tokens * width * (width + 7 * ff), 26_000_000, 2 * tokens * ff, vmem=44, free=range(8),
        resident=[rows16, rows32, ((tokens, LANES), F32), rows32, ((8, width), F32), hidden, hidden],
    )(scal, gain_a, gain_m, kept, recv, att, got, ct_kept, ct_recv, wo, wg, wu, wd)


def ffn_backward_kernel(
    scal, gain_a, gain_row_m, dgate_ref, dup_ref, dmixed2_ref, norm1_ref, root1_ref, att_ref,
    wo, wg, wu,
    dmixed1_out, do_out, do_send_out, send_out, keep_out,
    wo_buf, wg_buf, wu_buf, dmixed1_ref, do_ref, do_send_ref, send_ref, keep_ref, da_ref, sems,
):
    core = scal[0]
    tokens, width = dmixed2_ref.shape
    cols = width // 2
    height = width // SUPER
    chunks = cols // LANES
    other = 1 - core
    ff = wg.shape[1]
    io = Copies(sems)
    weights = []
    for f in range(2):
        part = slice(f * ff // 2, (f + 1) * ff // 2)
        for weight, buffer in ((wg, wg_buf), (wu, wu_buf)):
            weights.append(io.start(weight.at[:, part], buffer.at[:, part]))
    last = load_output_weight(io, wo_buf, wo, core, cols)
    d_x1 = dmixed2_ref[...]
    for f in range(2):
        part = slice(f * ff // 2, (f + 1) * ff // 2)
        for n, (left, right) in enumerate(((dgate_ref, wg_buf), (dup_ref, wu_buf))):
            weights[2 * f + n].wait()
            d_x1 += dot_nt(left[:, part], right[:, part])
    norm = norm1_ref[...]
    gain_row = jnp.sum(d_x1 * norm, axis=0, keepdims=True)
    d_norm = d_x1 * gain_a[...]
    d_mixed = root1_ref[:, 0:1] * (d_norm - norm * mean_row(d_norm * norm))
    dmixed1_ref[...] = d_mixed
    da_ref[...] = d_mixed.astype(BF16)
    io.send(dmixed1_ref, dmixed1_out)
    for copy in last:
        copy.wait()
    d_att = dot_nt(da_ref[...], wo_buf[...]).astype(BF16)
    for p in range(chunks):
        do_ref[p] = d_att[:, p * LANES:(p + 1) * LANES]
        do_send_ref[p] = d_att[:, cols + p * LANES:cols + (p + 1) * LANES]
    io.send(do_ref, do_out)
    io.send(do_send_ref, do_send_out)
    right = jnp.concatenate([da_ref[:, aligned(other, cols)], da_ref[:, aligned(core, cols)]], axis=1)
    grad = dot_tn(att_ref[...], right).astype(BF16)
    for heads, row0 in ((core, 0), (other, cols)):
        for b in range(cols // height):
            position = 2 * reversed_bits(b, 3) + heads
            for j in range(2 * chunks):
                target = send_ref if j < chunks else keep_ref
                target[position, (j % chunks) * height:(j % chunks + 1) * height, :] = grad[
                    row0 + b * height:row0 + (b + 1) * height, j * LANES:(j + 1) * LANES
                ]
    for target, half in ((send_ref, other), (keep_ref, core)):
        row = jnp.broadcast_to(jnp.where(half == 0, gain_row, gain_row_m[0:1, :]), (16, width))
        for b in range(SUPER):
            turned = pltpu.roll(row, width - b * height, 1) if b else row
            target[xy_first(b), chunks * height:, :] = turned[:, :LANES].astype(BF16)
    io.send(send_ref, send_out)
    io.send(keep_ref, keep_out)
    io.drain()


def ffn_backward(scal, gain_a, gain_row_m, dgate, dup, dmixed2, norm1, root1, att, wo, wg, wu):
    tokens, width = dmixed2.shape
    ff = wg.shape[1]
    chunks = width // 2 // LANES
    packed = ((SUPER, chunks * (width // SUPER) + 16, LANES), BF16)
    split = ((chunks, tokens, LANES), BF16)
    outs = [((tokens, width), F32), split, split, packed, packed]
    return kernel_call(
        ffn_backward_kernel, "ffn_backward", outs,
        [sspec()] + [vspec()] * 8 + [hspec()] * 3,
        [pltpu.VMEM(*z) for z in [
            ((width, width), BF16), ((width, ff), BF16), ((width, ff), BF16),
        ] + outs + [((tokens, width), BF16)]] + [pltpu.SemaphoreType.DMA((11,))],
        2 * tokens * width * (2 * width + 2 * ff), 12_000_000, vmem=26, free=(3, 4),
    )(scal, gain_a, gain_row_m, dgate, dup, dmixed2, norm1, root1, att, wo, wg, wu)


def attention_backward_kernel(
    scal, qa, ka, va, att, do_own, do_oth, x_all, tables, dmixed1, w_all, wo_keep, wo_got,
    own_out, send_out, grad_a, grad_b, first_a, first_b,
    qa_ref, ka_ref, va_ref, att_ref, do_ref, x_ref, t_ref, dst_ref, doa_ref, dz_ref, a_ref, b_ref,
    wo_ref, w_buf, own_ref, send_ref, sems,
):
    core, chip, lead, second = scal[0], scal[1], scal[3], scal[4]
    pairs, _, full, _ = qa_ref.shape
    block = full // 4
    cols = pairs * PAIR
    scale = float(HEAD_DIM) ** (-0.5)
    other, far = 1 - core, 1 - chip
    io = Copies(sems)
    loads = []
    for p in range(pairs):
        copies = []
        for source, t, place in (
            (do_own.at[p], 0, 2 * chip + core),
            (do_own.at[p], 1, 2 * far + core),
            (do_oth.at[p], 0, 2 * chip + other),
            (do_oth.at[p], 1, 2 * far + other),
        ):
            copies.append(
                io.start(source.at[pl.ds(t * block, block), :], do_ref.at[p, aligned(place, block), :])
            )
        for source, target in ((att, att_ref), (ka, ka_ref), (qa, qa_ref), (va, va_ref)):
            copies.append(io.start(source.at[p], target.at[p]))
        if p == 0:
            copies.append(io.start(tables, t_ref))
        loads.append(copies)
        if p == 0:
            late = io.start(x_all, x_ref)
    outputs = [io.start(wo_keep, wo_ref.at[0]), io.start(wo_got, wo_ref.at[1])]
    last = [io.start(dmixed1, own_ref), io.start(w_all, w_buf)]

    lane = lax.broadcasted_iota(jnp.int32, (1, PAIR), 1)
    low = lane < HEAD_DIM
    causal = lax.broadcasted_iota(jnp.int32, (block, block), 0) <= lax.broadcasted_iota(
        jnp.int32, (block, block), 1
    )
    height = x_ref.shape[1] // SUPER

    def back(g, rows):
        return (
            g * t_ref[0, rows, :]
            - pltpu.roll(g, 96, 1) * t_ref[2, rows, :]
            - pltpu.roll(g, 32, 1) * t_ref[1, rows, :]
        ).astype(BF16)

    for p in range(pairs):
        for copy in loads[p]:
            copy.wait()
        grad_do = do_ref[p].astype(F32)
        prod = grad_do * att_ref[p].astype(F32)
        for h in range(2):
            mine = low if h == 0 else jnp.logical_not(low)
            delta = jnp.sum(jnp.where(mine, prod, 0.0), axis=1, keepdims=True)
            doa_ref[h] = beside(lane, h, grad_do, split_three(-delta)).astype(BF16)
        for j in range(4):
            keys = slice(j * block, (j + 1) * block)
            span = slice(j * block, full)
            dk, dv = [], []
            for h in range(2):
                st = dot_nt(ka_ref[p, h, keys, :], qa_ref[p, h, span, :])
                dpt = dot_nt(va_ref[p, h, keys, :], doa_ref[h, span, :])
                pt = jnp.exp(st)
                diag = jnp.where(causal, pt[:, :block], 0.0)
                pt = diag if j == 3 else jnp.concatenate([diag, pt[:, block:]], axis=1)
                dst = (pt * dpt).astype(BF16)
                dst_ref[h, keys, span] = dst
                dv.append(dot_nn(pt.astype(BF16), doa_ref[h, span, :]))
                dk.append(dot_nn(dst, qa_ref[p, h, span, :]))
            dz_ref[p, keys, PAIR:2 * PAIR] = back(jnp.where(low, dk[0], dk[1]), keys)
            dz_ref[p, keys, 2 * PAIR:] = jnp.where(low, dv[0], dv[1]).astype(BF16)
        for i in range(4):
            rows = slice(i * block, (i + 1) * block)
            span = slice(0, (i + 1) * block)
            dq = [dot_tn(dst_ref[h, span, rows], ka_ref[p, h, span, :]) for h in range(2)]
            dz_ref[p, rows, :PAIR] = back(jnp.where(low, dq[0], dq[1]) * scale, rows)
        if p == 0:
            late.wait()
        grad = dot_tn(x_ref[...], dz_ref[p])
        if p < pairs - 1:
            pack(a_ref, grad, xy_first, 0, p * 3 * height, height)
        else:
            for copy in outputs:
                copy.wait()
            above = wo_ref.shape[2]
            b_ref[:, :above, :] = (wo_ref[0].astype(F32) + wo_ref[1].astype(F32)).astype(BF16)
            pack(b_ref, grad, xy_first, 0, above, height)
        if p == pairs - 2:
            io.send(a_ref, grad_a)
            io.send(a_ref.at[aligned(1 - lead, 8)], first_a)
    io.send(b_ref, grad_b)
    for i in range(2):
        io.send(b_ref.at[aligned(2 * i + 1 - second, 4)], first_b.at[4 * i:4 * i + 4])
    for copy in last:
        copy.wait()
    for side, target, out in ((other, send_ref, send_out), (core, own_ref, own_out)):
        left = jnp.concatenate(
            [
                jnp.concatenate(
                    [
                        dz_ref[p, aligned(2 * x + side, block), i * PAIR:(i + 1) * PAIR]
                        for i in range(3)
                        for p in range(pairs)
                    ],
                    axis=1,
                )
                for x in (chip, far)
            ]
        )
        grad = dot_nt(left, w_buf[...])
        if target is own_ref:
            grad += own_ref[...]
        target[...] = grad.astype(target.dtype)
        io.send(target, out)
    io.drain()


def attention_backward(
    scal, qa, ka, va, att, do_own, do_oth, x_all, tables, dmixed1, w_all, wo_keep, wo_got
):
    full, width = x_all.shape
    pairs = qa.shape[0]
    height = 3 * (width // SUPER)
    aug, rows = (qa.shape, BF16), ((pairs, full, PAIR), BF16)
    own, send = (dmixed1.shape, F32), (dmixed1.shape, BF16)
    part_a = ((pairs - 1) * height, LANES)
    part_b = (wo_keep.shape[1] + height, LANES)
    grads = [((SUPER,) + part_a, BF16), ((SUPER,) + part_b, BF16)]
    halves = [((SUPER // 2,) + part_a, BF16), ((SUPER // 2,) + part_b, BF16)]
    return kernel_call(
        attention_backward_kernel, "attention_backward", [own, send] + grads + halves,
        [sspec()] + [hspec()] * 5 + [aspec()] + [hspec()] * 4 + [aspec()] * 2,
        [pltpu.VMEM(*z) for z in [
            aug, aug, aug, rows, rows, ((full, width), BF16), (tables.shape, F32),
            ((2, full, full), BF16), ((2, full, PAIR), BF16), ((pairs, full, 3 * PAIR), BF16),
        ] + grads + [
            ((2,) + wo_keep.shape, BF16), ((width, pairs * 3 * PAIR), BF16), own, send,
        ]] + [pltpu.SemaphoreType.DMA((12 * pairs + 6,))],
        pairs * (10 * full * full * PAIR + 9 * full * width * PAIR), 20_000_000, full * full * 6, vmem=32,
        free=range(2, 6),
        through=[
            (n, (z.shape, z.dtype))
            for n, z in ((1, qa), (2, ka), (3, va), (4, att), (7, x_all), (8, tables), (9, dmixed1), (10, w_all))
        ],
    )(scal, qa, ka, va, att, do_own, do_oth, x_all, tables, dmixed1, w_all, wo_keep, wo_got)[:6]


def assemble_kernel(layout, scal, stay, got, *outs):
    core = scal[0]
    for source, side in ((stay, core), (got, 1 - core)):
        row = 0
        for out, (rows, chunks) in zip(outs, layout):
            for j in range(chunks):
                out[:, aligned(side * chunks + j, LANES)] = source[row:row + rows, :]
                row += rows


def assemble(scal, stay, got, layout):
    return pl.pallas_call(
        functools.partial(assemble_kernel, layout),
        out_shape=tuple(jax.ShapeDtypeStruct((r, 2 * c * LANES), F32) for r, c in layout),
        in_specs=[sspec(), vspec(), vspec()],
        out_specs=(vspec(),) * len(layout),
        compiler_params=pltpu.CompilerParams(vmem_limit_bytes=16 * 1024 * 1024),
        cost_estimate=pl.CostEstimate(flops=0, bytes_accessed=16 * stay.shape[0] * LANES, transcendentals=0),
        name="assemble",
    )(scal, stay, got)


def assemble_pairs_kernel(half, pairs, scal, stay, got, *outs):
    core = scal[0]
    for source, side in ((stay, core), (got, 1 - core)):
        for i, out in enumerate(outs):
            for p in range(pairs):
                if i == 0:
                    chunk = 3 * pairs - 3 + p
                else:
                    chunk = 3 * p + i - 1 + (pairs if p == pairs - 1 else 0)
                out[:, aligned(side * pairs + p, LANES)] = source[chunk * half:(chunk + 1) * half, :]


def assemble_pairs(scal, stay, got, half, pairs):
    return pl.pallas_call(
        functools.partial(assemble_pairs_kernel, half, pairs),
        out_shape=(jax.ShapeDtypeStruct((half, 2 * pairs * LANES), F32),) * 4,
        in_specs=[sspec(), vspec(), vspec()],
        out_specs=(vspec(),) * 4,
        compiler_params=pltpu.CompilerParams(vmem_limit_bytes=16 * 1024 * 1024),
        cost_estimate=pl.CostEstimate(flops=0, bytes_accessed=16 * stay.shape[0] * LANES, transcendentals=0),
        name="assemble_pairs",
    )(scal, stay, got)


class Part:
    def __init__(self, names, leaves):
        self.names = list(names)
        dims = (2,) * len(self.names)
        self.leaves = [leaf.reshape(dims + leaf.shape[-2:]) for leaf in leaves]

    def take(self, index):
        return [lax.dynamic_index_in_dim(leaf, index, 0, keepdims=False) for leaf in self.leaves]

    def outgoing(self, me):
        return sum(leaf.astype(F32) for leaf in self.take(1 - me)).astype(BF16)

    def incoming(self, me, got):
        self.names = self.names[1:]
        dims = (2,) * len(self.names)
        stay = self.take(me)
        if len(self.names) < 3:
            stay = [lax.optimization_barrier(sum(leaf.astype(F32) for leaf in stay))]
        self.leaves = stay + [got.reshape(dims + (-1, got.shape[-1]))]

    def result(self):
        return sum(leaf.astype(F32) for leaf in self.leaves)


def swap_seq(value, bit):
    return lax.ppermute(value, "seq", [(i, i ^ bit) for i in range(4)])


def after(value, *others):
    return lax.optimization_barrier((value,) + others)[0]


def on_device(
    batch_size,
    hidden_in,
    cotangent,
    lengths,
    w_query,
    w_key,
    w_value,
    w_output,
    w_gate,
    w_up,
    w_down,
    gain_attn,
    gain_mlp,
):
    seqs, block, width = hidden_in.shape
    tokens = seqs * block
    cols = width // 2
    pairs = cols // PAIR
    height = width // SUPER
    rank = lax.axis_index("seq")
    batch = lax.axis_index("batch")
    chip, core = rank // 2, rank % 2
    far, other = 1 - chip, 1 - core

    def pick(z, index):
        return lax.dynamic_index_in_dim(z, index, 0, keepdims=False)

    def home(kept, back):
        first = chip == 0
        return jnp.stack([jnp.where(first, kept, back), jnp.where(first, back, kept)])

    kept = pick(hidden_in, chip)
    recv = swap_seq(pick(hidden_in, far), 2)
    kept_o = swap_seq(kept, 1)
    recv_o = swap_seq(recv, 1)
    ct_kept = pick(cotangent, chip)
    ct_recv = swap_seq(after(pick(cotangent, far), recv), 2)
    tables = rope_tables(4 * block)
    gain_a, gain_m = gain_attn[None, :], gain_mlp[None, :]

    bits = batch_size.bit_length() - 1
    names = ["b%d" % i for i in reversed(range(bits))] + ["x"]
    top, rest = names[:4][::-1], names[4:]

    def index_of(name):
        return chip if name == "x" else (batch >> int(name[1:])) & 1

    scal = jnp.stack(
        [core, chip, pick(lengths, chip), index_of(top[0]), index_of(top[1])]
    ).astype(jnp.int32)

    def exchange(value, name):
        if name == "x":
            return swap_seq(value, 2)
        bit = 1 << int(name[1:])
        return lax.ppermute(value, "batch", [(i, i ^ bit) for i in range(batch_size)])

    class Sum:
        def __init__(self, *parts):
            self.parts = list(parts)

        def out(self, ready=None):
            me = index_of(self.parts[0].names[0])
            sends = [part.outgoing(me) for part in self.parts] if ready is None else [ready]
            self.sent = sends[0] if len(sends) == 1 else jnp.concatenate(sends, axis=-2)
            return self.sent

        def move(self):
            self.got = exchange(self.sent, self.parts[0].names[0])

        def land(self):
            me, row = index_of(self.parts[0].names[0]), 0
            for part in self.parts:
                rows = part.leaves[0].shape[-2]
                part.incoming(me, lax.slice_in_dim(self.got, row, row + rows, axis=self.got.ndim - 2))
                row += rows

        def hop(self):
            self.out()
            self.move()
            self.land()

    def swapped(part):
        part.names = [part.names[1], part.names[0]] + part.names[2:]
        part.leaves = [leaf.swapaxes(0, 1) for leaf in part.leaves]
        return part

    q, k, v, att, att_oth, x_all, w_all, tables = attention_forward(
        scal, kept, recv, kept_o, recv_o, w_query, w_key, w_value, tables
    )
    got = swap_seq(att_oth, 1)
    (
        attended, norm1, root1, dmixed2, gain_row_m, dgate, dup,
        lay_kept, lay_away, down_keep, down_send, gate_keep, gate_send, up_keep, up_send,
    ) = ffn_forward(
        scal, gain_a, gain_m, kept, recv, att, got, ct_kept, ct_recv, w_output, w_gate, w_up, w_down
    )
    first = [swap_seq(z, 1) for z in (gate_send, up_send, down_send)]
    lay_back = swap_seq(lay_away, 2)
    dmixed1, do_own, do_send, wo_send, wo_keep = ffn_backward(
        scal, gain_a, gain_row_m, dgate, dup, dmixed2, norm1, root1, attended, w_output, w_gate, w_up
    )

    do_send, wo_send, lay_back, *first = lax.optimization_barrier(
        (do_send, wo_send, lay_back, *first)
    )
    do_oth, wo_got = swap_seq(do_send, 1), swap_seq(wo_send, 1)
    yz_names = [top[1], top[2], top[0], top[3]]
    xz_names = [top[0], top[2], top[1], top[3]]
    zy_names = [top[2], top[1], top[0], top[3]]
    gates = Sum(Part(xz_names, [gate_keep, first[0]]))
    ups = Sum(Part(yz_names, [up_keep, first[1]]))
    downs = Sum(Part(zy_names, [down_keep, first[2]]))
    sent = [z.out() for z in (gates, ups, downs)]
    scal_d = after(scal, *sent)
    for z in (gates, ups, downs):
        z.move()
    own_in, send_in, grads_a, grads_b, first_a, first_b = attention_backward(
        scal_d, q, k, v, att, do_own, do_oth, x_all, tables, dmixed1, w_all,
        wo_keep, wo_got,
    )

    send_in, first_a, first_b, gates.got, ups.got, downs.got = lax.optimization_barrier(
        (send_in, first_a, first_b, gates.got, ups.got, downs.got)
    )
    got_in = swap_seq(send_in, 1)
    alpha = Sum(Part(top, [grads_a]))
    beta = Sum(swapped(Part(top, [grads_b])))
    alpha.out(first_a)
    beta.out(first_b)
    alpha.move()
    beta.move()
    for z in (ups, downs, gates):
        z.land()
        z.out()
        z.move()
    g_in = (own_in + got_in.astype(F32)).astype(BF16)
    g_back = swap_seq(g_in[block:], 2)

    alpha.land()
    beta.land()
    alpha.out()
    beta.out()
    alpha.move()
    beta.move()
    gates.got = after(gates.got, alpha.sent)
    ups.got = after(ups.got, alpha.sent)
    downs.got = after(downs.got, beta.sent)
    for z in (gates, ups, downs):
        z.land()
        z.out()
        z.move()
    alpha.land()
    beta.land()
    others = Sum(*alpha.parts, *beta.parts)
    others.out()
    others.move()
    for z in (gates, ups, downs):
        z.got = after(z.got, others.sent)
        z.land()
    feeds = Sum(*gates.parts, *ups.parts, *downs.parts)
    feeds.out()
    feeds.move()
    others.land()
    others.out()
    others.move()
    feeds.got = after(feeds.got, others.sent)
    others.land()
    feeds.land()
    lay_kept = after(lay_kept, feeds.sent)

    high = w_gate.shape[1] // SUPER
    wide = w_gate.shape[1] // 2 // LANES
    gate_sum, up_sum, down_sum = [z.result() for z in feeds.parts]
    alpha_sum, beta_sum = [z.result() for z in others.parts]
    above = pairs * height
    gain_rows = beta_sum[above:above + 16]
    feed = [(high, pairs)] + [(height, wide)] * 2
    feed_sums = [down_sum, gate_sum, up_sum]
    rest_layout = [(height, 1)] * (3 * pairs - 3) + [(height, pairs)] + [(height, 1)] * 3
    rest_sums = [alpha_sum, beta_sum[:above], beta_sum[above + 16:]]
    grad_in_of = lambda: home(g_in[:block], g_back)
    if rest:
        return finish_general(
            feed, feed_sums, rest_layout, rest_sums, gain_rows, rest, index_of, exchange, core, pairs,
            home(lay_kept, lay_back), grad_in_of(),
        )

    def sides(totals, layout):
        total, row, pieces = jnp.concatenate(totals), 0, []
        for rows, chunks in layout:
            pieces.append(total[row:row + rows * chunks].reshape(chunks, 2, rows // 2, LANES))
            row += rows * chunks
        return [
            jnp.concatenate(
                [lax.dynamic_index_in_dim(z, i, 1, keepdims=False).reshape(-1, LANES) for z in pieces]
            )
            for i in (other, core)
        ]

    away, stay = sides(feed_sums, feed)
    g_down, g_gate, g_up = assemble(
        scal, stay, swap_seq(away, 1), [(rows // 2, chunks) for rows, chunks in feed]
    )
    half = height // 2
    away, stay = sides(rest_sums, rest_layout)
    last = swap_seq(jnp.concatenate([away, gain_rows[:8]]), 1)
    g_output, g_query, g_key, g_value = assemble_pairs(scal, stay, last, half, pairs)
    gains = jnp.where(core == 0, jnp.stack([gain_rows[0], last[-8]]), jnp.stack([last[-8], gain_rows[0]]))
    gains = lax.dynamic_slice_in_dim(gains, core * half, half, axis=1)
    layer_out = home(lay_kept, lay_back)
    return (
        layer_out, grad_in_of(), g_query, g_key, g_value, g_output, g_gate, g_up, g_down,
        gains[0], gains[1],
    )


def finish_general(
    feed, feed_sums, rest_layout, rest_sums, gain_rows, rest, index_of, exchange, core, pairs,
    layer_out, grad_in,
):
    def finish(packed, rows, chunks):
        matrix = packed.reshape(chunks, rows, LANES).transpose(1, 0, 2).reshape(rows, chunks * LANES)
        for name in rest:
            matrix = matrix.reshape(2, matrix.shape[0] // 2, matrix.shape[1])
            me = index_of(name)
            away = lax.dynamic_index_in_dim(matrix, 1 - me, 0, keepdims=False)
            stay = lax.dynamic_index_in_dim(matrix, me, 0, keepdims=False)
            matrix = stay + exchange(away.astype(BF16), name).astype(F32)
        matrix = matrix.reshape(2, matrix.shape[0] // 2, matrix.shape[1])
        stay = lax.dynamic_index_in_dim(matrix, core, 0, keepdims=False)
        got = swap_seq(lax.dynamic_index_in_dim(matrix, 1 - core, 0, keepdims=False), 1)
        return jnp.where(
            core == 0,
            jnp.concatenate([stay, got], axis=-1),
            jnp.concatenate([got, stay], axis=-1),
        )

    def matrices(total, layout):
        row, out = 0, []
        for rows, chunks in layout:
            out.append((total[row:row + rows * chunks], rows, chunks))
            row += rows * chunks
        return out

    down, gate, up = matrices(jnp.concatenate(feed_sums), feed)
    qkv = matrices(jnp.concatenate(rest_sums), rest_layout)
    output = qkv.pop(3 * pairs - 3)
    height = output[1]
    by_matrix = [
        (jnp.concatenate([qkv[3 * p + i][0] for p in range(pairs)]), height, pairs) for i in range(3)
    ]
    gains = jnp.broadcast_to(gain_rows[0, :height, None], (height, LANES))
    outs = [finish(*z) for z in by_matrix + [output, gate, up, down, (gains, height, 1)]]
    gains = outs.pop()
    return (layer_out, grad_in, *outs, gains[:, 0], gains[:, LANES])


def solution(mesh):
    tokens = P("batch", "seq", None)
    rows = P(("batch", "seq"), None)
    return jax.shard_map(
        functools.partial(on_device, mesh.shape["batch"]),
        mesh=mesh,
        in_specs=(tokens, tokens, P("batch")) + (P(),) * 9,
        out_specs=(tokens, tokens) + (rows,) * 7 + (P(("batch", "seq")),) * 2,
        check_vma=False,
    )
```

```python
import functools

import jax
import jax.numpy as jnp
import numpy as np
from jax import lax
from jax.experimental import pallas as pl
from jax.experimental.pallas import tpu as pltpu
from jax.sharding import PartitionSpec as P

HEADS = 12
HEAD_DIM = 64
PAIR = 2 * HEAD_DIM

EPS = 1e-06
NEG = -1e30
LANES = 128
SUPER = 16

F32 = jnp.float32
BF16 = jnp.bfloat16


def dot_nn(left, right):
    return lax.dot_general(left, right, (((1,), (0,)), ((), ())), preferred_element_type=F32)


def dot_nt(left, right):
    return lax.dot_general(left, right, (((1,), (1,)), ((), ())), preferred_element_type=F32)


def dot_tn(left, right):
    return lax.dot_general(left, right, (((0,), (0,)), ((), ())), preferred_element_type=F32)


def rope_tables(count):
    half = HEAD_DIM // 2
    inverse = 10000.0 ** (-(np.arange(half, dtype=np.float32) * np.float32(2.0)) / HEAD_DIM)
    angles = np.arange(count, dtype=np.float32)[:, None] * inverse.astype(np.float32)[None, :]
    cosine, sine = np.cos(angles), np.sin(angles)
    zero = np.zeros_like(sine)
    tables = (
        np.concatenate([cosine] * 4, axis=-1),
        np.concatenate([zero, sine] * 2, axis=-1),
        np.concatenate([-sine, zero] * 2, axis=-1),
    )
    return jnp.asarray(np.stack(tables), F32)


def start(source, target, sem):
    copy = pltpu.make_async_copy(source, target, sem)
    copy.start()
    return copy


def aligned(index, size):
    return pl.ds(pl.multiple_of(index * size, size), size)


def vspec():
    return pl.BlockSpec(memory_space=pltpu.VMEM)


def hspec():
    return pl.BlockSpec(memory_space=pltpu.HBM)


def aspec():
    return pl.BlockSpec(memory_space=pl.ANY)


def sspec():
    return pl.BlockSpec(memory_space=pltpu.SMEM)


def mean_row(z):
    return jnp.sum(z, axis=1, keepdims=True) * (1.0 / z.shape[1])


def reversed_bits(index, bits):
    out = 0
    for i in range(bits):
        out |= ((index >> i) & 1) << (bits - 1 - i)
    return out


def xy_first(b):
    return reversed_bits(b, 4)


def xz_first(b):
    zh, zl, y, x = (b >> 3) & 1, (b >> 2) & 1, (b >> 1) & 1, b & 1
    return x * 8 + zl * 4 + y * 2 + zh


def yz_first(b):
    zh, zl, y, x = (b >> 3) & 1, (b >> 2) & 1, (b >> 1) & 1, b & 1
    return y * 8 + zl * 4 + x * 2 + zh


def zy_first(b):
    zh, zl, y, x = (b >> 3) & 1, (b >> 2) & 1, (b >> 1) & 1, b & 1
    return zl * 8 + y * 4 + x * 2 + zh


def pack(out_ref, value, place, block0, row0, height):
    low = value.astype(BF16)
    for b in range(value.shape[0] // height):
        for j in range(value.shape[1] // LANES):
            out_ref[place(block0 + b), row0 + j * height:row0 + (j + 1) * height, :] = low[
                b * height:(b + 1) * height, j * LANES:(j + 1) * LANES
            ]


def kernel_call(
    kernel, name, outs, specs, scratch, flops, moved, exps=0, resident=(), vmem=16, free=(), through=(),
    updated=None,
):
    count = len(resident) + len(outs)
    through = tuple(through)
    if through:
        inner = kernel

        def kernel(*refs):
            at = len(specs) + count
            inner(*refs[:at], *refs[at + len(through):])

    return pl.pallas_call(
        kernel,
        out_shape=tuple(pltpu.VMEM(*z) for z in resident)
        + tuple(
            jax.ShapeDtypeStruct(*z) if i in free else pltpu.HBM(*z) for i, z in enumerate(outs)
        )
        + tuple(pltpu.HBM(*z) for _, z in through),
        in_specs=specs,
        out_specs=(vspec(),) * len(resident)
        + tuple(aspec() if i in free else hspec() for i in range(len(outs)))
        + (hspec(),) * len(through),
        input_output_aliases={n: count + i for i, (n, _) in enumerate(through)} | (updated or {}),
        scratch_shapes=scratch,
        compiler_params=pltpu.CompilerParams(vmem_limit_bytes=vmem * 1024 * 1024),
        cost_estimate=pl.CostEstimate(flops=flops, bytes_accessed=moved, transcendentals=exps),
        name=name,
    )


class Copies:
    def __init__(self, sems):
        self.sems, self.used, self.open = sems, 0, []

    def start(self, source, target):
        copy = start(source, target, self.sems.at[self.used])
        self.used += 1
        return copy

    def send(self, source, target):
        self.open.append(self.start(source, target))

    def drain(self):
        for copy in self.open:
            copy.wait()


def split_three(value):
    first = value.astype(BF16).astype(F32)
    rest = value - first
    second = rest.astype(BF16).astype(F32)
    return first, second, (rest - second).astype(BF16).astype(F32)


def beside(lane, head, mine, pieces):
    own = (lane < HEAD_DIM) if head == 0 else (lane >= HEAD_DIM)
    first = (1 - head) * HEAD_DIM
    out = jnp.zeros_like(mine)
    for i, piece in enumerate(pieces):
        out = jnp.where(lane == first + i, piece, out)
    return jnp.where(own, mine, out)


def project(x_ref, w_buf, t_ref, q_ref, k_ref, v_ref, places, length):
    pairs = q_ref.shape[0]
    block = x_ref.shape[0] // 2
    scale = float(HEAD_DIM) ** (-0.5)
    lane = lax.broadcasted_iota(jnp.int32, (1, PAIR), 1)
    z_all = dot_nn(x_ref[...], w_buf[...])
    for t, place in enumerate(places):
        z = z_all[t * block:(t + 1) * block]
        rows = aligned(place, block)
        c, a, b = t_ref[0, rows, :], t_ref[1, rows, :], t_ref[2, rows, :]
        slot = place * block + lax.broadcasted_iota(jnp.int32, (block, PAIR), 0)
        bias = jnp.where(slot < length, 0.0, NEG)
        for p in range(3 * pairs):
            part = z[:, p * PAIR:(p + 1) * PAIR]
            if p < 2 * pairs:
                part = part * c + pltpu.roll(part, 32, 1) * a + pltpu.roll(part, 96, 1) * b
            for h in range(2):
                if p < pairs:
                    mine = part.astype(BF16).astype(F32) * scale
                    q_ref[p, h, rows, :] = beside(lane, h, mine, (0.0, 0.0, 0.0, 1.0)).astype(BF16)
                elif p < 2 * pairs:
                    k_ref[p - pairs, h, rows, :] = beside(
                        lane, h, part, (1.0, 1.0, 1.0, bias)
                    ).astype(BF16)
                else:
                    own = (lane < HEAD_DIM) if h == 0 else (lane >= HEAD_DIM)
                    v_ref[p - 2 * pairs, h, rows, :] = jnp.where(own, part, 1.0).astype(BF16)


def project_kept_kernel(
    scal, kept, kept_o, wq, wk, wv, tables, w_buf, t_ref, q_ref, k_ref, v_ref, w_out, t_out, x_ref, sems
):
    core, chip, length = scal[0], scal[1], scal[2]
    block = kept.shape[0]
    cols = wq.shape[1] // 2
    io = Copies(sems)
    columns = pl.ds(pl.multiple_of(core * cols, PAIR), cols)
    needed = [
        io.start(w.at[:, columns], w_buf.at[:, i * cols:(i + 1) * cols])
        for i, w in enumerate((wq, wk, wv))
    ]
    needed.append(io.start(kept, x_ref.at[0:block, :]))
    needed.append(io.start(kept_o, x_ref.at[block:, :]))
    needed.append(io.start(tables, t_ref))
    for copy in needed:
        copy.wait()
    io.send(w_buf, w_out)
    io.send(t_ref, t_out)
    places = (2 * chip + core, 2 * chip + 1 - core)
    project(x_ref, w_buf, t_ref, q_ref, k_ref, v_ref, places, length)
    io.drain()


def project_kept(scal, kept, kept_o, wq, wk, wv, tables):
    block, width = kept.shape
    cols = width // 2
    aug = ((cols // PAIR, 2, 4 * block, PAIR), BF16)
    weights, turns = ((width, 3 * cols), BF16), (tables.shape, F32)
    return kernel_call(
        project_kept_kernel, "project_kept", [weights, turns],
        [sspec()] + [aspec()] * 2 + [hspec()] * 4,
        [pltpu.VMEM((2 * block, width), BF16), pltpu.SemaphoreType.DMA((8,))],
        4 * block * width * 3 * cols, 8_000_000, vmem=40, resident=[weights, turns, aug, aug, aug],
    )(scal, kept, kept_o, wq, wk, wv, tables)


def attention_forward_kernel(
    scal, kept, recv, kept_o, recv_o, w_buf, t_ref, q_in, k_in, v_in,
    q_ref, k_ref, v_ref,
    q_out, k_out, v_out, att_out, oth_out, x_out,
    x_ref, x_new, att_ref, sems,
):
    del q_in, k_in, v_in
    core, chip, length = scal[0], scal[1], scal[2]
    block = kept.shape[0]
    pairs = q_ref.shape[0]
    other, far = 1 - core, 1 - chip
    io = Copies(sems)
    needed = [io.start(recv, x_new.at[0:block, :]), io.start(recv_o, x_new.at[block:, :])]
    blocks = [
        io.start(source, x_ref.at[aligned(place, block), :])
        for source, place in (
            (kept, 2 * chip + core),
            (recv, 2 * far + core),
            (kept_o, 2 * chip + other),
            (recv_o, 2 * far + other),
        )
    ]
    for copy in needed:
        copy.wait()
    project(x_new, w_buf, t_ref, q_ref, k_ref, v_ref, (2 * far + core, 2 * far + other), length)
    for copy in blocks:
        copy.wait()
    for source, out in ((x_ref, x_out), (k_ref, k_out), (v_ref, v_out)):
        io.send(source, out)

    lane = lax.broadcasted_iota(jnp.int32, (1, PAIR), 1)
    low = lane < HEAD_DIM
    causal = lax.broadcasted_iota(jnp.int32, (block, block), 1) <= lax.broadcasted_iota(
        jnp.int32, (block, block), 0
    )

    def scores(p, h, i):
        span = (i + 1) * block
        s = dot_nt(q_ref[p, h, i * block:span, :], k_ref[p, h, :span, :])
        diag = jnp.where(causal, s[:, i * block:], NEG)
        return jnp.concatenate([s[:, :i * block], diag], axis=1) if i else diag

    outs, tops = {}, {}

    def attend(unit, e):
        p, h, i = unit
        outs[unit] = dot_nn(e, v_ref[p, h, :(i + 1) * block, :])

    def finish(p):
        for i in range(4):
            rows = slice(i * block, (i + 1) * block)
            first, second = outs[p, 0, i], outs[p, 1, i]
            sums = pltpu.roll(jnp.where(low, second, first), HEAD_DIM, 1)
            att_ref[p, rows, :] = (jnp.where(low, first, second) / sums).astype(BF16)
            for h in range(2):
                lse = tops[p, h, i] + jnp.log(outs[p, h, i])
                mine = q_ref[p, h, rows, :].astype(F32)
                for n, piece in enumerate(split_three(-lse)):
                    mine = jnp.where(lane == (1 - h) * HEAD_DIM + n, piece, mine)
                q_ref[p, h, rows, :] = mine.astype(BF16)
        io.send(q_ref.at[p], q_out.at[p])
        io.send(att_ref.at[p], att_out.at[p])
        for t in range(2):
            place = 2 * (chip if t == 0 else far) + other
            io.send(
                att_ref.at[p, aligned(place, block), :], oth_out.at[p, t * block:(t + 1) * block, :]
            )

    units = [(p, h, i) for p in range(pairs) for h in range(2) for i in (3, 2, 1, 0)]
    ahead, behind = scores(*units[0]), None
    for n, unit in enumerate(units):
        s = ahead
        ahead = scores(*units[n + 1]) if n + 1 < len(units) else None
        if behind is not None:
            attend(*behind)
        if n and n % 8 == 0:
            finish(unit[0] - 1)
        top = jnp.max(s, axis=1, keepdims=True)
        tops[unit] = top
        behind = (unit, jnp.exp(s - top).astype(BF16))
    attend(*behind)
    finish(pairs - 1)
    io.drain()


def attention_forward(scal, kept, recv, kept_o, recv_o, w_all, turns, q, k, v):
    block, width = kept.shape
    full = 4 * block
    pairs = q.shape[0]
    aug = (q.shape, BF16)
    return kernel_call(
        attention_forward_kernel, "attention_forward",
        [aug, aug, aug, ((pairs, full, PAIR), BF16), ((pairs, full // 2, PAIR), BF16),
         ((full, width), BF16)],
        [sspec()] + [aspec()] * 4 + [vspec()] * 5,
        [
            pltpu.VMEM((full, width), BF16),
            pltpu.VMEM((full // 2, width), BF16),
            pltpu.VMEM((pairs, full, PAIR), BF16),
            pltpu.SemaphoreType.DMA((9 + 4 * pairs,)),
        ],
        full * width * width * 3 // 2 + 4 * full * full * pairs * PAIR, 14_000_000, full * full * 6,
        resident=[aug, aug, aug], vmem=44, updated={7: 0, 8: 1, 9: 2},
    )(scal, kept, recv, kept_o, recv_o, w_all, turns, q, k, v)[3:]


def load_attended(io, target, att, got, places, block):
    pairs = att.shape[0]
    copies = []
    for p in range(pairs):
        for t in range(2):
            copies.append(
                io.start(
                    att.at[p, aligned(places[t], block), :],
                    target.at[t * block:(t + 1) * block, p * PAIR:(p + 1) * PAIR],
                )
            )
        copies.append(io.start(got.at[p], target.at[:, (pairs + p) * PAIR:(pairs + p + 1) * PAIR]))
    return copies


def load_output_weight(io, target, wo, core, cols):
    return [
        io.start(wo.at[aligned(core, cols), :], target.at[0:cols, :]),
        io.start(wo.at[aligned(1 - core, cols), :], target.at[cols:, :]),
    ]


def ffn_forward_kernel(
    scal, gain_a, gain_m, kept, recv, att, got, ct_kept, ct_recv, wo, wg, wu, wd,
    att_ref, norm1_ref, root1_ref, dmixed2_ref, gain_row_ref, dgate_ref, dup_ref,
    lay_kept, lay_away, down_keep, down_send, gate_keep, gate_send, up_keep, up_send,
    wo_buf, wg_buf, wu_buf, wd_buf, x_ref, ct_ref, lay_ref, x1_low_ref, dm_ref, gate_ref, up_ref,
    hid_ref, dk_ref, ds_ref, gk_ref, gs_ref, uk_ref, us_ref, sems,
):
    core, chip, length = scal[0], scal[1], scal[2]
    block, width = kept.shape
    cols = width // 2
    ff = wg.shape[1]
    step = ff // 4
    other, far = 1 - core, 1 - chip
    places = (2 * chip + core, 2 * far + core)
    io = Copies(sems)
    first = load_attended(io, att_ref, att, got, places, block)
    first += load_output_weight(io, wo_buf, wo, core, cols)
    first.append(io.start(kept, x_ref.at[0:block, :]))
    first.append(io.start(recv, x_ref.at[block:, :]))
    weights = []
    for f in range(4):
        part = slice(f * step, (f + 1) * step)
        weights.append(io.start(wg.at[:, part], wg_buf.at[:, part]))
        weights.append(io.start(wu.at[:, part], wu_buf.at[:, part]))
    down = io.start(wd, wd_buf)
    late = [io.start(ct_kept, ct_ref.at[0:block, :]), io.start(ct_recv, ct_ref.at[block:, :])]
    for copy in first:
        copy.wait()
    mixed = x_ref[...].astype(F32) + dot_nn(att_ref[...], wo_buf[...])
    root = lax.rsqrt(mean_row(mixed * mixed) + EPS)
    norm = mixed * root
    norm1_ref[...] = norm
    root1_ref[...] = jnp.broadcast_to(root, root1_ref.shape)
    x1_low_ref[...] = (norm * gain_a[...]).astype(BF16)
    for f in range(4):
        part = slice(f * step, (f + 1) * step)
        weights[2 * f].wait()
        weights[2 * f + 1].wait()
        gate = dot_nn(x1_low_ref[...], wg_buf[:, part])
        up = dot_nn(x1_low_ref[...], wu_buf[:, part])
        hid_ref[:, part] = (gate * jax.nn.sigmoid(gate) * up).astype(BF16)
        gate_ref[:, part] = gate.astype(BF16)
        up_ref[:, part] = up.astype(BF16)
    down.wait()
    mixed = norm1_ref[...] * gain_a[...] + dot_nn(hid_ref[...], wd_buf[...])
    root = lax.rsqrt(mean_row(mixed * mixed) + EPS)
    norm = mixed * root
    slot = lax.broadcasted_iota(jnp.int32, (2 * block, 1), 0)
    slot = jnp.where(slot < block, places[0] * block + slot, (places[1] - 1) * block + slot)
    valid = (slot < length).astype(F32)
    lay_ref[...] = (valid * (norm * gain_m[...])).astype(BF16)
    io.send(lay_ref.at[0:block, :], lay_kept)
    io.send(lay_ref.at[block:, :], lay_away)
    for copy in late:
        copy.wait()
    d_out = valid * ct_ref[...].astype(F32)
    gain_row = jnp.sum(d_out * norm, axis=0, keepdims=True)
    gain_row_ref[...] = jnp.broadcast_to(gain_row, gain_row_ref.shape)
    d_norm = d_out * gain_m[...]
    d_mixed = root * (d_norm - norm * mean_row(d_norm * norm))
    dmixed2_ref[...] = d_mixed
    dm_ref[...] = d_mixed.astype(BF16)
    right = jnp.concatenate([dm_ref[:, aligned(other, cols)], dm_ref[:, aligned(core, cols)]], axis=1)
    height = ff // SUPER
    for f in range(4):
        grad = dot_tn(hid_ref[:, f * step:(f + 1) * step], right)
        pack(ds_ref, grad[:, :cols], zy_first, f * step // height, 0, height)
        pack(dk_ref, grad[:, cols:], zy_first, f * step // height, 0, height)
    io.send(ds_ref, down_send)
    io.send(dk_ref, down_keep)
    height = width // SUPER
    rows = step // LANES * height
    for gate_part, gate_out, up_part, up_out, side in (
        (gs_ref, gate_send, us_ref, up_send, other), (gk_ref, gate_keep, uk_ref, up_keep, core),
    ):
        for sub in range(2):
            part = aligned(side * 2 + sub, step)
            d_hid = dot_nt(dm_ref[...], wd_buf[part, :])
            g = gate_ref[:, part].astype(F32)
            sigma = jax.nn.sigmoid(g)
            d_up = (d_hid * (g * sigma)).astype(BF16)
            d_gate = (
                d_hid * up_ref[:, part].astype(F32) * sigma * (1.0 + g * (1.0 - sigma))
            ).astype(BF16)
            dgate_ref[:, part] = d_gate
            dup_ref[:, part] = d_up
            pack(gate_part, dot_tn(x1_low_ref[...], d_gate), xz_first, 0, sub * rows, height)
            pack(up_part, dot_tn(x1_low_ref[...], d_up), yz_first, 0, sub * rows, height)
            at = slice(sub * rows, (sub + 1) * rows)
            io.send(gate_part.at[:, at, :], gate_out.at[:, at, :])
            io.send(up_part.at[:, at, :], up_out.at[:, at, :])
    io.drain()


def ffn_forward(scal, gain_a, gain_m, kept, recv, att, got, ct_kept, ct_recv, wo, wg, wu, wd):
    block, width = kept.shape
    ff = wg.shape[1]
    tokens, cols = 2 * block, width // 2
    half = ((block, width), BF16)
    down = ((SUPER, ff // SUPER * (cols // LANES), LANES), BF16)
    wide = ((SUPER, width // SUPER * (ff // 2 // LANES), LANES), BF16)
    rows16, rows32 = ((tokens, width), BF16), ((tokens, width), F32)
    hidden = ((tokens, ff), BF16)
    return kernel_call(
        ffn_forward_kernel, "ffn_forward", [half, half, down, down, wide, wide, wide, wide],
        [sspec(), vspec(), vspec()] + [aspec()] * 2 + [hspec()] + [aspec()] * 3 + [hspec()] * 4,
        [pltpu.VMEM(*z) for z in [
            ((width, width), BF16), ((width, ff), BF16), ((width, ff), BF16), ((ff, width), BF16),
            rows16, rows16, rows16, rows16, rows16, hidden, hidden, hidden,
            down, down, wide, wide, wide, wide,
        ]] + [pltpu.SemaphoreType.DMA((27 + 3 * (cols // PAIR),))],
        2 * tokens * width * (width + 7 * ff), 26_000_000, 2 * tokens * ff, vmem=44,
        resident=[rows16, rows32, ((tokens, LANES), F32), rows32, ((8, width), F32), hidden, hidden],
    )(scal, gain_a, gain_m, kept, recv, att, got, ct_kept, ct_recv, wo, wg, wu, wd)


def ffn_backward_kernel(
    scal, gain_a, gain_row_m, dgate_ref, dup_ref, dmixed2_ref, norm1_ref, root1_ref, att_ref,
    wo, wg, wu,
    dmixed1_out, do_out, do_send_out, send_out, keep_out,
    wo_buf, wg_buf, wu_buf, dmixed1_ref, do_ref, do_send_ref, send_ref, keep_ref, da_ref, sems,
):
    core = scal[0]
    tokens, width = dmixed2_ref.shape
    cols = width // 2
    height = width // SUPER
    chunks = cols // LANES
    other = 1 - core
    ff = wg.shape[1]
    io = Copies(sems)
    weights = []
    for f in range(2):
        part = slice(f * ff // 2, (f + 1) * ff // 2)
        for weight, buffer in ((wg, wg_buf), (wu, wu_buf)):
            weights.append(io.start(weight.at[:, part], buffer.at[:, part]))
    last = load_output_weight(io, wo_buf, wo, core, cols)
    d_x1 = dmixed2_ref[...]
    for f in range(2):
        part = slice(f * ff // 2, (f + 1) * ff // 2)
        for n, (left, right) in enumerate(((dgate_ref, wg_buf), (dup_ref, wu_buf))):
            weights[2 * f + n].wait()
            d_x1 += dot_nt(left[:, part], right[:, part])
    norm = norm1_ref[...]
    gain_row = jnp.sum(d_x1 * norm, axis=0, keepdims=True)
    d_norm = d_x1 * gain_a[...]
    d_mixed = root1_ref[:, 0:1] * (d_norm - norm * mean_row(d_norm * norm))
    dmixed1_ref[...] = d_mixed
    da_ref[...] = d_mixed.astype(BF16)
    io.send(dmixed1_ref, dmixed1_out)
    for copy in last:
        copy.wait()
    d_att = dot_nt(da_ref[...], wo_buf[...]).astype(BF16)
    for p in range(chunks):
        do_ref[p] = d_att[:, p * LANES:(p + 1) * LANES]
        do_send_ref[p] = d_att[:, cols + p * LANES:cols + (p + 1) * LANES]
    io.send(do_ref, do_out)
    io.send(do_send_ref, do_send_out)
    right = jnp.concatenate([da_ref[:, aligned(other, cols)], da_ref[:, aligned(core, cols)]], axis=1)
    grad = dot_tn(att_ref[...], right).astype(BF16)
    for heads, row0 in ((core, 0), (other, cols)):
        for b in range(cols // height):
            position = 2 * reversed_bits(b, 3) + heads
            for j in range(2 * chunks):
                target = send_ref if j < chunks else keep_ref
                target[position, (j % chunks) * height:(j % chunks + 1) * height, :] = grad[
                    row0 + b * height:row0 + (b + 1) * height, j * LANES:(j + 1) * LANES
                ]
    for target, half in ((send_ref, other), (keep_ref, core)):
        row = jnp.broadcast_to(jnp.where(half == 0, gain_row, gain_row_m[0:1, :]), (16, width))
        for b in range(SUPER):
            turned = pltpu.roll(row, width - b * height, 1) if b else row
            target[xy_first(b), chunks * height:, :] = turned[:, :LANES].astype(BF16)
    io.send(send_ref, send_out)
    io.send(keep_ref, keep_out)
    io.drain()


def ffn_backward(scal, gain_a, gain_row_m, dgate, dup, dmixed2, norm1, root1, att, wo, wg, wu):
    tokens, width = dmixed2.shape
    ff = wg.shape[1]
    chunks = width // 2 // LANES
    packed = ((SUPER, chunks * (width // SUPER) + 16, LANES), BF16)
    split = ((chunks, tokens, LANES), BF16)
    outs = [((tokens, width), F32), split, split, packed, packed]
    return kernel_call(
        ffn_backward_kernel, "ffn_backward", outs,
        [sspec()] + [vspec()] * 8 + [hspec()] * 3,
        [pltpu.VMEM(*z) for z in [
            ((width, width), BF16), ((width, ff), BF16), ((width, ff), BF16),
        ] + outs + [((tokens, width), BF16)]] + [pltpu.SemaphoreType.DMA((11,))],
        2 * tokens * width * (2 * width + 2 * ff), 12_000_000, vmem=26,
    )(scal, gain_a, gain_row_m, dgate, dup, dmixed2, norm1, root1, att, wo, wg, wu)


def attention_backward_kernel(
    scal, qa, ka, va, att, do_own, do_oth, x_all, tables, dmixed1, w_all, wo_keep, wo_got,
    own_out, send_out, grad_a, grad_b, first_a, first_b,
    qa_ref, ka_ref, va_ref, att_ref, do_ref, x_ref, t_ref, dst_ref, doa_ref, dz_ref, a_ref, b_ref,
    wo_ref, w_buf, own_ref, send_ref, sems,
):
    core, chip, lead, second = scal[0], scal[1], scal[3], scal[4]
    pairs, _, full, _ = qa_ref.shape
    block = full // 4
    cols = pairs * PAIR
    scale = float(HEAD_DIM) ** (-0.5)
    other, far = 1 - core, 1 - chip
    io = Copies(sems)
    loads = []
    for p in range(pairs):
        copies = []
        for source, t, place in (
            (do_own.at[p], 0, 2 * chip + core),
            (do_own.at[p], 1, 2 * far + core),
            (do_oth.at[p], 0, 2 * chip + other),
            (do_oth.at[p], 1, 2 * far + other),
        ):
            copies.append(
                io.start(source.at[pl.ds(t * block, block), :], do_ref.at[p, aligned(place, block), :])
            )
        for source, target in ((att, att_ref), (ka, ka_ref), (qa, qa_ref), (va, va_ref)):
            copies.append(io.start(source.at[p], target.at[p]))
        if p == 0:
            copies.append(io.start(tables, t_ref))
        loads.append(copies)
        if p == 0:
            late = io.start(x_all, x_ref)
    outputs = [io.start(wo_keep, wo_ref.at[0]), io.start(wo_got, wo_ref.at[1])]
    last = [io.start(dmixed1, own_ref), io.start(w_all, w_buf)]

    lane = lax.broadcasted_iota(jnp.int32, (1, PAIR), 1)
    low = lane < HEAD_DIM
    causal = lax.broadcasted_iota(jnp.int32, (block, block), 0) <= lax.broadcasted_iota(
        jnp.int32, (block, block), 1
    )
    height = x_ref.shape[1] // SUPER

    def back(g, rows):
        return (
            g * t_ref[0, rows, :]
            - pltpu.roll(g, 96, 1) * t_ref[2, rows, :]
            - pltpu.roll(g, 32, 1) * t_ref[1, rows, :]
        ).astype(BF16)

    for p in range(pairs):
        for copy in loads[p]:
            copy.wait()
        grad_do = do_ref[p].astype(F32)
        prod = grad_do * att_ref[p].astype(F32)
        for h in range(2):
            mine = low if h == 0 else jnp.logical_not(low)
            delta = jnp.sum(jnp.where(mine, prod, 0.0), axis=1, keepdims=True)
            doa_ref[h] = beside(lane, h, grad_do, split_three(-delta)).astype(BF16)
        for j in range(4):
            keys = slice(j * block, (j + 1) * block)
            span = slice(j * block, full)
            dk, dv = [], []
            for h in range(2):
                st = dot_nt(ka_ref[p, h, keys, :], qa_ref[p, h, span, :])
                dpt = dot_nt(va_ref[p, h, keys, :], doa_ref[h, span, :])
                pt = jnp.exp(st)
                diag = jnp.where(causal, pt[:, :block], 0.0)
                pt = diag if j == 3 else jnp.concatenate([diag, pt[:, block:]], axis=1)
                dst = (pt * dpt).astype(BF16)
                dst_ref[h, keys, span] = dst
                dv.append(dot_nn(pt.astype(BF16), doa_ref[h, span, :]))
                dk.append(dot_nn(dst, qa_ref[p, h, span, :]))
            dz_ref[p, keys, PAIR:2 * PAIR] = back(jnp.where(low, dk[0], dk[1]), keys)
            dz_ref[p, keys, 2 * PAIR:] = jnp.where(low, dv[0], dv[1]).astype(BF16)
        for i in range(4):
            rows = slice(i * block, (i + 1) * block)
            span = slice(0, (i + 1) * block)
            dq = [dot_tn(dst_ref[h, span, rows], ka_ref[p, h, span, :]) for h in range(2)]
            dz_ref[p, rows, :PAIR] = back(jnp.where(low, dq[0], dq[1]) * scale, rows)
        if p == 0:
            late.wait()
        grad = dot_tn(x_ref[...], dz_ref[p])
        if p < pairs - 1:
            pack(a_ref, grad, xy_first, 0, p * 3 * height, height)
        else:
            for copy in outputs:
                copy.wait()
            above = wo_ref.shape[2]
            b_ref[:, :above, :] = (wo_ref[0].astype(F32) + wo_ref[1].astype(F32)).astype(BF16)
            pack(b_ref, grad, xy_first, 0, above, height)
        if p == pairs - 2:
            io.send(a_ref, grad_a)
            io.send(a_ref.at[aligned(1 - lead, 8)], first_a)
    io.send(b_ref, grad_b)
    for i in range(2):
        io.send(b_ref.at[aligned(2 * i + 1 - second, 4)], first_b.at[4 * i:4 * i + 4])
    for copy in last:
        copy.wait()
    for side, target, out in ((other, send_ref, send_out), (core, own_ref, own_out)):
        left = jnp.concatenate(
            [
                jnp.concatenate(
                    [
                        dz_ref[p, aligned(2 * x + side, block), i * PAIR:(i + 1) * PAIR]
                        for i in range(3)
                        for p in range(pairs)
                    ],
                    axis=1,
                )
                for x in (chip, far)
            ]
        )
        grad = dot_nt(left, w_buf[...])
        if target is own_ref:
            grad += own_ref[...]
        target[...] = grad.astype(target.dtype)
        io.send(target, out)
    io.drain()


def attention_backward(
    scal, qa, ka, va, att, do_own, do_oth, x_all, tables, dmixed1, w_all, wo_keep, wo_got
):
    full, width = x_all.shape
    pairs = qa.shape[0]
    height = 3 * (width // SUPER)
    aug, rows = (qa.shape, BF16), ((pairs, full, PAIR), BF16)
    own, send = (dmixed1.shape, F32), (dmixed1.shape, BF16)
    part_a = ((pairs - 1) * height, LANES)
    part_b = (wo_keep.shape[1] + height, LANES)
    grads = [((SUPER,) + part_a, BF16), ((SUPER,) + part_b, BF16)]
    halves = [((SUPER // 2,) + part_a, BF16), ((SUPER // 2,) + part_b, BF16)]
    return kernel_call(
        attention_backward_kernel, "attention_backward", [own, send] + grads + halves,
        [sspec()] + [hspec()] * 5 + [aspec()] + [hspec()] * 4 + [aspec()] * 2,
        [pltpu.VMEM(*z) for z in [
            aug, aug, aug, rows, rows, ((full, width), BF16), (tables.shape, F32),
            ((2, full, full), BF16), ((2, full, PAIR), BF16), ((pairs, full, 3 * PAIR), BF16),
        ] + grads + [
            ((2,) + wo_keep.shape, BF16), ((width, pairs * 3 * PAIR), BF16), own, send,
        ]] + [pltpu.SemaphoreType.DMA((12 * pairs + 6,))],
        pairs * (10 * full * full * PAIR + 9 * full * width * PAIR), 20_000_000, full * full * 6, vmem=32,
        through=[
            (n, (z.shape, z.dtype))
            for n, z in ((1, qa), (2, ka), (3, va), (4, att), (7, x_all), (8, tables), (9, dmixed1), (10, w_all))
        ],
    )(scal, qa, ka, va, att, do_own, do_oth, x_all, tables, dmixed1, w_all, wo_keep, wo_got)[:6]


def assemble_kernel(layout, scal, stay, got, *outs):
    core = scal[0]
    for source, side in ((stay, core), (got, 1 - core)):
        row = 0
        for out, (rows, chunks) in zip(outs, layout):
            for j in range(chunks):
                out[:, aligned(side * chunks + j, LANES)] = source[row:row + rows, :]
                row += rows


def assemble(scal, stay, got, layout):
    return pl.pallas_call(
        functools.partial(assemble_kernel, layout),
        out_shape=tuple(jax.ShapeDtypeStruct((r, 2 * c * LANES), F32) for r, c in layout),
        in_specs=[sspec(), vspec(), vspec()],
        out_specs=(vspec(),) * len(layout),
        compiler_params=pltpu.CompilerParams(vmem_limit_bytes=16 * 1024 * 1024),
        cost_estimate=pl.CostEstimate(flops=0, bytes_accessed=16 * stay.shape[0] * LANES, transcendentals=0),
        name="assemble",
    )(scal, stay, got)


def assemble_pairs_kernel(half, pairs, scal, stay, got, *outs):
    core = scal[0]
    for source, side in ((stay, core), (got, 1 - core)):
        for i, out in enumerate(outs):
            for p in range(pairs):
                if i == 0:
                    chunk = 3 * pairs - 3 + p
                else:
                    chunk = 3 * p + i - 1 + (pairs if p == pairs - 1 else 0)
                out[:, aligned(side * pairs + p, LANES)] = source[chunk * half:(chunk + 1) * half, :]


def assemble_pairs(scal, stay, got, half, pairs):
    return pl.pallas_call(
        functools.partial(assemble_pairs_kernel, half, pairs),
        out_shape=(jax.ShapeDtypeStruct((half, 2 * pairs * LANES), F32),) * 4,
        in_specs=[sspec(), vspec(), vspec()],
        out_specs=(vspec(),) * 4,
        compiler_params=pltpu.CompilerParams(vmem_limit_bytes=16 * 1024 * 1024),
        cost_estimate=pl.CostEstimate(flops=0, bytes_accessed=16 * stay.shape[0] * LANES, transcendentals=0),
        name="assemble_pairs",
    )(scal, stay, got)


class Part:
    def __init__(self, names, leaves):
        self.names = list(names)
        dims = (2,) * len(self.names)
        self.leaves = [leaf.reshape(dims + leaf.shape[-2:]) for leaf in leaves]

    def take(self, index):
        return [lax.dynamic_index_in_dim(leaf, index, 0, keepdims=False) for leaf in self.leaves]

    def outgoing(self, me):
        return sum(leaf.astype(F32) for leaf in self.take(1 - me)).astype(BF16)

    def incoming(self, me, got):
        self.names = self.names[1:]
        dims = (2,) * len(self.names)
        stay = self.take(me)
        if len(self.names) < 3:
            stay = [lax.optimization_barrier(sum(leaf.astype(F32) for leaf in stay))]
        self.leaves = stay + [got.reshape(dims + (-1, got.shape[-1]))]

    def result(self):
        return sum(leaf.astype(F32) for leaf in self.leaves)


def swap_seq(value, bit):
    return lax.ppermute(value, "seq", [(i, i ^ bit) for i in range(4)])


def after(value, *others):
    return lax.optimization_barrier((value,) + others)[0]


def on_device(
    batch_size,
    hidden_in,
    cotangent,
    lengths,
    w_query,
    w_key,
    w_value,
    w_output,
    w_gate,
    w_up,
    w_down,
    gain_attn,
    gain_mlp,
):
    seqs, block, width = hidden_in.shape
    tokens = seqs * block
    cols = width // 2
    pairs = cols // PAIR
    height = width // SUPER
    rank = lax.axis_index("seq")
    batch = lax.axis_index("batch")
    chip, core = rank // 2, rank % 2
    far, other = 1 - chip, 1 - core

    def pick(z, index):
        return lax.dynamic_index_in_dim(z, index, 0, keepdims=False)

    def home(kept, back):
        first = chip == 0
        return jnp.stack([jnp.where(first, kept, back), jnp.where(first, back, kept)])

    kept = pick(hidden_in, chip)
    recv = swap_seq(pick(hidden_in, far), 2)
    kept_o = swap_seq(kept, 1)
    tables = rope_tables(4 * block)
    gain_a, gain_m = gain_attn[None, :], gain_mlp[None, :]

    bits = batch_size.bit_length() - 1
    names = ["b%d" % i for i in reversed(range(bits))] + ["x"]
    top, rest = names[:4][::-1], names[4:]

    def index_of(name):
        return chip if name == "x" else (batch >> int(name[1:])) & 1

    scal = jnp.stack(
        [core, chip, pick(lengths, chip), index_of(top[0]), index_of(top[1])]
    ).astype(jnp.int32)

    def exchange(value, name):
        if name == "x":
            return swap_seq(value, 2)
        bit = 1 << int(name[1:])
        return lax.ppermute(value, "batch", [(i, i ^ bit) for i in range(batch_size)])

    class Sum:
        def __init__(self, *parts):
            self.parts = list(parts)

        def out(self, ready=None):
            me = index_of(self.parts[0].names[0])
            sends = [part.outgoing(me) for part in self.parts] if ready is None else [ready]
            self.sent = sends[0] if len(sends) == 1 else jnp.concatenate(sends, axis=-2)
            return self.sent

        def move(self):
            self.got = exchange(self.sent, self.parts[0].names[0])

        def land(self):
            me, row = index_of(self.parts[0].names[0]), 0
            for part in self.parts:
                rows = part.leaves[0].shape[-2]
                part.incoming(me, lax.slice_in_dim(self.got, row, row + rows, axis=self.got.ndim - 2))
                row += rows

        def hop(self):
            self.out()
            self.move()
            self.land()

    def swapped(part):
        part.names = [part.names[1], part.names[0]] + part.names[2:]
        part.leaves = [leaf.swapaxes(0, 1) for leaf in part.leaves]
        return part

    w_near, turns, q, k, v, w_all, tables = project_kept(
        scal, kept, kept_o, w_query, w_key, w_value, tables
    )
    ct_kept, ct_far = pick(cotangent, chip), pick(cotangent, far)
    recv, ct_kept, ct_far, _ = lax.optimization_barrier((recv, ct_kept, ct_far, w_all))
    recv_o = swap_seq(recv, 1)
    ct_recv = swap_seq(ct_far, 2)
    q, k, v, att, att_oth, x_all = attention_forward(
        scal, kept, recv, kept_o, recv_o, w_near, turns, q, k, v
    )
    got = swap_seq(att_oth, 1)
    (
        attended, norm1, root1, dmixed2, gain_row_m, dgate, dup,
        lay_kept, lay_away, down_keep, down_send, gate_keep, gate_send, up_keep, up_send,
    ) = ffn_forward(
        scal, gain_a, gain_m, kept, recv, att, got, ct_kept, ct_recv, w_output, w_gate, w_up, w_down
    )
    first = [swap_seq(z, 1) for z in (gate_send, up_send, down_send)]
    lay_back = swap_seq(lay_away, 2)
    dmixed1, do_own, do_send, wo_send, wo_keep = ffn_backward(
        scal, gain_a, gain_row_m, dgate, dup, dmixed2, norm1, root1, attended, w_output, w_gate, w_up
    )

    do_send, wo_send, lay_back, *first = lax.optimization_barrier(
        (do_send, wo_send, lay_back, *first)
    )
    do_oth, wo_got = swap_seq(do_send, 1), swap_seq(wo_send, 1)
    yz_names = [top[1], top[2], top[0], top[3]]
    xz_names = [top[0], top[2], top[1], top[3]]
    zy_names = [top[2], top[1], top[0], top[3]]
    gates = Sum(Part(xz_names, [gate_keep, first[0]]))
    ups = Sum(Part(yz_names, [up_keep, first[1]]))
    downs = Sum(Part(zy_names, [down_keep, first[2]]))
    sent = [z.out() for z in (gates, ups, downs)]
    scal_d = after(scal, *sent)
    for z in (gates, ups, downs):
        z.move()
    own_in, send_in, grads_a, grads_b, first_a, first_b = attention_backward(
        scal_d, q, k, v, att, do_own, do_oth, x_all, tables, dmixed1, w_all,
        wo_keep, wo_got,
    )

    send_in, first_a, first_b, gates.got, ups.got, downs.got = lax.optimization_barrier(
        (send_in, first_a, first_b, gates.got, ups.got, downs.got)
    )
    got_in = swap_seq(send_in, 1)
    alpha = Sum(Part(top, [grads_a]))
    beta = Sum(swapped(Part(top, [grads_b])))
    alpha.out(first_a)
    beta.out(first_b)
    alpha.move()
    beta.move()
    for z in (ups, downs, gates):
        z.land()
        z.out()
        z.move()
    g_in = (own_in + got_in.astype(F32)).astype(BF16)
    g_back = swap_seq(g_in[block:], 2)

    alpha.land()
    beta.land()
    alpha.out()
    beta.out()
    alpha.move()
    beta.move()
    gates.got = after(gates.got, alpha.sent)
    ups.got = after(ups.got, alpha.sent)
    downs.got = after(downs.got, beta.sent)
    for z in (gates, ups, downs):
        z.land()
        z.out()
        z.move()
    alpha.land()
    beta.land()
    others = Sum(*alpha.parts, *beta.parts)
    others.out()
    others.move()
    for z in (gates, ups, downs):
        z.got = after(z.got, others.sent)
        z.land()
    feeds = Sum(*gates.parts, *ups.parts, *downs.parts)
    feeds.out()
    feeds.move()
    others.land()
    others.out()
    others.move()
    feeds.got = after(feeds.got, others.sent)
    others.land()
    feeds.land()
    lay_kept = after(lay_kept, feeds.sent)

    high = w_gate.shape[1] // SUPER
    wide = w_gate.shape[1] // 2 // LANES
    gate_sum, up_sum, down_sum = [z.result() for z in feeds.parts]
    alpha_sum, beta_sum = [z.result() for z in others.parts]
    above = pairs * height
    gain_rows = beta_sum[above:above + 16]
    feed = [(high, pairs)] + [(height, wide)] * 2
    feed_sums = [down_sum, gate_sum, up_sum]
    rest_layout = [(height, 1)] * (3 * pairs - 3) + [(height, pairs)] + [(height, 1)] * 3
    rest_sums = [alpha_sum, beta_sum[:above], beta_sum[above + 16:]]
    grad_in_of = lambda: home(g_in[:block], g_back)
    if rest:
        return finish_general(
            feed, feed_sums, rest_layout, rest_sums, gain_rows, rest, index_of, exchange, core, pairs,
            home(lay_kept, lay_back), grad_in_of(),
        )

    def sides(totals, layout):
        total, row, pieces = jnp.concatenate(totals), 0, []
        for rows, chunks in layout:
            pieces.append(total[row:row + rows * chunks].reshape(chunks, 2, rows // 2, LANES))
            row += rows * chunks
        return [
            jnp.concatenate(
                [lax.dynamic_index_in_dim(z, i, 1, keepdims=False).reshape(-1, LANES) for z in pieces]
            )
            for i in (other, core)
        ]

    away, stay = sides(feed_sums, feed)
    g_down, g_gate, g_up = assemble(
        scal, stay, swap_seq(away, 1), [(rows // 2, chunks) for rows, chunks in feed]
    )
    half = height // 2
    away, stay = sides(rest_sums, rest_layout)
    last = swap_seq(jnp.concatenate([away, gain_rows[:8]]), 1)
    g_output, g_query, g_key, g_value = assemble_pairs(scal, stay, last, half, pairs)
    gains = jnp.where(core == 0, jnp.stack([gain_rows[0], last[-8]]), jnp.stack([last[-8], gain_rows[0]]))
    gains = lax.dynamic_slice_in_dim(gains, core * half, half, axis=1)
    layer_out = home(lay_kept, lay_back)
    return (
        layer_out, grad_in_of(), g_query, g_key, g_value, g_output, g_gate, g_up, g_down,
        gains[0], gains[1],
    )


def finish_general(
    feed, feed_sums, rest_layout, rest_sums, gain_rows, rest, index_of, exchange, core, pairs,
    layer_out, grad_in,
):
    def finish(packed, rows, chunks):
        matrix = packed.reshape(chunks, rows, LANES).transpose(1, 0, 2).reshape(rows, chunks * LANES)
        for name in rest:
            matrix = matrix.reshape(2, matrix.shape[0] // 2, matrix.shape[1])
            me = index_of(name)
            away = lax.dynamic_index_in_dim(matrix, 1 - me, 0, keepdims=False)
            stay = lax.dynamic_index_in_dim(matrix, me, 0, keepdims=False)
            matrix = stay + exchange(away.astype(BF16), name).astype(F32)
        matrix = matrix.reshape(2, matrix.shape[0] // 2, matrix.shape[1])
        stay = lax.dynamic_index_in_dim(matrix, core, 0, keepdims=False)
        got = swap_seq(lax.dynamic_index_in_dim(matrix, 1 - core, 0, keepdims=False), 1)
        return jnp.where(
            core == 0,
            jnp.concatenate([stay, got], axis=-1),
            jnp.concatenate([got, stay], axis=-1),
        )

    def matrices(total, layout):
        row, out = 0, []
        for rows, chunks in layout:
            out.append((total[row:row + rows * chunks], rows, chunks))
            row += rows * chunks
        return out

    down, gate, up = matrices(jnp.concatenate(feed_sums), feed)
    qkv = matrices(jnp.concatenate(rest_sums), rest_layout)
    output = qkv.pop(3 * pairs - 3)
    height = output[1]
    by_matrix = [
        (jnp.concatenate([qkv[3 * p + i][0] for p in range(pairs)]), height, pairs) for i in range(3)
    ]
    gains = jnp.broadcast_to(gain_rows[0, :height, None], (height, LANES))
    outs = [finish(*z) for z in by_matrix + [output, gate, up, down, (gains, height, 1)]]
    gains = outs.pop()
    return (layer_out, grad_in, *outs, gains[:, 0], gains[:, LANES])


def solution(mesh):
    tokens = P("batch", "seq", None)
    rows = P(("batch", "seq"), None)
    return jax.shard_map(
        functools.partial(on_device, mesh.shape["batch"]),
        mesh=mesh,
        in_specs=(tokens, tokens, P("batch")) + (P(),) * 9,
        out_specs=(tokens, tokens) + (rows,) * 7 + (P(("batch", "seq")),) * 2,
        check_vma=False,
    )
```

```python
import functools

import jax
import jax.numpy as jnp
import numpy as np
from jax import lax
from jax.experimental import pallas as pl
from jax.experimental.pallas import tpu as pltpu
from jax.sharding import PartitionSpec as P

HEADS = 12
HEAD_DIM = 64
PAIR = 2 * HEAD_DIM

EPS = 1e-06
NEG = -1e30
LANES = 128
SUPER = 16

F32 = jnp.float32
BF16 = jnp.bfloat16


def dot_nn(left, right):
    return lax.dot_general(left, right, (((1,), (0,)), ((), ())), preferred_element_type=F32)


def dot_nt(left, right):
    return lax.dot_general(left, right, (((1,), (1,)), ((), ())), preferred_element_type=F32)


def dot_tn(left, right):
    return lax.dot_general(left, right, (((0,), (0,)), ((), ())), preferred_element_type=F32)


def rope_tables(count):
    half = HEAD_DIM // 2
    inverse = 10000.0 ** (-(np.arange(half, dtype=np.float32) * np.float32(2.0)) / HEAD_DIM)
    angles = np.arange(count, dtype=np.float32)[:, None] * inverse.astype(np.float32)[None, :]
    cosine, sine = np.cos(angles), np.sin(angles)
    zero = np.zeros_like(sine)
    tables = (
        np.concatenate([cosine] * 4, axis=-1),
        np.concatenate([zero, sine] * 2, axis=-1),
        np.concatenate([-sine, zero] * 2, axis=-1),
    )
    return jnp.asarray(np.stack(tables), F32)


def start(source, target, sem):
    copy = pltpu.make_async_copy(source, target, sem)
    copy.start()
    return copy


def aligned(index, size):
    return pl.ds(pl.multiple_of(index * size, size), size)


def vspec():
    return pl.BlockSpec(memory_space=pltpu.VMEM)


def hspec():
    return pl.BlockSpec(memory_space=pltpu.HBM)


def aspec():
    return pl.BlockSpec(memory_space=pl.ANY)


def sspec():
    return pl.BlockSpec(memory_space=pltpu.SMEM)


def mean_row(z):
    return jnp.sum(z, axis=1, keepdims=True) * (1.0 / z.shape[1])


def reversed_bits(index, bits):
    out = 0
    for i in range(bits):
        out |= ((index >> i) & 1) << (bits - 1 - i)
    return out


def xy_first(b):
    return reversed_bits(b, 4)


def xz_first(b):
    zh, zl, y, x = (b >> 3) & 1, (b >> 2) & 1, (b >> 1) & 1, b & 1
    return x * 8 + zl * 4 + y * 2 + zh


def yz_first(b):
    zh, zl, y, x = (b >> 3) & 1, (b >> 2) & 1, (b >> 1) & 1, b & 1
    return y * 8 + zl * 4 + x * 2 + zh


def zy_first(b):
    zh, zl, y, x = (b >> 3) & 1, (b >> 2) & 1, (b >> 1) & 1, b & 1
    return zl * 8 + y * 4 + x * 2 + zh


def pack(out_ref, value, place, block0, row0, height):
    low = value.astype(BF16)
    for b in range(value.shape[0] // height):
        for j in range(value.shape[1] // LANES):
            out_ref[place(block0 + b), row0 + j * height:row0 + (j + 1) * height, :] = low[
                b * height:(b + 1) * height, j * LANES:(j + 1) * LANES
            ]


def kernel_call(
    kernel, name, outs, specs, scratch, flops, moved, exps=0, resident=(), vmem=16, free=(), through=(),
    updated=None,
):
    count = len(resident) + len(outs)
    through = tuple(through)
    if through:
        inner = kernel

        def kernel(*refs):
            at = len(specs) + count
            inner(*refs[:at], *refs[at + len(through):])

    return pl.pallas_call(
        kernel,
        out_shape=tuple(pltpu.VMEM(*z) for z in resident)
        + tuple(
            jax.ShapeDtypeStruct(*z) if i in free else pltpu.HBM(*z) for i, z in enumerate(outs)
        )
        + tuple(pltpu.HBM(*z) for _, z in through),
        in_specs=specs,
        out_specs=(vspec(),) * len(resident)
        + tuple(aspec() if i in free else hspec() for i in range(len(outs)))
        + (hspec(),) * len(through),
        input_output_aliases={n: count + i for i, (n, _) in enumerate(through)} | (updated or {}),
        scratch_shapes=scratch,
        compiler_params=pltpu.CompilerParams(vmem_limit_bytes=vmem * 1024 * 1024),
        cost_estimate=pl.CostEstimate(flops=flops, bytes_accessed=moved, transcendentals=exps),
        name=name,
    )


class Copies:
    def __init__(self, sems):
        self.sems, self.used, self.open = sems, 0, []

    def start(self, source, target):
        copy = start(source, target, self.sems.at[self.used])
        self.used += 1
        return copy

    def send(self, source, target):
        self.open.append(self.start(source, target))

    def drain(self):
        for copy in self.open:
            copy.wait()


def split_three(value):
    first = value.astype(BF16).astype(F32)
    rest = value - first
    second = rest.astype(BF16).astype(F32)
    return first, second, (rest - second).astype(BF16).astype(F32)


def beside(lane, head, mine, pieces):
    own = (lane < HEAD_DIM) if head == 0 else (lane >= HEAD_DIM)
    first = (1 - head) * HEAD_DIM
    out = jnp.zeros_like(mine)
    for i, piece in enumerate(pieces):
        out = jnp.where(lane == first + i, piece, out)
    return jnp.where(own, mine, out)


def project(x_ref, w_buf, t_ref, q_ref, k_ref, v_ref, places, length):
    pairs = q_ref.shape[0]
    block = x_ref.shape[0] // 2
    scale = float(HEAD_DIM) ** (-0.5)
    lane = lax.broadcasted_iota(jnp.int32, (1, PAIR), 1)
    z_all = dot_nn(x_ref[...], w_buf[...])
    for t, place in enumerate(places):
        z = z_all[t * block:(t + 1) * block]
        rows = aligned(place, block)
        c, a, b = t_ref[0, rows, :], t_ref[1, rows, :], t_ref[2, rows, :]
        slot = place * block + lax.broadcasted_iota(jnp.int32, (block, PAIR), 0)
        bias = jnp.where(slot < length, 0.0, NEG)
        for p in range(3 * pairs):
            part = z[:, p * PAIR:(p + 1) * PAIR]
            if p < 2 * pairs:
                part = part * c + pltpu.roll(part, 32, 1) * a + pltpu.roll(part, 96, 1) * b
            for h in range(2):
                if p < pairs:
                    mine = part.astype(BF16).astype(F32) * scale
                    q_ref[p, h, rows, :] = beside(lane, h, mine, (0.0, 0.0, 0.0, 1.0)).astype(BF16)
                elif p < 2 * pairs:
                    k_ref[p - pairs, h, rows, :] = beside(
                        lane, h, part, (1.0, 1.0, 1.0, bias)
                    ).astype(BF16)
                else:
                    own = (lane < HEAD_DIM) if h == 0 else (lane >= HEAD_DIM)
                    v_ref[p - 2 * pairs, h, rows, :] = jnp.where(own, part, 1.0).astype(BF16)


def project_kept_kernel(
    scal, kept, kept_o, wq, wk, wv, tables, w_buf, t_ref, q_ref, k_ref, v_ref, w_out, t_out, x_ref, sems
):
    core, chip, length = scal[0], scal[1], scal[2]
    block = kept.shape[0]
    cols = wq.shape[1] // 2
    io = Copies(sems)
    columns = pl.ds(pl.multiple_of(core * cols, PAIR), cols)
    needed = [
        io.start(w.at[:, columns], w_buf.at[:, i * cols:(i + 1) * cols])
        for i, w in enumerate((wq, wk, wv))
    ]
    needed.append(io.start(kept, x_ref.at[0:block, :]))
    needed.append(io.start(kept_o, x_ref.at[block:, :]))
    needed.append(io.start(tables, t_ref))
    for copy in needed:
        copy.wait()
    io.send(w_buf, w_out)
    io.send(t_ref, t_out)
    places = (2 * chip + core, 2 * chip + 1 - core)
    project(x_ref, w_buf, t_ref, q_ref, k_ref, v_ref, places, length)
    io.drain()


def project_kept(scal, kept, kept_o, wq, wk, wv, tables):
    block, width = kept.shape
    cols = width // 2
    aug = ((cols // PAIR, 2, 4 * block, PAIR), BF16)
    weights, turns = ((width, 3 * cols), BF16), (tables.shape, F32)
    return kernel_call(
        project_kept_kernel, "project_kept", [weights, turns],
        [sspec()] + [aspec()] * 2 + [hspec()] * 4,
        [pltpu.VMEM((2 * block, width), BF16), pltpu.SemaphoreType.DMA((8,))],
        4 * block * width * 3 * cols, 8_000_000, vmem=40, resident=[weights, turns, aug, aug, aug],
    )(scal, kept, kept_o, wq, wk, wv, tables)


def attention_forward_kernel(
    scal, kept, recv, kept_o, recv_o, w_buf, t_ref, q_in, k_in, v_in,
    q_ref, k_ref, v_ref,
    q_out, k_out, v_out, att_out, oth_out, x_out,
    x_ref, x_new, att_ref, sems,
):
    del q_in, k_in, v_in
    core, chip, length = scal[0], scal[1], scal[2]
    block = kept.shape[0]
    pairs = q_ref.shape[0]
    other, far = 1 - core, 1 - chip
    io = Copies(sems)
    needed = [io.start(recv, x_new.at[0:block, :]), io.start(recv_o, x_new.at[block:, :])]
    blocks = [
        io.start(source, x_ref.at[aligned(place, block), :])
        for source, place in (
            (kept, 2 * chip + core),
            (recv, 2 * far + core),
            (kept_o, 2 * chip + other),
            (recv_o, 2 * far + other),
        )
    ]
    for copy in needed:
        copy.wait()
    project(x_new, w_buf, t_ref, q_ref, k_ref, v_ref, (2 * far + core, 2 * far + other), length)
    for copy in blocks:
        copy.wait()
    for source, out in ((x_ref, x_out), (k_ref, k_out), (v_ref, v_out)):
        io.send(source, out)

    lane = lax.broadcasted_iota(jnp.int32, (1, PAIR), 1)
    low = lane < HEAD_DIM
    causal = lax.broadcasted_iota(jnp.int32, (block, block), 1) <= lax.broadcasted_iota(
        jnp.int32, (block, block), 0
    )

    def scores(p, h, i):
        span = (i + 1) * block
        s = dot_nt(q_ref[p, h, i * block:span, :], k_ref[p, h, :span, :])
        diag = jnp.where(causal, s[:, i * block:], NEG)
        return jnp.concatenate([s[:, :i * block], diag], axis=1) if i else diag

    outs, tops = {}, {}

    def attend(unit, e):
        p, h, i = unit
        outs[unit] = dot_nn(e, v_ref[p, h, :(i + 1) * block, :])

    def finish(p):
        for i in range(4):
            rows = slice(i * block, (i + 1) * block)
            first, second = outs[p, 0, i], outs[p, 1, i]
            sums = pltpu.roll(jnp.where(low, second, first), HEAD_DIM, 1)
            att_ref[p, rows, :] = (jnp.where(low, first, second) / sums).astype(BF16)
            for h in range(2):
                lse = tops[p, h, i] + jnp.log(outs[p, h, i])
                mine = q_ref[p, h, rows, :].astype(F32)
                for n, piece in enumerate(split_three(-lse)):
                    mine = jnp.where(lane == (1 - h) * HEAD_DIM + n, piece, mine)
                q_ref[p, h, rows, :] = mine.astype(BF16)
        io.send(q_ref.at[p], q_out.at[p])
        io.send(att_ref.at[p], att_out.at[p])
        for t in range(2):
            place = 2 * (chip if t == 0 else far) + other
            io.send(
                att_ref.at[p, aligned(place, block), :], oth_out.at[p, t * block:(t + 1) * block, :]
            )

    units = [(p, h, i) for p in range(pairs) for h in range(2) for i in (3, 2, 1, 0)]
    ahead, behind = scores(*units[0]), None
    for n, unit in enumerate(units):
        s = ahead
        ahead = scores(*units[n + 1]) if n + 1 < len(units) else None
        if behind is not None:
            attend(*behind)
        if n and n % 8 == 0:
            finish(unit[0] - 1)
        top = jnp.max(s, axis=1, keepdims=True)
        tops[unit] = top
        behind = (unit, jnp.exp(s - top).astype(BF16))
    attend(*behind)
    finish(pairs - 1)
    io.drain()


def attention_forward(scal, kept, recv, kept_o, recv_o, w_all, turns, q, k, v):
    block, width = kept.shape
    full = 4 * block
    pairs = q.shape[0]
    aug = (q.shape, BF16)
    return kernel_call(
        attention_forward_kernel, "attention_forward",
        [aug, aug, aug, ((pairs, full, PAIR), BF16), ((pairs, full // 2, PAIR), BF16),
         ((full, width), BF16)],
        [sspec()] + [aspec()] * 4 + [vspec()] * 5,
        [
            pltpu.VMEM((full, width), BF16),
            pltpu.VMEM((full // 2, width), BF16),
            pltpu.VMEM((pairs, full, PAIR), BF16),
            pltpu.SemaphoreType.DMA((9 + 4 * pairs,)),
        ],
        full * width * width * 3 // 2 + 4 * full * full * pairs * PAIR, 14_000_000, full * full * 6,
        resident=[aug, aug, aug], vmem=44, updated={7: 0, 8: 1, 9: 2},
    )(scal, kept, recv, kept_o, recv_o, w_all, turns, q, k, v)[3:]


def load_attended(io, target, att, got, places, block):
    pairs = att.shape[0]
    copies = []
    for p in range(pairs):
        for t in range(2):
            copies.append(
                io.start(
                    att.at[p, aligned(places[t], block), :],
                    target.at[t * block:(t + 1) * block, p * PAIR:(p + 1) * PAIR],
                )
            )
        copies.append(io.start(got.at[p], target.at[:, (pairs + p) * PAIR:(pairs + p + 1) * PAIR]))
    return copies


def load_output_weight(io, target, wo, core, cols):
    return [
        io.start(wo.at[aligned(core, cols), :], target.at[0:cols, :]),
        io.start(wo.at[aligned(1 - core, cols), :], target.at[cols:, :]),
    ]


def ffn_forward_kernel(
    scal, gain_a, gain_m, kept, recv, att, got, ct_kept, ct_recv, wo, wg, wu, wd,
    att_ref, norm1_ref, root1_ref, dmixed2_ref, gain_row_ref, dgate_ref, dup_ref,
    lay_kept, lay_away, down_keep, down_send, gate_keep, gate_send, up_keep, up_send,
    wo_buf, wg_buf, wu_buf, wd_buf, x_ref, ct_ref, lay_ref, x1_low_ref, dm_ref, gate_ref, up_ref,
    hid_ref, dk_ref, ds_ref, gk_ref, gs_ref, uk_ref, us_ref, sems,
):
    core, chip, length = scal[0], scal[1], scal[2]
    block, width = kept.shape
    cols = width // 2
    ff = wg.shape[1]
    step = ff // 4
    other, far = 1 - core, 1 - chip
    places = (2 * chip + core, 2 * far + core)
    io = Copies(sems)
    first = load_attended(io, att_ref, att, got, places, block)
    first += load_output_weight(io, wo_buf, wo, core, cols)
    first.append(io.start(kept, x_ref.at[0:block, :]))
    first.append(io.start(recv, x_ref.at[block:, :]))
    weights = []
    for f in range(4):
        part = slice(f * step, (f + 1) * step)
        weights.append(io.start(wg.at[:, part], wg_buf.at[:, part]))
        weights.append(io.start(wu.at[:, part], wu_buf.at[:, part]))
    down = io.start(wd, wd_buf)
    late = [io.start(ct_kept, ct_ref.at[0:block, :]), io.start(ct_recv, ct_ref.at[block:, :])]
    for copy in first:
        copy.wait()
    mixed = x_ref[...].astype(F32) + dot_nn(att_ref[...], wo_buf[...])
    root = lax.rsqrt(mean_row(mixed * mixed) + EPS)
    norm = mixed * root
    norm1_ref[...] = norm
    root1_ref[...] = jnp.broadcast_to(root, root1_ref.shape)
    x1_low_ref[...] = (norm * gain_a[...]).astype(BF16)
    for f in range(4):
        part = slice(f * step, (f + 1) * step)
        weights[2 * f].wait()
        weights[2 * f + 1].wait()
        gate = dot_nn(x1_low_ref[...], wg_buf[:, part])
        up = dot_nn(x1_low_ref[...], wu_buf[:, part])
        hid_ref[:, part] = (gate * jax.nn.sigmoid(gate) * up).astype(BF16)
        gate_ref[:, part] = gate.astype(BF16)
        up_ref[:, part] = up.astype(BF16)
    down.wait()
    mixed = norm1_ref[...] * gain_a[...] + dot_nn(hid_ref[...], wd_buf[...])
    root = lax.rsqrt(mean_row(mixed * mixed) + EPS)
    norm = mixed * root
    slot = lax.broadcasted_iota(jnp.int32, (2 * block, 1), 0)
    slot = jnp.where(slot < block, places[0] * block + slot, (places[1] - 1) * block + slot)
    valid = (slot < length).astype(F32)
    lay_ref[...] = (valid * (norm * gain_m[...])).astype(BF16)
    io.send(lay_ref.at[0:block, :], lay_kept)
    io.send(lay_ref.at[block:, :], lay_away)
    for copy in late:
        copy.wait()
    d_out = valid * ct_ref[...].astype(F32)
    gain_row = jnp.sum(d_out * norm, axis=0, keepdims=True)
    gain_row_ref[...] = jnp.broadcast_to(gain_row, gain_row_ref.shape)
    d_norm = d_out * gain_m[...]
    d_mixed = root * (d_norm - norm * mean_row(d_norm * norm))
    dmixed2_ref[...] = d_mixed
    dm_ref[...] = d_mixed.astype(BF16)
    right = jnp.concatenate([dm_ref[:, aligned(other, cols)], dm_ref[:, aligned(core, cols)]], axis=1)
    height = ff // SUPER
    for f in range(4):
        grad = dot_tn(hid_ref[:, f * step:(f + 1) * step], right)
        pack(ds_ref, grad[:, :cols], zy_first, f * step // height, 0, height)
        pack(dk_ref, grad[:, cols:], zy_first, f * step // height, 0, height)
    io.send(ds_ref, down_send)
    io.send(dk_ref, down_keep)
    height = width // SUPER
    rows = step // LANES * height
    for gate_part, gate_out, up_part, up_out, side in (
        (gs_ref, gate_send, us_ref, up_send, other), (gk_ref, gate_keep, uk_ref, up_keep, core),
    ):
        for sub in range(2):
            part = aligned(side * 2 + sub, step)
            d_hid = dot_nt(dm_ref[...], wd_buf[part, :])
            g = gate_ref[:, part].astype(F32)
            sigma = jax.nn.sigmoid(g)
            d_up = (d_hid * (g * sigma)).astype(BF16)
            d_gate = (
                d_hid * up_ref[:, part].astype(F32) * sigma * (1.0 + g * (1.0 - sigma))
            ).astype(BF16)
            dgate_ref[:, part] = d_gate
            dup_ref[:, part] = d_up
            pack(gate_part, dot_tn(x1_low_ref[...], d_gate), xz_first, 0, sub * rows, height)
            pack(up_part, dot_tn(x1_low_ref[...], d_up), yz_first, 0, sub * rows, height)
            at = slice(sub * rows, (sub + 1) * rows)
            io.send(gate_part.at[:, at, :], gate_out.at[:, at, :])
            io.send(up_part.at[:, at, :], up_out.at[:, at, :])
    io.drain()


def ffn_forward(scal, gain_a, gain_m, kept, recv, att, got, ct_kept, ct_recv, wo, wg, wu, wd):
    block, width = kept.shape
    ff = wg.shape[1]
    tokens, cols = 2 * block, width // 2
    half = ((block, width), BF16)
    down = ((SUPER, ff // SUPER * (cols // LANES), LANES), BF16)
    wide = ((SUPER, width // SUPER * (ff // 2 // LANES), LANES), BF16)
    rows16, rows32 = ((tokens, width), BF16), ((tokens, width), F32)
    hidden = ((tokens, ff), BF16)
    return kernel_call(
        ffn_forward_kernel, "ffn_forward", [half, half, down, down, wide, wide, wide, wide],
        [sspec(), vspec(), vspec()] + [aspec()] * 2 + [hspec()] + [aspec()] * 3 + [hspec()] * 4,
        [pltpu.VMEM(*z) for z in [
            ((width, width), BF16), ((width, ff), BF16), ((width, ff), BF16), ((ff, width), BF16),
            rows16, rows16, rows16, rows16, rows16, hidden, hidden, hidden,
            down, down, wide, wide, wide, wide,
        ]] + [pltpu.SemaphoreType.DMA((27 + 3 * (cols // PAIR),))],
        2 * tokens * width * (width + 7 * ff), 26_000_000, 2 * tokens * ff, vmem=44,
        resident=[rows16, rows32, ((tokens, LANES), F32), rows32, ((8, width), F32), hidden, hidden],
    )(scal, gain_a, gain_m, kept, recv, att, got, ct_kept, ct_recv, wo, wg, wu, wd)


def ffn_backward_kernel(
    scal, gain_a, gain_row_m, dgate_ref, dup_ref, dmixed2_ref, norm1_ref, root1_ref, att_ref,
    wo, wg, wu,
    dmixed1_out, do_out, do_send_out, send_out, keep_out,
    wo_buf, wg_buf, wu_buf, dmixed1_ref, do_ref, do_send_ref, send_ref, keep_ref, da_ref, sems,
):
    core = scal[0]
    tokens, width = dmixed2_ref.shape
    cols = width // 2
    height = width // SUPER
    chunks = cols // LANES
    other = 1 - core
    ff = wg.shape[1]
    io = Copies(sems)
    weights = []
    for f in range(2):
        part = slice(f * ff // 2, (f + 1) * ff // 2)
        for weight, buffer in ((wg, wg_buf), (wu, wu_buf)):
            weights.append(io.start(weight.at[:, part], buffer.at[:, part]))
    last = load_output_weight(io, wo_buf, wo, core, cols)
    d_x1 = dmixed2_ref[...]
    for f in range(2):
        part = slice(f * ff // 2, (f + 1) * ff // 2)
        for n, (left, right) in enumerate(((dgate_ref, wg_buf), (dup_ref, wu_buf))):
            weights[2 * f + n].wait()
            d_x1 += dot_nt(left[:, part], right[:, part])
    norm = norm1_ref[...]
    gain_row = jnp.sum(d_x1 * norm, axis=0, keepdims=True)
    d_norm = d_x1 * gain_a[...]
    d_mixed = root1_ref[:, 0:1] * (d_norm - norm * mean_row(d_norm * norm))
    dmixed1_ref[...] = d_mixed
    da_ref[...] = d_mixed.astype(BF16)
    io.send(dmixed1_ref, dmixed1_out)
    for copy in last:
        copy.wait()
    d_att = dot_nt(da_ref[...], wo_buf[...]).astype(BF16)
    for p in range(chunks):
        do_ref[p] = d_att[:, p * LANES:(p + 1) * LANES]
        do_send_ref[p] = d_att[:, cols + p * LANES:cols + (p + 1) * LANES]
    io.send(do_ref, do_out)
    io.send(do_send_ref, do_send_out)
    right = jnp.concatenate([da_ref[:, aligned(other, cols)], da_ref[:, aligned(core, cols)]], axis=1)
    grad = dot_tn(att_ref[...], right).astype(BF16)
    for heads, row0 in ((core, 0), (other, cols)):
        for b in range(cols // height):
            position = 2 * reversed_bits(b, 3) + heads
            for j in range(2 * chunks):
                target = send_ref if j < chunks else keep_ref
                target[position, (j % chunks) * height:(j % chunks + 1) * height, :] = grad[
                    row0 + b * height:row0 + (b + 1) * height, j * LANES:(j + 1) * LANES
                ]
    for target, half in ((send_ref, other), (keep_ref, core)):
        row = jnp.broadcast_to(jnp.where(half == 0, gain_row, gain_row_m[0:1, :]), (16, width))
        for b in range(SUPER):
            turned = pltpu.roll(row, width - b * height, 1) if b else row
            target[xy_first(b), chunks * height:, :] = turned[:, :LANES].astype(BF16)
    io.send(send_ref, send_out)
    io.send(keep_ref, keep_out)
    io.drain()


def ffn_backward(scal, gain_a, gain_row_m, dgate, dup, dmixed2, norm1, root1, att, wo, wg, wu):
    tokens, width = dmixed2.shape
    ff = wg.shape[1]
    chunks = width // 2 // LANES
    packed = ((SUPER, chunks * (width // SUPER) + 16, LANES), BF16)
    split = ((chunks, tokens, LANES), BF16)
    outs = [((tokens, width), F32), split, split, packed, packed]
    return kernel_call(
        ffn_backward_kernel, "ffn_backward", outs,
        [sspec()] + [vspec()] * 8 + [hspec()] * 3,
        [pltpu.VMEM(*z) for z in [
            ((width, width), BF16), ((width, ff), BF16), ((width, ff), BF16),
        ] + outs + [((tokens, width), BF16)]] + [pltpu.SemaphoreType.DMA((11,))],
        2 * tokens * width * (2 * width + 2 * ff), 12_000_000, vmem=26,
    )(scal, gain_a, gain_row_m, dgate, dup, dmixed2, norm1, root1, att, wo, wg, wu)


def attention_backward_kernel(
    scal, qa, ka, va, att, do_own, do_oth, x_all, tables, dmixed1, w_all, wo_keep, wo_got,
    own_out, send_out, grad_a, grad_b, first_a, first_b,
    qa_ref, ka_ref, va_ref, att_ref, do_ref, x_ref, t_ref, dst_ref, doa_ref, dz_ref, a_ref, b_ref,
    wo_ref, w_buf, own_ref, send_ref, sems,
):
    core, chip, lead, second = scal[0], scal[1], scal[3], scal[4]
    pairs, _, full, _ = qa_ref.shape
    block = full // 4
    cols = pairs * PAIR
    scale = float(HEAD_DIM) ** (-0.5)
    other, far = 1 - core, 1 - chip
    io = Copies(sems)
    loads = []
    for p in range(pairs):
        copies = []
        for source, t, place in (
            (do_own.at[p], 0, 2 * chip + core),
            (do_own.at[p], 1, 2 * far + core),
            (do_oth.at[p], 0, 2 * chip + other),
            (do_oth.at[p], 1, 2 * far + other),
        ):
            copies.append(
                io.start(source.at[pl.ds(t * block, block), :], do_ref.at[p, aligned(place, block), :])
            )
        for source, target in ((att, att_ref), (ka, ka_ref), (qa, qa_ref), (va, va_ref)):
            copies.append(io.start(source.at[p], target.at[p]))
        if p == 0:
            copies.append(io.start(tables, t_ref))
        loads.append(copies)
        if p == 0:
            late = io.start(x_all, x_ref)
    outputs = [io.start(wo_keep, wo_ref.at[0]), io.start(wo_got, wo_ref.at[1])]
    last = [io.start(dmixed1, own_ref), io.start(w_all, w_buf)]

    lane = lax.broadcasted_iota(jnp.int32, (1, PAIR), 1)
    low = lane < HEAD_DIM
    causal = lax.broadcasted_iota(jnp.int32, (block, block), 0) <= lax.broadcasted_iota(
        jnp.int32, (block, block), 1
    )
    height = x_ref.shape[1] // SUPER

    def back(g, rows):
        return (
            g * t_ref[0, rows, :]
            - pltpu.roll(g, 96, 1) * t_ref[2, rows, :]
            - pltpu.roll(g, 32, 1) * t_ref[1, rows, :]
        ).astype(BF16)

    for p in range(pairs):
        for copy in loads[p]:
            copy.wait()
        grad_do = do_ref[p].astype(F32)
        prod = grad_do * att_ref[p].astype(F32)
        for h in range(2):
            mine = low if h == 0 else jnp.logical_not(low)
            delta = jnp.sum(jnp.where(mine, prod, 0.0), axis=1, keepdims=True)
            doa_ref[h] = beside(lane, h, grad_do, split_three(-delta)).astype(BF16)
        for j in range(4):
            keys = slice(j * block, (j + 1) * block)
            span = slice(j * block, full)
            dk, dv = [], []
            for h in range(2):
                st = dot_nt(ka_ref[p, h, keys, :], qa_ref[p, h, span, :])
                dpt = dot_nt(va_ref[p, h, keys, :], doa_ref[h, span, :])
                pt = jnp.exp(st)
                diag = jnp.where(causal, pt[:, :block], 0.0)
                pt = diag if j == 3 else jnp.concatenate([diag, pt[:, block:]], axis=1)
                dst = (pt * dpt).astype(BF16)
                dst_ref[h, keys, span] = dst
                dv.append(dot_nn(pt.astype(BF16), doa_ref[h, span, :]))
                dk.append(dot_nn(dst, qa_ref[p, h, span, :]))
            dz_ref[p, keys, PAIR:2 * PAIR] = back(jnp.where(low, dk[0], dk[1]), keys)
            dz_ref[p, keys, 2 * PAIR:] = jnp.where(low, dv[0], dv[1]).astype(BF16)
        for i in range(4):
            rows = slice(i * block, (i + 1) * block)
            span = slice(0, (i + 1) * block)
            dq = [dot_tn(dst_ref[h, span, rows], ka_ref[p, h, span, :]) for h in range(2)]
            dz_ref[p, rows, :PAIR] = back(jnp.where(low, dq[0], dq[1]) * scale, rows)
        if p == 0:
            late.wait()
        grad = dot_tn(x_ref[...], dz_ref[p])
        if p < pairs - 1:
            pack(a_ref, grad, xy_first, 0, p * 3 * height, height)
        else:
            for copy in outputs:
                copy.wait()
            above = wo_ref.shape[2]
            b_ref[:, :above, :] = (wo_ref[0].astype(F32) + wo_ref[1].astype(F32)).astype(BF16)
            pack(b_ref, grad, xy_first, 0, above, height)
        if p == pairs - 2:
            io.send(a_ref, grad_a)
            io.send(a_ref.at[aligned(1 - lead, 8)], first_a)
    io.send(b_ref, grad_b)
    for i in range(2):
        io.send(b_ref.at[aligned(2 * i + 1 - second, 4)], first_b.at[4 * i:4 * i + 4])
    for copy in last:
        copy.wait()
    for side, target, out in ((other, send_ref, send_out), (core, own_ref, own_out)):
        left = jnp.concatenate(
            [
                jnp.concatenate(
                    [
                        dz_ref[p, aligned(2 * x + side, block), i * PAIR:(i + 1) * PAIR]
                        for i in range(3)
                        for p in range(pairs)
                    ],
                    axis=1,
                )
                for x in (chip, far)
            ]
        )
        grad = dot_nt(left, w_buf[...])
        if target is own_ref:
            grad += own_ref[...]
        target[...] = grad.astype(target.dtype)
        io.send(target, out)
    io.drain()


def attention_backward(
    scal, qa, ka, va, att, do_own, do_oth, x_all, tables, dmixed1, w_all, wo_keep, wo_got
):
    full, width = x_all.shape
    pairs = qa.shape[0]
    height = 3 * (width // SUPER)
    aug, rows = (qa.shape, BF16), ((pairs, full, PAIR), BF16)
    own, send = (dmixed1.shape, F32), (dmixed1.shape, BF16)
    part_a = ((pairs - 1) * height, LANES)
    part_b = (wo_keep.shape[1] + height, LANES)
    grads = [((SUPER,) + part_a, BF16), ((SUPER,) + part_b, BF16)]
    halves = [((SUPER // 2,) + part_a, BF16), ((SUPER // 2,) + part_b, BF16)]
    return kernel_call(
        attention_backward_kernel, "attention_backward", [own, send] + grads + halves,
        [sspec()] + [hspec()] * 5 + [aspec()] + [hspec()] * 4 + [aspec()] * 2,
        [pltpu.VMEM(*z) for z in [
            aug, aug, aug, rows, rows, ((full, width), BF16), (tables.shape, F32),
            ((2, full, full), BF16), ((2, full, PAIR), BF16), ((pairs, full, 3 * PAIR), BF16),
        ] + grads + [
            ((2,) + wo_keep.shape, BF16), ((width, pairs * 3 * PAIR), BF16), own, send,
        ]] + [pltpu.SemaphoreType.DMA((12 * pairs + 6,))],
        pairs * (10 * full * full * PAIR + 9 * full * width * PAIR), 20_000_000, full * full * 6, vmem=32,
        through=[
            (n, (z.shape, z.dtype))
            for n, z in ((1, qa), (2, ka), (3, va), (4, att), (7, x_all), (8, tables), (9, dmixed1), (10, w_all))
        ],
    )(scal, qa, ka, va, att, do_own, do_oth, x_all, tables, dmixed1, w_all, wo_keep, wo_got)[:6]


def assemble_kernel(layout, scal, stay, got, *outs):
    core = scal[0]
    for source, side in ((stay, core), (got, 1 - core)):
        row = 0
        for out, (rows, chunks) in zip(outs, layout):
            for j in range(chunks):
                out[:, aligned(side * chunks + j, LANES)] = source[row:row + rows, :]
                row += rows


def assemble(scal, stay, got, layout):
    return pl.pallas_call(
        functools.partial(assemble_kernel, layout),
        out_shape=tuple(jax.ShapeDtypeStruct((r, 2 * c * LANES), F32) for r, c in layout),
        in_specs=[sspec(), vspec(), vspec()],
        out_specs=(vspec(),) * len(layout),
        compiler_params=pltpu.CompilerParams(vmem_limit_bytes=16 * 1024 * 1024),
        cost_estimate=pl.CostEstimate(flops=0, bytes_accessed=16 * stay.shape[0] * LANES, transcendentals=0),
        name="assemble",
    )(scal, stay, got)


def assemble_pairs_kernel(half, pairs, scal, stay, got, *outs):
    core = scal[0]
    for source, side in ((stay, core), (got, 1 - core)):
        for i, out in enumerate(outs):
            for p in range(pairs):
                if i == 0:
                    chunk = 3 * pairs - 3 + p
                else:
                    chunk = 3 * p + i - 1 + (pairs if p == pairs - 1 else 0)
                out[:, aligned(side * pairs + p, LANES)] = source[chunk * half:(chunk + 1) * half, :]


def assemble_pairs(scal, stay, got, half, pairs):
    return pl.pallas_call(
        functools.partial(assemble_pairs_kernel, half, pairs),
        out_shape=(jax.ShapeDtypeStruct((half, 2 * pairs * LANES), F32),) * 4,
        in_specs=[sspec(), vspec(), vspec()],
        out_specs=(vspec(),) * 4,
        compiler_params=pltpu.CompilerParams(vmem_limit_bytes=16 * 1024 * 1024),
        cost_estimate=pl.CostEstimate(flops=0, bytes_accessed=16 * stay.shape[0] * LANES, transcendentals=0),
        name="assemble_pairs",
    )(scal, stay, got)


class Part:
    def __init__(self, names, leaves):
        self.names = list(names)
        dims = (2,) * len(self.names)
        self.leaves = [leaf.reshape(dims + leaf.shape[-2:]) for leaf in leaves]

    def take(self, index):
        return [lax.dynamic_index_in_dim(leaf, index, 0, keepdims=False) for leaf in self.leaves]

    def outgoing(self, me):
        return sum(leaf.astype(F32) for leaf in self.take(1 - me)).astype(BF16)

    def incoming(self, me, got):
        self.names = self.names[1:]
        dims = (2,) * len(self.names)
        stay = self.take(me)
        if len(self.names) < 3:
            stay = [lax.optimization_barrier(sum(leaf.astype(F32) for leaf in stay))]
        self.leaves = stay + [got.reshape(dims + (-1, got.shape[-1]))]

    def result(self):
        return sum(leaf.astype(F32) for leaf in self.leaves)


def swap_seq(value, bit):
    return lax.ppermute(value, "seq", [(i, i ^ bit) for i in range(4)])


def after(value, *others):
    return lax.optimization_barrier((value,) + others)[0]


def on_device(
    batch_size,
    hidden_in,
    cotangent,
    lengths,
    w_query,
    w_key,
    w_value,
    w_output,
    w_gate,
    w_up,
    w_down,
    gain_attn,
    gain_mlp,
):
    seqs, block, width = hidden_in.shape
    tokens = seqs * block
    cols = width // 2
    pairs = cols // PAIR
    height = width // SUPER
    rank = lax.axis_index("seq")
    batch = lax.axis_index("batch")
    chip, core = rank // 2, rank % 2
    far, other = 1 - chip, 1 - core

    def pick(z, index):
        return lax.dynamic_index_in_dim(z, index, 0, keepdims=False)

    def home(kept, back):
        first = chip == 0
        return jnp.stack([jnp.where(first, kept, back), jnp.where(first, back, kept)])

    kept = pick(hidden_in, chip)
    recv = swap_seq(pick(hidden_in, far), 2)
    kept_o = swap_seq(kept, 1)
    tables = rope_tables(4 * block)
    gain_a, gain_m = gain_attn[None, :], gain_mlp[None, :]

    bits = batch_size.bit_length() - 1
    names = ["b%d" % i for i in reversed(range(bits))] + ["x"]
    top, rest = names[:4][::-1], names[4:]

    def index_of(name):
        return chip if name == "x" else (batch >> int(name[1:])) & 1

    scal = jnp.stack(
        [core, chip, pick(lengths, chip), index_of(top[0]), index_of(top[1])]
    ).astype(jnp.int32)

    def exchange(value, name):
        if name == "x":
            return swap_seq(value, 2)
        bit = 1 << int(name[1:])
        return lax.ppermute(value, "batch", [(i, i ^ bit) for i in range(batch_size)])

    class Sum:
        def __init__(self, *parts):
            self.parts = list(parts)

        def out(self, ready=None):
            me = index_of(self.parts[0].names[0])
            sends = [part.outgoing(me) for part in self.parts] if ready is None else [ready]
            self.sent = sends[0] if len(sends) == 1 else jnp.concatenate(sends, axis=-2)
            return self.sent

        def move(self):
            self.got = exchange(self.sent, self.parts[0].names[0])

        def land(self):
            me, row = index_of(self.parts[0].names[0]), 0
            for part in self.parts:
                rows = part.leaves[0].shape[-2]
                part.incoming(me, lax.slice_in_dim(self.got, row, row + rows, axis=self.got.ndim - 2))
                row += rows

        def hop(self):
            self.out()
            self.move()
            self.land()

    def swapped(part):
        part.names = [part.names[1], part.names[0]] + part.names[2:]
        part.leaves = [leaf.swapaxes(0, 1) for leaf in part.leaves]
        return part

    w_near, turns, q, k, v, w_all, tables = project_kept(
        scal, kept, kept_o, w_query, w_key, w_value, tables
    )
    ct_kept, ct_far = pick(cotangent, chip), pick(cotangent, far)
    recv, ct_kept, ct_far, _ = lax.optimization_barrier((recv, ct_kept, ct_far, w_all))
    recv_o = swap_seq(recv, 1)
    ct_recv = swap_seq(ct_far, 2)
    q, k, v, att, att_oth, x_all = attention_forward(
        scal, kept, recv, kept_o, recv_o, w_near, turns, q, k, v
    )
    got = swap_seq(att_oth, 1)
    (
        attended, norm1, root1, dmixed2, gain_row_m, dgate, dup,
        lay_kept, lay_away, down_keep, down_send, gate_keep, gate_send, up_keep, up_send,
    ) = ffn_forward(
        scal, gain_a, gain_m, kept, recv, att, got, ct_kept, ct_recv, w_output, w_gate, w_up, w_down
    )
    first = [swap_seq(z, 1) for z in (gate_send, up_send, down_send)]
    lay_back = swap_seq(lay_away, 2)
    dmixed1, do_own, do_send, wo_send, wo_keep = ffn_backward(
        scal, gain_a, gain_row_m, dgate, dup, dmixed2, norm1, root1, attended, w_output, w_gate, w_up
    )

    do_send, wo_send, lay_back, *first = lax.optimization_barrier(
        (do_send, wo_send, lay_back, *first)
    )
    do_oth, wo_got = swap_seq(do_send, 1), swap_seq(wo_send, 1)
    yz_names = [top[1], top[2], top[0], top[3]]
    xz_names = [top[0], top[2], top[1], top[3]]
    zy_names = [top[2], top[1], top[0], top[3]]
    gates = Sum(Part(xz_names, [gate_keep, first[0]]))
    ups = Sum(Part(yz_names, [up_keep, first[1]]))
    downs = Sum(Part(zy_names, [down_keep, first[2]]))
    sent = [z.out() for z in (gates, ups, downs)]
    scal_d = after(scal, *sent)
    for z in (gates, ups, downs):
        z.move()
    own_in, send_in, grads_a, grads_b, first_a, first_b = attention_backward(
        scal_d, q, k, v, att, do_own, do_oth, x_all, tables, dmixed1, w_all,
        wo_keep, wo_got,
    )

    send_in, first_a, first_b, gates.got, ups.got, downs.got = lax.optimization_barrier(
        (send_in, first_a, first_b, gates.got, ups.got, downs.got)
    )
    got_in = swap_seq(send_in, 1)
    alpha = Sum(Part(top, [grads_a]))
    beta = Sum(swapped(Part(top, [grads_b])))
    alpha.out(first_a)
    beta.out(first_b)
    alpha.move()
    beta.move()
    for z in (ups, downs, gates):
        z.land()
        z.out()
        z.move()
    g_in = (own_in + got_in.astype(F32)).astype(BF16)
    g_back = swap_seq(g_in[block:], 2)

    alpha.land()
    beta.land()
    alpha.out()
    beta.out()
    alpha.move()
    beta.move()
    gates.got = after(gates.got, alpha.sent)
    ups.got = after(ups.got, alpha.sent)
    downs.got = after(downs.got, beta.sent)
    for z in (gates, ups, downs):
        z.land()
        z.out()
        z.move()
    alpha.land()
    beta.land()
    others = Sum(*alpha.parts, *beta.parts)
    others.out()
    others.move()
    for z in (gates, ups,):
        z.got = after(z.got, others.sent)
        z.land()
    soon = Sum(*gates.parts, *ups.parts)
    soon.out()
    soon.move()
    for z in (downs,):
        z.got = after(z.got, soon.sent)
        z.land()
    feeds = Sum(*downs.parts)
    feeds.out()
    feeds.move()
    others.land()
    others.out()
    others.move()
    soon.got = after(soon.got, others.sent)
    feeds.got = after(feeds.got, others.sent)
    soon.land()
    others.land()
    feeds.land()
    lay_kept = after(lay_kept, feeds.sent)

    high = w_gate.shape[1] // SUPER
    wide = w_gate.shape[1] // 2 // LANES
    gate_sum, up_sum, down_sum = [z.parts[0].result() for z in (gates, ups, downs)]
    alpha_sum, beta_sum = [z.result() for z in others.parts]
    above = pairs * height
    gain_rows = beta_sum[above:above + 16]
    feed = [(high, pairs)] + [(height, wide)] * 2
    feed_sums = [down_sum, gate_sum, up_sum]
    rest_layout = [(height, 1)] * (3 * pairs - 3) + [(height, pairs)] + [(height, 1)] * 3
    rest_sums = [alpha_sum, beta_sum[:above], beta_sum[above + 16:]]
    grad_in_of = lambda: home(g_in[:block], g_back)
    if rest:
        return finish_general(
            feed, feed_sums, rest_layout, rest_sums, gain_rows, rest, index_of, exchange, core, pairs,
            home(lay_kept, lay_back), grad_in_of(),
        )

    def sides(totals, layout):
        total, row, pieces = jnp.concatenate(totals), 0, []
        for rows, chunks in layout:
            pieces.append(total[row:row + rows * chunks].reshape(chunks, 2, rows // 2, LANES))
            row += rows * chunks
        return [
            jnp.concatenate(
                [lax.dynamic_index_in_dim(z, i, 1, keepdims=False).reshape(-1, LANES) for z in pieces]
            )
            for i in (other, core)
        ]

    away, stay = sides(feed_sums, feed)
    g_down, g_gate, g_up = assemble(
        scal, stay, swap_seq(away, 1), [(rows // 2, chunks) for rows, chunks in feed]
    )
    half = height // 2
    away, stay = sides(rest_sums, rest_layout)
    last = swap_seq(jnp.concatenate([away, gain_rows[:8]]), 1)
    g_output, g_query, g_key, g_value = assemble_pairs(scal, stay, last, half, pairs)
    gains = jnp.where(core == 0, jnp.stack([gain_rows[0], last[-8]]), jnp.stack([last[-8], gain_rows[0]]))
    gains = lax.dynamic_slice_in_dim(gains, core * half, half, axis=1)
    layer_out = home(lay_kept, lay_back)
    return (
        layer_out, grad_in_of(), g_query, g_key, g_value, g_output, g_gate, g_up, g_down,
        gains[0], gains[1],
    )


def finish_general(
    feed, feed_sums, rest_layout, rest_sums, gain_rows, rest, index_of, exchange, core, pairs,
    layer_out, grad_in,
):
    def finish(packed, rows, chunks):
        matrix = packed.reshape(chunks, rows, LANES).transpose(1, 0, 2).reshape(rows, chunks * LANES)
        for name in rest:
            matrix = matrix.reshape(2, matrix.shape[0] // 2, matrix.shape[1])
            me = index_of(name)
            away = lax.dynamic_index_in_dim(matrix, 1 - me, 0, keepdims=False)
            stay = lax.dynamic_index_in_dim(matrix, me, 0, keepdims=False)
            matrix = stay + exchange(away.astype(BF16), name).astype(F32)
        matrix = matrix.reshape(2, matrix.shape[0] // 2, matrix.shape[1])
        stay = lax.dynamic_index_in_dim(matrix, core, 0, keepdims=False)
        got = swap_seq(lax.dynamic_index_in_dim(matrix, 1 - core, 0, keepdims=False), 1)
        return jnp.where(
            core == 0,
            jnp.concatenate([stay, got], axis=-1),
            jnp.concatenate([got, stay], axis=-1),
        )

    def matrices(total, layout):
        row, out = 0, []
        for rows, chunks in layout:
            out.append((total[row:row + rows * chunks], rows, chunks))
            row += rows * chunks
        return out

    down, gate, up = matrices(jnp.concatenate(feed_sums), feed)
    qkv = matrices(jnp.concatenate(rest_sums), rest_layout)
    output = qkv.pop(3 * pairs - 3)
    height = output[1]
    by_matrix = [
        (jnp.concatenate([qkv[3 * p + i][0] for p in range(pairs)]), height, pairs) for i in range(3)
    ]
    gains = jnp.broadcast_to(gain_rows[0, :height, None], (height, LANES))
    outs = [finish(*z) for z in by_matrix + [output, gate, up, down, (gains, height, 1)]]
    gains = outs.pop()
    return (layer_out, grad_in, *outs, gains[:, 0], gains[:, LANES])


def solution(mesh):
    tokens = P("batch", "seq", None)
    rows = P(("batch", "seq"), None)
    return jax.shard_map(
        functools.partial(on_device, mesh.shape["batch"]),
        mesh=mesh,
        in_specs=(tokens, tokens, P("batch")) + (P(),) * 9,
        out_specs=(tokens, tokens) + (rows,) * 7 + (P(("batch", "seq")),) * 2,
        check_vma=False,
    )
```

```python
import functools

import jax
import jax.numpy as jnp
import numpy as np
from jax import lax
from jax.experimental import pallas as pl
from jax.experimental.pallas import tpu as pltpu
from jax.sharding import PartitionSpec as P

HEADS = 12
HEAD_DIM = 64
PAIR = 2 * HEAD_DIM

EPS = 1e-06
NEG = -1e30
LANES = 128
SUPER = 16

F32 = jnp.float32
BF16 = jnp.bfloat16


def dot_nn(left, right):
    return lax.dot_general(left, right, (((1,), (0,)), ((), ())), preferred_element_type=F32)


def dot_nt(left, right):
    return lax.dot_general(left, right, (((1,), (1,)), ((), ())), preferred_element_type=F32)


def dot_tn(left, right):
    return lax.dot_general(left, right, (((0,), (0,)), ((), ())), preferred_element_type=F32)


def rope_tables(count):
    half = HEAD_DIM // 2
    inverse = 10000.0 ** (-(np.arange(half, dtype=np.float32) * np.float32(2.0)) / HEAD_DIM)
    angles = np.arange(count, dtype=np.float32)[:, None] * inverse.astype(np.float32)[None, :]
    cosine, sine = np.cos(angles), np.sin(angles)
    zero = np.zeros_like(sine)
    tables = (
        np.concatenate([cosine] * 4, axis=-1),
        np.concatenate([zero, sine] * 2, axis=-1),
        np.concatenate([-sine, zero] * 2, axis=-1),
    )
    return jnp.asarray(np.stack(tables), F32)


def start(source, target, sem):
    copy = pltpu.make_async_copy(source, target, sem)
    copy.start()
    return copy


def aligned(index, size):
    return pl.ds(pl.multiple_of(index * size, size), size)


def vspec():
    return pl.BlockSpec(memory_space=pltpu.VMEM)


def hspec():
    return pl.BlockSpec(memory_space=pltpu.HBM)


def aspec():
    return pl.BlockSpec(memory_space=pl.ANY)


def sspec():
    return pl.BlockSpec(memory_space=pltpu.SMEM)


def mean_row(z):
    return jnp.sum(z, axis=1, keepdims=True) * (1.0 / z.shape[1])


def reversed_bits(index, bits):
    out = 0
    for i in range(bits):
        out |= ((index >> i) & 1) << (bits - 1 - i)
    return out


def xy_first(b):
    return reversed_bits(b, 4)


def xz_first(b):
    zh, zl, y, x = (b >> 3) & 1, (b >> 2) & 1, (b >> 1) & 1, b & 1
    return x * 8 + zl * 4 + y * 2 + zh


def yz_first(b):
    zh, zl, y, x = (b >> 3) & 1, (b >> 2) & 1, (b >> 1) & 1, b & 1
    return y * 8 + zl * 4 + x * 2 + zh


def zy_first(b):
    zh, zl, y, x = (b >> 3) & 1, (b >> 2) & 1, (b >> 1) & 1, b & 1
    return zl * 8 + y * 4 + x * 2 + zh


def pack(out_ref, value, place, block0, row0, height):
    low = value.astype(BF16)
    for b in range(value.shape[0] // height):
        for j in range(value.shape[1] // LANES):
            out_ref[place(block0 + b), row0 + j * height:row0 + (j + 1) * height, :] = low[
                b * height:(b + 1) * height, j * LANES:(j + 1) * LANES
            ]


def kernel_call(
    kernel, name, outs, specs, scratch, flops, moved, exps=0, resident=(), vmem=16, free=(), through=(),
    updated=None,
):
    count = len(resident) + len(outs)
    through = tuple(through)
    if through:
        inner = kernel

        def kernel(*refs):
            at = len(specs) + count
            inner(*refs[:at], *refs[at + len(through):])

    return pl.pallas_call(
        kernel,
        out_shape=tuple(pltpu.VMEM(*z) for z in resident)
        + tuple(
            jax.ShapeDtypeStruct(*z) if i in free else pltpu.HBM(*z) for i, z in enumerate(outs)
        )
        + tuple(pltpu.HBM(*z) for _, z in through),
        in_specs=specs,
        out_specs=(vspec(),) * len(resident)
        + tuple(aspec() if i in free else hspec() for i in range(len(outs)))
        + (hspec(),) * len(through),
        input_output_aliases={n: count + i for i, (n, _) in enumerate(through)} | (updated or {}),
        scratch_shapes=scratch,
        compiler_params=pltpu.CompilerParams(vmem_limit_bytes=vmem * 1024 * 1024),
        cost_estimate=pl.CostEstimate(flops=flops, bytes_accessed=moved, transcendentals=exps),
        name=name,
    )


class Copies:
    def __init__(self, sems):
        self.sems, self.used, self.open = sems, 0, []

    def start(self, source, target):
        copy = start(source, target, self.sems.at[self.used])
        self.used += 1
        return copy

    def send(self, source, target):
        self.open.append(self.start(source, target))

    def drain(self):
        for copy in self.open:
            copy.wait()


def split_three(value):
    first = value.astype(BF16).astype(F32)
    rest = value - first
    second = rest.astype(BF16).astype(F32)
    return first, second, (rest - second).astype(BF16).astype(F32)


def beside(lane, head, mine, pieces):
    own = (lane < HEAD_DIM) if head == 0 else (lane >= HEAD_DIM)
    first = (1 - head) * HEAD_DIM
    out = jnp.zeros_like(mine)
    for i, piece in enumerate(pieces):
        out = jnp.where(lane == first + i, piece, out)
    return jnp.where(own, mine, out)


def project(x_ref, w_buf, t_ref, q_ref, k_ref, v_ref, places, length):
    pairs = q_ref.shape[0]
    block = x_ref.shape[0] // 2
    scale = float(HEAD_DIM) ** (-0.5)
    lane = lax.broadcasted_iota(jnp.int32, (1, PAIR), 1)
    z_all = dot_nn(x_ref[...], w_buf[...])
    for t, place in enumerate(places):
        z = z_all[t * block:(t + 1) * block]
        rows = aligned(place, block)
        c, a, b = t_ref[0, rows, :], t_ref[1, rows, :], t_ref[2, rows, :]
        slot = place * block + lax.broadcasted_iota(jnp.int32, (block, PAIR), 0)
        bias = jnp.where(slot < length, 0.0, NEG)
        for p in range(3 * pairs):
            part = z[:, p * PAIR:(p + 1) * PAIR]
            if p < 2 * pairs:
                part = part * c + pltpu.roll(part, 32, 1) * a + pltpu.roll(part, 96, 1) * b
            for h in range(2):
                if p < pairs:
                    mine = part.astype(BF16).astype(F32) * scale
                    q_ref[p, h, rows, :] = beside(lane, h, mine, (0.0, 0.0, 0.0, 1.0)).astype(BF16)
                elif p < 2 * pairs:
                    k_ref[p - pairs, h, rows, :] = beside(
                        lane, h, part, (1.0, 1.0, 1.0, bias)
                    ).astype(BF16)
                else:
                    own = (lane < HEAD_DIM) if h == 0 else (lane >= HEAD_DIM)
                    v_ref[p - 2 * pairs, h, rows, :] = jnp.where(own, part, 1.0).astype(BF16)


def project_kept_kernel(
    scal, kept, kept_o, wq, wk, wv, tables, w_buf, t_ref, q_ref, k_ref, v_ref, w_out, t_out, x_ref, sems
):
    core, chip, length = scal[0], scal[1], scal[2]
    block = kept.shape[0]
    cols = wq.shape[1] // 2
    io = Copies(sems)
    columns = pl.ds(pl.multiple_of(core * cols, PAIR), cols)
    needed = [
        io.start(w.at[:, columns], w_buf.at[:, i * cols:(i + 1) * cols])
        for i, w in enumerate((wq, wk, wv))
    ]
    needed.append(io.start(kept, x_ref.at[0:block, :]))
    needed.append(io.start(kept_o, x_ref.at[block:, :]))
    needed.append(io.start(tables, t_ref))
    for copy in needed:
        copy.wait()
    io.send(w_buf, w_out)
    io.send(t_ref, t_out)
    places = (2 * chip + core, 2 * chip + 1 - core)
    project(x_ref, w_buf, t_ref, q_ref, k_ref, v_ref, places, length)
    io.drain()


def project_kept(scal, kept, kept_o, wq, wk, wv, tables):
    block, width = kept.shape
    cols = width // 2
    aug = ((cols // PAIR, 2, 4 * block, PAIR), BF16)
    weights, turns = ((width, 3 * cols), BF16), (tables.shape, F32)
    return kernel_call(
        project_kept_kernel, "project_kept", [weights, turns],
        [sspec()] + [aspec()] * 2 + [hspec()] * 4,
        [pltpu.VMEM((2 * block, width), BF16), pltpu.SemaphoreType.DMA((8,))],
        4 * block * width * 3 * cols, 8_000_000, vmem=40, resident=[weights, turns, aug, aug, aug],
    )(scal, kept, kept_o, wq, wk, wv, tables)


def attention_forward_kernel(
    scal, kept, recv, kept_o, recv_o, w_buf, t_ref, q_in, k_in, v_in,
    q_ref, k_ref, v_ref,
    q_out, k_out, v_out, att_out, oth_out, x_out,
    x_ref, x_new, att_ref, sems,
):
    del q_in, k_in, v_in
    core, chip, length = scal[0], scal[1], scal[2]
    block = kept.shape[0]
    pairs = q_ref.shape[0]
    other, far = 1 - core, 1 - chip
    io = Copies(sems)
    needed = [io.start(recv, x_new.at[0:block, :]), io.start(recv_o, x_new.at[block:, :])]
    blocks = [
        io.start(source, x_ref.at[aligned(place, block), :])
        for source, place in (
            (kept, 2 * chip + core),
            (recv, 2 * far + core),
            (kept_o, 2 * chip + other),
            (recv_o, 2 * far + other),
        )
    ]
    for copy in needed:
        copy.wait()
    project(x_new, w_buf, t_ref, q_ref, k_ref, v_ref, (2 * far + core, 2 * far + other), length)
    for copy in blocks:
        copy.wait()
    for source, out in ((x_ref, x_out), (k_ref, k_out), (v_ref, v_out)):
        io.send(source, out)

    lane = lax.broadcasted_iota(jnp.int32, (1, PAIR), 1)
    low = lane < HEAD_DIM
    causal = lax.broadcasted_iota(jnp.int32, (block, block), 1) <= lax.broadcasted_iota(
        jnp.int32, (block, block), 0
    )

    def scores(p, h, i):
        span = (i + 1) * block
        s = dot_nt(q_ref[p, h, i * block:span, :], k_ref[p, h, :span, :])
        diag = jnp.where(causal, s[:, i * block:], NEG)
        return jnp.concatenate([s[:, :i * block], diag], axis=1) if i else diag

    outs, tops = {}, {}

    def attend(unit, e):
        p, h, i = unit
        outs[unit] = dot_nn(e, v_ref[p, h, :(i + 1) * block, :])

    def finish(p):
        for i in range(4):
            rows = slice(i * block, (i + 1) * block)
            first, second = outs[p, 0, i], outs[p, 1, i]
            sums = pltpu.roll(jnp.where(low, second, first), HEAD_DIM, 1)
            att_ref[p, rows, :] = (jnp.where(low, first, second) / sums).astype(BF16)
            for h in range(2):
                lse = tops[p, h, i] + jnp.log(outs[p, h, i])
                mine = q_ref[p, h, rows, :].astype(F32)
                for n, piece in enumerate(split_three(-lse)):
                    mine = jnp.where(lane == (1 - h) * HEAD_DIM + n, piece, mine)
                q_ref[p, h, rows, :] = mine.astype(BF16)
        io.send(q_ref.at[p], q_out.at[p])
        io.send(att_ref.at[p], att_out.at[p])
        for t in range(2):
            place = 2 * (chip if t == 0 else far) + other
            io.send(
                att_ref.at[p, aligned(place, block), :], oth_out.at[p, t * block:(t + 1) * block, :]
            )

    units = [(p, h, i) for p in range(pairs) for h in range(2) for i in (3, 2, 1, 0)]
    ahead, behind = scores(*units[0]), None
    for n, unit in enumerate(units):
        s = ahead
        ahead = scores(*units[n + 1]) if n + 1 < len(units) else None
        if behind is not None:
            attend(*behind)
        if n and n % 8 == 0:
            finish(unit[0] - 1)
        top = jnp.max(s, axis=1, keepdims=True)
        tops[unit] = top
        behind = (unit, jnp.exp(s - top).astype(BF16))
    attend(*behind)
    finish(pairs - 1)
    io.drain()


def attention_forward(scal, kept, recv, kept_o, recv_o, w_all, turns, q, k, v):
    block, width = kept.shape
    full = 4 * block
    pairs = q.shape[0]
    aug = (q.shape, BF16)
    return kernel_call(
        attention_forward_kernel, "attention_forward",
        [aug, aug, aug, ((pairs, full, PAIR), BF16), ((pairs, full // 2, PAIR), BF16),
         ((full, width), BF16)],
        [sspec()] + [aspec()] * 4 + [vspec()] * 5,
        [
            pltpu.VMEM((full, width), BF16),
            pltpu.VMEM((full // 2, width), BF16),
            pltpu.VMEM((pairs, full, PAIR), BF16),
            pltpu.SemaphoreType.DMA((9 + 4 * pairs,)),
        ],
        full * width * width * 3 // 2 + 4 * full * full * pairs * PAIR, 14_000_000, full * full * 6,
        resident=[aug, aug, aug], vmem=44, updated={7: 0, 8: 1, 9: 2},
    )(scal, kept, recv, kept_o, recv_o, w_all, turns, q, k, v)[3:]


def load_attended(io, target, att, got, places, block):
    pairs = att.shape[0]
    copies = []
    for p in range(pairs):
        for t in range(2):
            copies.append(
                io.start(
                    att.at[p, aligned(places[t], block), :],
                    target.at[t * block:(t + 1) * block, p * PAIR:(p + 1) * PAIR],
                )
            )
        copies.append(io.start(got.at[p], target.at[:, (pairs + p) * PAIR:(pairs + p + 1) * PAIR]))
    return copies


def load_output_weight(io, target, wo, core, cols):
    return [
        io.start(wo.at[aligned(core, cols), :], target.at[0:cols, :]),
        io.start(wo.at[aligned(1 - core, cols), :], target.at[cols:, :]),
    ]


def ffn_forward_kernel(
    scal, gain_a, gain_m, kept, recv, att, got, ct_kept, ct_recv, wo, wg, wu, wd,
    att_ref, norm1_ref, root1_ref, dmixed2_ref, gain_row_ref, dgate_ref, dup_ref,
    lay_kept, lay_away, down_keep, down_send, gate_keep, gate_send, up_keep, up_send,
    wo_buf, wg_buf, wu_buf, wd_buf, x_ref, ct_ref, lay_ref, x1_low_ref, dm_ref, gate_ref, up_ref,
    hid_ref, dk_ref, ds_ref, gk_ref, gs_ref, uk_ref, us_ref, sems,
):
    core, chip, length = scal[0], scal[1], scal[2]
    block, width = kept.shape
    cols = width // 2
    ff = wg.shape[1]
    step = ff // 4
    other, far = 1 - core, 1 - chip
    places = (2 * chip + core, 2 * far + core)
    io = Copies(sems)
    first = load_attended(io, att_ref, att, got, places, block)
    first += load_output_weight(io, wo_buf, wo, core, cols)
    first.append(io.start(kept, x_ref.at[0:block, :]))
    first.append(io.start(recv, x_ref.at[block:, :]))
    weights = []
    for f in range(4):
        part = slice(f * step, (f + 1) * step)
        weights.append(io.start(wg.at[:, part], wg_buf.at[:, part]))
        weights.append(io.start(wu.at[:, part], wu_buf.at[:, part]))
    down = io.start(wd, wd_buf)
    late = [io.start(ct_kept, ct_ref.at[0:block, :]), io.start(ct_recv, ct_ref.at[block:, :])]
    for copy in first:
        copy.wait()
    mixed = x_ref[...].astype(F32) + dot_nn(att_ref[...], wo_buf[...])
    root = lax.rsqrt(mean_row(mixed * mixed) + EPS)
    norm = mixed * root
    norm1_ref[...] = norm
    root1_ref[...] = jnp.broadcast_to(root, root1_ref.shape)
    x1_low_ref[...] = (norm * gain_a[...]).astype(BF16)
    for f in range(4):
        part = slice(f * step, (f + 1) * step)
        weights[2 * f].wait()
        weights[2 * f + 1].wait()
        gate = dot_nn(x1_low_ref[...], wg_buf[:, part])
        up = dot_nn(x1_low_ref[...], wu_buf[:, part])
        hid_ref[:, part] = (gate * jax.nn.sigmoid(gate) * up).astype(BF16)
        gate_ref[:, part] = gate.astype(BF16)
        up_ref[:, part] = up.astype(BF16)
    down.wait()
    mixed = norm1_ref[...] * gain_a[...] + dot_nn(hid_ref[...], wd_buf[...])
    root = lax.rsqrt(mean_row(mixed * mixed) + EPS)
    norm = mixed * root
    slot = lax.broadcasted_iota(jnp.int32, (2 * block, 1), 0)
    slot = jnp.where(slot < block, places[0] * block + slot, (places[1] - 1) * block + slot)
    valid = (slot < length).astype(F32)
    lay_ref[...] = (valid * (norm * gain_m[...])).astype(BF16)
    io.send(lay_ref.at[0:block, :], lay_kept)
    io.send(lay_ref.at[block:, :], lay_away)
    for copy in late:
        copy.wait()
    d_out = valid * ct_ref[...].astype(F32)
    gain_row = jnp.sum(d_out * norm, axis=0, keepdims=True)
    gain_row_ref[...] = jnp.broadcast_to(gain_row, gain_row_ref.shape)
    d_norm = d_out * gain_m[...]
    d_mixed = root * (d_norm - norm * mean_row(d_norm * norm))
    dmixed2_ref[...] = d_mixed
    dm_ref[...] = d_mixed.astype(BF16)
    right = jnp.concatenate([dm_ref[:, aligned(other, cols)], dm_ref[:, aligned(core, cols)]], axis=1)
    height = ff // SUPER
    for f in range(4):
        grad = dot_tn(hid_ref[:, f * step:(f + 1) * step], right)
        pack(ds_ref, grad[:, :cols], zy_first, f * step // height, 0, height)
        pack(dk_ref, grad[:, cols:], zy_first, f * step // height, 0, height)
    io.send(ds_ref, down_send)
    io.send(dk_ref, down_keep)
    height = width // SUPER
    rows = step // LANES * height
    for gate_part, gate_out, up_part, up_out, side in (
        (gs_ref, gate_send, us_ref, up_send, other), (gk_ref, gate_keep, uk_ref, up_keep, core),
    ):
        for sub in range(2):
            part = aligned(side * 2 + sub, step)
            d_hid = dot_nt(dm_ref[...], wd_buf[part, :])
            g = gate_ref[:, part].astype(F32)
            sigma = jax.nn.sigmoid(g)
            d_up = (d_hid * (g * sigma)).astype(BF16)
            d_gate = (
                d_hid * up_ref[:, part].astype(F32) * sigma * (1.0 + g * (1.0 - sigma))
            ).astype(BF16)
            dgate_ref[:, part] = d_gate
            dup_ref[:, part] = d_up
            pack(gate_part, dot_tn(x1_low_ref[...], d_gate), xz_first, 0, sub * rows, height)
            pack(up_part, dot_tn(x1_low_ref[...], d_up), yz_first, 0, sub * rows, height)
            at = slice(sub * rows, (sub + 1) * rows)
            io.send(gate_part.at[:, at, :], gate_out.at[:, at, :])
            io.send(up_part.at[:, at, :], up_out.at[:, at, :])
    io.drain()


def ffn_forward(scal, gain_a, gain_m, kept, recv, att, got, ct_kept, ct_recv, wo, wg, wu, wd):
    block, width = kept.shape
    ff = wg.shape[1]
    tokens, cols = 2 * block, width // 2
    half = ((block, width), BF16)
    down = ((SUPER, ff // SUPER * (cols // LANES), LANES), BF16)
    wide = ((SUPER, width // SUPER * (ff // 2 // LANES), LANES), BF16)
    rows16, rows32 = ((tokens, width), BF16), ((tokens, width), F32)
    hidden = ((tokens, ff), BF16)
    return kernel_call(
        ffn_forward_kernel, "ffn_forward", [half, half, down, down, wide, wide, wide, wide],
        [sspec(), vspec(), vspec()] + [aspec()] * 2 + [hspec()] + [aspec()] * 3 + [hspec()] * 4,
        [pltpu.VMEM(*z) for z in [
            ((width, width), BF16), ((width, ff), BF16), ((width, ff), BF16), ((ff, width), BF16),
            rows16, rows16, rows16, rows16, rows16, hidden, hidden, hidden,
            down, down, wide, wide, wide, wide,
        ]] + [pltpu.SemaphoreType.DMA((27 + 3 * (cols // PAIR),))],
        2 * tokens * width * (width + 7 * ff), 26_000_000, 2 * tokens * ff, vmem=44,
        resident=[rows16, rows32, ((tokens, LANES), F32), rows32, ((8, width), F32), hidden, hidden],
    )(scal, gain_a, gain_m, kept, recv, att, got, ct_kept, ct_recv, wo, wg, wu, wd)


def ffn_backward_kernel(
    scal, gain_a, gain_row_m, dgate_ref, dup_ref, dmixed2_ref, norm1_ref, root1_ref, att_ref,
    wo, wg, wu,
    dmixed1_out, do_out, do_send_out, send_out, keep_out,
    wo_buf, wg_buf, wu_buf, dmixed1_ref, do_ref, do_send_ref, send_ref, keep_ref, da_ref, sems,
):
    core = scal[0]
    tokens, width = dmixed2_ref.shape
    cols = width // 2
    height = width // SUPER
    chunks = cols // LANES
    other = 1 - core
    ff = wg.shape[1]
    io = Copies(sems)
    weights = []
    for f in range(2):
        part = slice(f * ff // 2, (f + 1) * ff // 2)
        for weight, buffer in ((wg, wg_buf), (wu, wu_buf)):
            weights.append(io.start(weight.at[:, part], buffer.at[:, part]))
    last = load_output_weight(io, wo_buf, wo, core, cols)
    d_x1 = dmixed2_ref[...]
    for f in range(2):
        part = slice(f * ff // 2, (f + 1) * ff // 2)
        for n, (left, right) in enumerate(((dgate_ref, wg_buf), (dup_ref, wu_buf))):
            weights[2 * f + n].wait()
            d_x1 += dot_nt(left[:, part], right[:, part])
    norm = norm1_ref[...]
    gain_row = jnp.sum(d_x1 * norm, axis=0, keepdims=True)
    d_norm = d_x1 * gain_a[...]
    d_mixed = root1_ref[:, 0:1] * (d_norm - norm * mean_row(d_norm * norm))
    dmixed1_ref[...] = d_mixed
    da_ref[...] = d_mixed.astype(BF16)
    io.send(dmixed1_ref, dmixed1_out)
    for copy in last:
        copy.wait()
    d_att = dot_nt(da_ref[...], wo_buf[...]).astype(BF16)
    for p in range(chunks):
        do_ref[p] = d_att[:, p * LANES:(p + 1) * LANES]
        do_send_ref[p] = d_att[:, cols + p * LANES:cols + (p + 1) * LANES]
    io.send(do_ref, do_out)
    io.send(do_send_ref, do_send_out)
    right = jnp.concatenate([da_ref[:, aligned(other, cols)], da_ref[:, aligned(core, cols)]], axis=1)
    grad = dot_tn(att_ref[...], right).astype(BF16)
    for heads, row0 in ((core, 0), (other, cols)):
        for b in range(cols // height):
            position = 2 * reversed_bits(b, 3) + heads
            for j in range(2 * chunks):
                target = send_ref if j < chunks else keep_ref
                target[position, (j % chunks) * height:(j % chunks + 1) * height, :] = grad[
                    row0 + b * height:row0 + (b + 1) * height, j * LANES:(j + 1) * LANES
                ]
    for target, half in ((send_ref, other), (keep_ref, core)):
        row = jnp.broadcast_to(jnp.where(half == 0, gain_row, gain_row_m[0:1, :]), (16, width))
        for b in range(SUPER):
            turned = pltpu.roll(row, width - b * height, 1) if b else row
            target[xy_first(b), chunks * height:, :] = turned[:, :LANES].astype(BF16)
    io.send(send_ref, send_out)
    io.send(keep_ref, keep_out)
    io.drain()


def ffn_backward(scal, gain_a, gain_row_m, dgate, dup, dmixed2, norm1, root1, att, wo, wg, wu):
    tokens, width = dmixed2.shape
    ff = wg.shape[1]
    chunks = width // 2 // LANES
    packed = ((SUPER, chunks * (width // SUPER) + 16, LANES), BF16)
    split = ((chunks, tokens, LANES), BF16)
    outs = [((tokens, width), F32), split, split, packed, packed]
    return kernel_call(
        ffn_backward_kernel, "ffn_backward", outs,
        [sspec()] + [vspec()] * 8 + [hspec()] * 3,
        [pltpu.VMEM(*z) for z in [
            ((width, width), BF16), ((width, ff), BF16), ((width, ff), BF16),
        ] + outs + [((tokens, width), BF16)]] + [pltpu.SemaphoreType.DMA((11,))],
        2 * tokens * width * (2 * width + 2 * ff), 12_000_000, vmem=26,
    )(scal, gain_a, gain_row_m, dgate, dup, dmixed2, norm1, root1, att, wo, wg, wu)


def attention_backward_kernel(
    scal, qa, ka, va, att, do_own, do_oth, x_all, tables, dmixed1, w_all, wo_keep, wo_got,
    own_out, send_out, grad_a, grad_b, first_a, first_b,
    qa_ref, ka_ref, va_ref, att_ref, do_ref, x_ref, t_ref, dst_ref, doa_ref, dz_ref, a_ref, b_ref,
    wo_ref, w_buf, own_ref, send_ref, sems,
):
    core, chip, lead, second = scal[0], scal[1], scal[3], scal[4]
    pairs, _, full, _ = qa_ref.shape
    block = full // 4
    cols = pairs * PAIR
    scale = float(HEAD_DIM) ** (-0.5)
    other, far = 1 - core, 1 - chip
    io = Copies(sems)
    loads = []
    for p in range(pairs):
        copies = []
        for source, t, place in (
            (do_own.at[p], 0, 2 * chip + core),
            (do_own.at[p], 1, 2 * far + core),
            (do_oth.at[p], 0, 2 * chip + other),
            (do_oth.at[p], 1, 2 * far + other),
        ):
            copies.append(
                io.start(source.at[pl.ds(t * block, block), :], do_ref.at[p, aligned(place, block), :])
            )
        for source, target in ((att, att_ref), (ka, ka_ref), (qa, qa_ref), (va, va_ref)):
            copies.append(io.start(source.at[p], target.at[p]))
        if p == 0:
            copies.append(io.start(tables, t_ref))
        loads.append(copies)
        if p == 0:
            late = io.start(x_all, x_ref)
    outputs = [io.start(wo_keep, wo_ref.at[0]), io.start(wo_got, wo_ref.at[1])]
    last = [io.start(dmixed1, own_ref), io.start(w_all, w_buf)]

    lane = lax.broadcasted_iota(jnp.int32, (1, PAIR), 1)
    low = lane < HEAD_DIM
    causal = lax.broadcasted_iota(jnp.int32, (block, block), 0) <= lax.broadcasted_iota(
        jnp.int32, (block, block), 1
    )
    height = x_ref.shape[1] // SUPER

    def back(g, rows):
        return (
            g * t_ref[0, rows, :]
            - pltpu.roll(g, 96, 1) * t_ref[2, rows, :]
            - pltpu.roll(g, 32, 1) * t_ref[1, rows, :]
        ).astype(BF16)

    for p in range(pairs):
        for copy in loads[p]:
            copy.wait()
        grad_do = do_ref[p].astype(F32)
        prod = grad_do * att_ref[p].astype(F32)
        for h in range(2):
            mine = low if h == 0 else jnp.logical_not(low)
            delta = jnp.sum(jnp.where(mine, prod, 0.0), axis=1, keepdims=True)
            doa_ref[h] = beside(lane, h, grad_do, split_three(-delta)).astype(BF16)
        for j in range(4):
            keys = slice(j * block, (j + 1) * block)
            span = slice(j * block, full)
            dk, dv = [], []
            for h in range(2):
                st = dot_nt(ka_ref[p, h, keys, :], qa_ref[p, h, span, :])
                dpt = dot_nt(va_ref[p, h, keys, :], doa_ref[h, span, :])
                pt = jnp.exp(st)
                diag = jnp.where(causal, pt[:, :block], 0.0)
                pt = diag if j == 3 else jnp.concatenate([diag, pt[:, block:]], axis=1)
                dst = (pt * dpt).astype(BF16)
                dst_ref[h, keys, span] = dst
                dv.append(dot_nn(pt.astype(BF16), doa_ref[h, span, :]))
                dk.append(dot_nn(dst, qa_ref[p, h, span, :]))
            dz_ref[p, keys, PAIR:2 * PAIR] = back(jnp.where(low, dk[0], dk[1]), keys)
            dz_ref[p, keys, 2 * PAIR:] = jnp.where(low, dv[0], dv[1]).astype(BF16)
        for i in range(4):
            rows = slice(i * block, (i + 1) * block)
            span = slice(0, (i + 1) * block)
            dq = [dot_tn(dst_ref[h, span, rows], ka_ref[p, h, span, :]) for h in range(2)]
            dz_ref[p, rows, :PAIR] = back(jnp.where(low, dq[0], dq[1]) * scale, rows)
        if p == 0:
            late.wait()
        grad = dot_tn(x_ref[...], dz_ref[p])
        if p < pairs - 1:
            pack(a_ref, grad, xy_first, 0, p * 3 * height, height)
        else:
            for copy in outputs:
                copy.wait()
            above = wo_ref.shape[2]
            b_ref[:, :above, :] = (wo_ref[0].astype(F32) + wo_ref[1].astype(F32)).astype(BF16)
            pack(b_ref, grad, xy_first, 0, above, height)
        if p == pairs - 2:
            io.send(a_ref, grad_a)
            io.send(a_ref.at[aligned(1 - lead, 8)], first_a)
    io.send(b_ref, grad_b)
    for i in range(2):
        io.send(b_ref.at[aligned(2 * i + 1 - second, 4)], first_b.at[4 * i:4 * i + 4])
    for copy in last:
        copy.wait()
    for side, target, out in ((other, send_ref, send_out), (core, own_ref, own_out)):
        left = jnp.concatenate(
            [
                jnp.concatenate(
                    [
                        dz_ref[p, aligned(2 * x + side, block), i * PAIR:(i + 1) * PAIR]
                        for i in range(3)
                        for p in range(pairs)
                    ],
                    axis=1,
                )
                for x in (chip, far)
            ]
        )
        grad = dot_nt(left, w_buf[...])
        if target is own_ref:
            grad += own_ref[...]
        target[...] = grad.astype(target.dtype)
        io.send(target, out)
    io.drain()


def attention_backward(
    scal, qa, ka, va, att, do_own, do_oth, x_all, tables, dmixed1, w_all, wo_keep, wo_got
):
    full, width = x_all.shape
    pairs = qa.shape[0]
    height = 3 * (width // SUPER)
    aug, rows = (qa.shape, BF16), ((pairs, full, PAIR), BF16)
    own, send = (dmixed1.shape, F32), (dmixed1.shape, BF16)
    part_a = ((pairs - 1) * height, LANES)
    part_b = (wo_keep.shape[1] + height, LANES)
    grads = [((SUPER,) + part_a, BF16), ((SUPER,) + part_b, BF16)]
    halves = [((SUPER // 2,) + part_a, BF16), ((SUPER // 2,) + part_b, BF16)]
    return kernel_call(
        attention_backward_kernel, "attention_backward", [own, send] + grads + halves,
        [sspec()] + [hspec()] * 5 + [aspec()] + [hspec()] * 4 + [aspec()] * 2,
        [pltpu.VMEM(*z) for z in [
            aug, aug, aug, rows, rows, ((full, width), BF16), (tables.shape, F32),
            ((2, full, full), BF16), ((2, full, PAIR), BF16), ((pairs, full, 3 * PAIR), BF16),
        ] + grads + [
            ((2,) + wo_keep.shape, BF16), ((width, pairs * 3 * PAIR), BF16), own, send,
        ]] + [pltpu.SemaphoreType.DMA((12 * pairs + 6,))],
        pairs * (10 * full * full * PAIR + 9 * full * width * PAIR), 20_000_000, full * full * 6, vmem=32,
        through=[
            (n, (z.shape, z.dtype))
            for n, z in ((1, qa), (2, ka), (3, va), (4, att), (7, x_all), (8, tables), (9, dmixed1), (10, w_all))
        ],
    )(scal, qa, ka, va, att, do_own, do_oth, x_all, tables, dmixed1, w_all, wo_keep, wo_got)[:6]


def assemble_kernel(layout, scal, stay, got, *outs):
    core = scal[0]
    for source, side in ((stay, core), (got, 1 - core)):
        row = 0
        for out, (rows, chunks) in zip(outs, layout):
            for j in range(chunks):
                out[:, aligned(side * chunks + j, LANES)] = source[row:row + rows, :]
                row += rows


def assemble(scal, stay, got, layout):
    return pl.pallas_call(
        functools.partial(assemble_kernel, layout),
        out_shape=tuple(jax.ShapeDtypeStruct((r, 2 * c * LANES), F32) for r, c in layout),
        in_specs=[sspec(), vspec(), vspec()],
        out_specs=(vspec(),) * len(layout),
        compiler_params=pltpu.CompilerParams(vmem_limit_bytes=16 * 1024 * 1024),
        cost_estimate=pl.CostEstimate(flops=0, bytes_accessed=16 * stay.shape[0] * LANES, transcendentals=0),
        name="assemble",
    )(scal, stay, got)


def assemble_pairs_kernel(half, pairs, scal, stay, got, *outs):
    core = scal[0]
    for source, side in ((stay, core), (got, 1 - core)):
        for i, out in enumerate(outs):
            for p in range(pairs):
                if i == 0:
                    chunk = 3 * pairs - 3 + p
                else:
                    chunk = 3 * p + i - 1 + (pairs if p == pairs - 1 else 0)
                out[:, aligned(side * pairs + p, LANES)] = source[chunk * half:(chunk + 1) * half, :]


def assemble_pairs(scal, stay, got, half, pairs):
    return pl.pallas_call(
        functools.partial(assemble_pairs_kernel, half, pairs),
        out_shape=(jax.ShapeDtypeStruct((half, 2 * pairs * LANES), F32),) * 4,
        in_specs=[sspec(), vspec(), vspec()],
        out_specs=(vspec(),) * 4,
        compiler_params=pltpu.CompilerParams(vmem_limit_bytes=16 * 1024 * 1024),
        cost_estimate=pl.CostEstimate(flops=0, bytes_accessed=16 * stay.shape[0] * LANES, transcendentals=0),
        name="assemble_pairs",
    )(scal, stay, got)


class Part:
    def __init__(self, names, leaves):
        self.names = list(names)
        dims = (2,) * len(self.names)
        self.leaves = [leaf.reshape(dims + leaf.shape[-2:]) for leaf in leaves]

    def take(self, index):
        return [lax.dynamic_index_in_dim(leaf, index, 0, keepdims=False) for leaf in self.leaves]

    def outgoing(self, me):
        return sum(leaf.astype(F32) for leaf in self.take(1 - me)).astype(BF16)

    def incoming(self, me, got):
        self.names = self.names[1:]
        dims = (2,) * len(self.names)
        stay = self.take(me)
        if len(self.names) < 3:
            stay = [lax.optimization_barrier(sum(leaf.astype(F32) for leaf in stay))]
        self.leaves = stay + [got.reshape(dims + (-1, got.shape[-1]))]

    def result(self):
        return sum(leaf.astype(F32) for leaf in self.leaves)


def swap_seq(value, bit):
    return lax.ppermute(value, "seq", [(i, i ^ bit) for i in range(4)])


def after(value, *others):
    return lax.optimization_barrier((value,) + others)[0]


def on_device(
    batch_size,
    hidden_in,
    cotangent,
    lengths,
    w_query,
    w_key,
    w_value,
    w_output,
    w_gate,
    w_up,
    w_down,
    gain_attn,
    gain_mlp,
):
    seqs, block, width = hidden_in.shape
    tokens = seqs * block
    cols = width // 2
    pairs = cols // PAIR
    height = width // SUPER
    rank = lax.axis_index("seq")
    batch = lax.axis_index("batch")
    chip, core = rank // 2, rank % 2
    far, other = 1 - chip, 1 - core

    def pick(z, index):
        return lax.dynamic_index_in_dim(z, index, 0, keepdims=False)

    def home(kept, back):
        first = chip == 0
        return jnp.stack([jnp.where(first, kept, back), jnp.where(first, back, kept)])

    away = pick(hidden_in, far)
    recv = swap_seq(away, 2)
    kept = pick(after(hidden_in, away), chip)
    kept_o = swap_seq(kept, 1)
    tables = rope_tables(4 * block)
    gain_a, gain_m = gain_attn[None, :], gain_mlp[None, :]

    bits = batch_size.bit_length() - 1
    names = ["b%d" % i for i in reversed(range(bits))] + ["x"]
    top, rest = names[:4][::-1], names[4:]

    def index_of(name):
        return chip if name == "x" else (batch >> int(name[1:])) & 1

    scal = jnp.stack(
        [core, chip, pick(lengths, chip), index_of(top[0]), index_of(top[1])]
    ).astype(jnp.int32)

    def exchange(value, name):
        if name == "x":
            return swap_seq(value, 2)
        bit = 1 << int(name[1:])
        return lax.ppermute(value, "batch", [(i, i ^ bit) for i in range(batch_size)])

    class Sum:
        def __init__(self, *parts):
            self.parts = list(parts)

        def out(self, ready=None):
            me = index_of(self.parts[0].names[0])
            sends = [part.outgoing(me) for part in self.parts] if ready is None else [ready]
            self.sent = sends[0] if len(sends) == 1 else jnp.concatenate(sends, axis=-2)
            return self.sent

        def move(self):
            self.got = exchange(self.sent, self.parts[0].names[0])

        def land(self):
            me, row = index_of(self.parts[0].names[0]), 0
            for part in self.parts:
                rows = part.leaves[0].shape[-2]
                part.incoming(me, lax.slice_in_dim(self.got, row, row + rows, axis=self.got.ndim - 2))
                row += rows

        def hop(self):
            self.out()
            self.move()
            self.land()

    def swapped(part):
        part.names = [part.names[1], part.names[0]] + part.names[2:]
        part.leaves = [leaf.swapaxes(0, 1) for leaf in part.leaves]
        return part

    w_near, turns, q, k, v, w_all, tables = project_kept(
        scal, kept, kept_o, w_query, w_key, w_value, tables
    )
    ct_kept, ct_far = pick(cotangent, chip), pick(cotangent, far)
    recv, ct_kept, ct_far, _ = lax.optimization_barrier((recv, ct_kept, ct_far, w_all))
    recv_o = swap_seq(recv, 1)
    ct_recv = swap_seq(ct_far, 2)
    q, k, v, att, att_oth, x_all = attention_forward(
        scal, kept, recv, kept_o, recv_o, w_near, turns, q, k, v
    )
    got = swap_seq(att_oth, 1)
    (
        attended, norm1, root1, dmixed2, gain_row_m, dgate, dup,
        lay_kept, lay_away, down_keep, down_send, gate_keep, gate_send, up_keep, up_send,
    ) = ffn_forward(
        scal, gain_a, gain_m, kept, recv, att, got, ct_kept, ct_recv, w_output, w_gate, w_up, w_down
    )
    first = [swap_seq(z, 1) for z in (gate_send, up_send, down_send)]
    lay_back = swap_seq(lay_away, 2)
    dmixed1, do_own, do_send, wo_send, wo_keep = ffn_backward(
        scal, gain_a, gain_row_m, dgate, dup, dmixed2, norm1, root1, attended, w_output, w_gate, w_up
    )

    do_send, wo_send, lay_back, *first = lax.optimization_barrier(
        (do_send, wo_send, lay_back, *first)
    )
    do_oth, wo_got = swap_seq(do_send, 1), swap_seq(wo_send, 1)
    yz_names = [top[1], top[2], top[0], top[3]]
    xz_names = [top[0], top[2], top[1], top[3]]
    zy_names = [top[2], top[1], top[0], top[3]]
    gates = Sum(Part(xz_names, [gate_keep, first[0]]))
    ups = Sum(Part(yz_names, [up_keep, first[1]]))
    downs = Sum(Part(zy_names, [down_keep, first[2]]))
    sent = [z.out() for z in (gates, ups, downs)]
    scal_d = after(scal, *sent)
    for z in (gates, ups, downs):
        z.move()
    own_in, send_in, grads_a, grads_b, first_a, first_b = attention_backward(
        scal_d, q, k, v, att, do_own, do_oth, x_all, tables, dmixed1, w_all,
        wo_keep, wo_got,
    )

    send_in, first_a, first_b, gates.got, ups.got, downs.got = lax.optimization_barrier(
        (send_in, first_a, first_b, gates.got, ups.got, downs.got)
    )
    got_in = swap_seq(send_in, 1)
    alpha = Sum(Part(top, [grads_a]))
    beta = Sum(swapped(Part(top, [grads_b])))
    alpha.out(first_a)
    beta.out(first_b)
    alpha.move()
    beta.move()
    for z in (ups, downs, gates):
        z.land()
        z.out()
        z.move()
    g_in = (own_in + got_in.astype(F32)).astype(BF16)
    g_back = swap_seq(g_in[block:], 2)

    alpha.land()
    beta.land()
    alpha.out()
    beta.out()
    alpha.move()
    beta.move()
    gates.got = after(gates.got, alpha.sent)
    ups.got = after(ups.got, alpha.sent)
    downs.got = after(downs.got, beta.sent)
    for z in (gates, ups, downs):
        z.land()
        z.out()
        z.move()
    alpha.land()
    beta.land()
    others = Sum(*alpha.parts, *beta.parts)
    others.out()
    others.move()
    for z in (gates, ups):
        z.got = after(z.got, others.sent)
        z.land()
    soon = Sum(*gates.parts, *ups.parts)
    soon.out()
    soon.move()
    downs.got = after(downs.got, soon.sent)
    downs.land()
    downs.out()
    downs.move()
    others.land()
    others.out()
    others.move()
    soon.got = after(soon.got, others.sent)
    downs.got = after(downs.got, others.sent)
    soon.land()
    downs.land()
    lay_kept = after(lay_kept, downs.sent)

    high = w_gate.shape[1] // SUPER
    wide = w_gate.shape[1] // 2 // LANES
    layer_out, grad_in = home(lay_kept, lay_back), home(g_in[:block], g_back)
    feed = [(high, pairs)] + [(height, wide)] * 2
    feed_sums = [z.parts[0].result() for z in (downs, gates, ups)]

    def sides(totals, layout):
        total, row, pieces = jnp.concatenate(totals), 0, []
        for rows, chunks in layout:
            pieces.append(total[row:row + rows * chunks].reshape(chunks, 2, rows // 2, LANES))
            row += rows * chunks
        return [
            jnp.concatenate(
                [lax.dynamic_index_in_dim(z, i, 1, keepdims=False).reshape(-1, LANES) for z in pieces]
            )
            for i in (other, core)
        ]

    if not rest:
        away, stay = sides(feed_sums, feed)
        g_down, g_gate, g_up = assemble(
            scal, stay, swap_seq(away, 1), [(rows // 2, chunks) for rows, chunks in feed]
        )
        others.got = after(others.got, grad_in)
    others.land()
    alpha_sum, beta_sum = [z.result() for z in others.parts]
    above = pairs * height
    gain_rows = beta_sum[above:above + 16]
    rest_layout = [(height, 1)] * (3 * pairs - 3) + [(height, pairs)] + [(height, 1)] * 3
    rest_sums = [alpha_sum, beta_sum[:above], beta_sum[above + 16:]]
    if rest:
        return finish_general(
            feed, feed_sums, rest_layout, rest_sums, gain_rows, rest, index_of, exchange, core, pairs,
            layer_out, grad_in,
        )
    half = height // 2
    away, stay = sides(rest_sums, rest_layout)
    last = swap_seq(jnp.concatenate([away, gain_rows[:8]]), 1)
    g_output, g_query, g_key, g_value = assemble_pairs(scal, stay, last, half, pairs)
    gains = jnp.where(core == 0, jnp.stack([gain_rows[0], last[-8]]), jnp.stack([last[-8], gain_rows[0]]))
    gains = lax.dynamic_slice_in_dim(gains, core * half, half, axis=1)
    return (
        layer_out, grad_in, g_query, g_key, g_value, g_output, g_gate, g_up, g_down,
        gains[0], gains[1],
    )


def finish_general(
    feed, feed_sums, rest_layout, rest_sums, gain_rows, rest, index_of, exchange, core, pairs,
    layer_out, grad_in,
):
    def finish(packed, rows, chunks):
        matrix = packed.reshape(chunks, rows, LANES).transpose(1, 0, 2).reshape(rows, chunks * LANES)
        for name in rest:
            matrix = matrix.reshape(2, matrix.shape[0] // 2, matrix.shape[1])
            me = index_of(name)
            away = lax.dynamic_index_in_dim(matrix, 1 - me, 0, keepdims=False)
            stay = lax.dynamic_index_in_dim(matrix, me, 0, keepdims=False)
            matrix = stay + exchange(away.astype(BF16), name).astype(F32)
        matrix = matrix.reshape(2, matrix.shape[0] // 2, matrix.shape[1])
        stay = lax.dynamic_index_in_dim(matrix, core, 0, keepdims=False)
        got = swap_seq(lax.dynamic_index_in_dim(matrix, 1 - core, 0, keepdims=False), 1)
        return jnp.where(
            core == 0,
            jnp.concatenate([stay, got], axis=-1),
            jnp.concatenate([got, stay], axis=-1),
        )

    def matrices(total, layout):
        row, out = 0, []
        for rows, chunks in layout:
            out.append((total[row:row + rows * chunks], rows, chunks))
            row += rows * chunks
        return out

    down, gate, up = matrices(jnp.concatenate(feed_sums), feed)
    qkv = matrices(jnp.concatenate(rest_sums), rest_layout)
    output = qkv.pop(3 * pairs - 3)
    height = output[1]
    by_matrix = [
        (jnp.concatenate([qkv[3 * p + i][0] for p in range(pairs)]), height, pairs) for i in range(3)
    ]
    gains = jnp.broadcast_to(gain_rows[0, :height, None], (height, LANES))
    outs = [finish(*z) for z in by_matrix + [output, gate, up, down, (gains, height, 1)]]
    gains = outs.pop()
    return (layer_out, grad_in, *outs, gains[:, 0], gains[:, LANES])


def solution(mesh):
    tokens = P("batch", "seq", None)
    rows = P(("batch", "seq"), None)
    return jax.shard_map(
        functools.partial(on_device, mesh.shape["batch"]),
        mesh=mesh,
        in_specs=(tokens, tokens, P("batch")) + (P(),) * 9,
        out_specs=(tokens, tokens) + (rows,) * 7 + (P(("batch", "seq")),) * 2,
        check_vma=False,
    )
```
